32 devices in a mesh: dp: 2 (over x), seq: 16 (over z, y, core).
Axes of the slice: x: 2, y: 2, z: 4, core: 2. Of those that a mesh axis runs over, the one named last changes fastest.
Arguments:
- queries: bfloat16 [2, 2048, 1024], P('dp', 'seq'), may hold values from -6 to 6
- keys: bfloat16 [2, 2048, 1024], P('dp', 'seq'), may hold values from -6 to 6
- values: bfloat16 [2, 2048, 1024], P('dp', 'seq'), may hold values from -6 to 6
- grad_out: bfloat16 [2, 2048, 1024], P('dp', 'seq'), may hold values from -6 to 6
- mem_keys: bfloat16 [16, 512, 1024], P('dp', 'seq'), may hold values from -6 to 6
- mem_values: bfloat16 [16, 512, 1024], P('dp', 'seq'), may hold values from -6 to 6
- seq_lengths: int32 [2], replicated, may hold values from 256 to 2048, as said below
- mem_counts: int32 [2], replicated, may hold values from 1 to 4, as said below
- block_lists: int32 [2, 4], replicated, may hold values from 0 to 15, as said below
- block_slots: int32 [16], replicated, may hold values from 0 to 15, each once
Outputs:
- grad_queries: bfloat16 [2, 2048, 1024], P('dp', 'seq')
- grad_keys: bfloat16 [2, 2048, 1024], P('dp', 'seq')
- grad_values: bfloat16 [2, 2048, 1024], P('dp', 'seq')
The draws below stay inside these ranges and needn't reach their ends.
Inputs may be any that keep to these rules, and one draw needn't show every extreme that they name: `seq_lengths`: some user has all 2048 events. `mem_counts`: some user attends to all 4 listed blocks. `block_lists`: the 4 ids of one user are distinct. `block_slots`: A permutation of the block ids.
All inputs are finite; a program needn't handle non-finite values.
Results may differ from the reference program's by a relative error of at most 0.0063.
Values may be sent and summed in bfloat16 or wider, within the bound.
No kernel may reach another device: no remote copies, remote signals or barrier semaphores. Data moves between devices by JAX's collectives and lax.ppermute only.
A program may use at most 128 MiB of HBM per device.

```python
import math
import jax
import jax.numpy as jnp
from jax import lax

D = 1024
H = 8
WINDOW = 512
BLK = 512
MB = 4
TOK_DEV = 128
USERS = 2
SEQLEN = 2048
NBLK = 16


def joint_rows(key):
    query_draw = jnp.clip(jax.random.normal(jax.random.fold_in(key, 11), (USERS, SEQLEN, D), jnp.float32), -6.0, 6.0)
    key_draw = jnp.clip(jax.random.normal(jax.random.fold_in(key, 12), (USERS, SEQLEN, D), jnp.float32), -6.0, 6.0)
    return (query_draw, key_draw)


def draw_queries(key, part):
    return joint_rows(key)[0].astype(jnp.bfloat16)


def draw_keys(key, part):
    return joint_rows(key)[1].astype(jnp.bfloat16)


def draw_seq_lengths(key, part):
    drawn = jax.random.randint(jax.random.fold_in(key, 21), (USERS,), 2 * TOK_DEV, SEQLEN + 1, jnp.int32)
    chosen = jax.random.randint(jax.random.fold_in(key, 22), (), 0, USERS, jnp.int32)
    return jnp.where(jnp.arange(USERS, dtype=jnp.int32) == chosen, SEQLEN, drawn).astype(jnp.int32)


def draw_mem_counts(key, part):
    drawn = jax.random.randint(jax.random.fold_in(key, 31), (USERS,), 1, MB + 1, jnp.int32)
    chosen = jax.random.randint(jax.random.fold_in(key, 32), (), 0, USERS, jnp.int32)
    return jnp.where(jnp.arange(USERS, dtype=jnp.int32) == chosen, MB, drawn).astype(jnp.int32)


def draw_block_lists(key, part):
    user_keys = jax.random.split(jax.random.fold_in(key, 41), USERS)

    def listing(user_key):
        return jax.random.permutation(user_key, NBLK)[:MB]
    return jax.vmap(listing)(user_keys).astype(jnp.int32)


def block_levels(rng, extent, pieces, low, largest):
    loudness, own = 1.0, jax.random.fold_in(rng, 6)
    for position, blocks in pieces:
        draws = jnp.exp(jax.random.uniform(jax.random.fold_in(own, position), (blocks,), jnp.float32, low / len(pieces), largest / len(pieces)))
        loudness = loudness * jnp.repeat(draws, extent[position] // blocks).reshape([-1 if axis == position else 1 for axis in range(len(extent))])
    return loudness


def scatter_about(key, dims, scale, most, cuts=(), held_as=jnp.bfloat16):
    result = scale * jax.random.normal(key, dims, jnp.float32)
    if cuts:
        result = result * block_levels(key, dims, cuts, -0.22, 0.18)
    return jnp.clip(result, -most, most).astype(held_as)


def setup_inputs(seed: int = 0) -> dict:
    arg_keys = jax.random.split(jax.random.key(seed), 11)
    return {
        "queries": draw_queries(jax.random.fold_in(arg_keys[10], 71), 0),
        "keys": draw_keys(jax.random.fold_in(arg_keys[10], 71), 0),
        "values": scatter_about(arg_keys[2], (USERS, SEQLEN, D), 1.0, 6.0, ((0, 2), (1, 16))),
        "grad_out": scatter_about(arg_keys[3], (USERS, SEQLEN, D), 1.0, 6.0, ((0, 2), (1, 16))),
        "mem_keys": scatter_about(arg_keys[4], (NBLK, BLK, D), 1.0, 6.0, ((0, 2), (1, 16))),
        "mem_values": scatter_about(arg_keys[5], (NBLK, BLK, D), 1.0, 6.0, ((0, 2), (1, 16))),
        "seq_lengths": draw_seq_lengths(jax.random.fold_in(arg_keys[10], 71), 0),
        "mem_counts": draw_mem_counts(jax.random.fold_in(arg_keys[10], 71), 0),
        "block_lists": draw_block_lists(jax.random.fold_in(arg_keys[10], 71), 0),
        "block_slots": jax.random.permutation(arg_keys[9], NBLK).astype(jnp.int32),
    }


def head_terms(query_h, key_h, value_h, grad_h, memk_h, memv_h, allow_window, allow_memory):
    scaling = 1.0 / math.sqrt(query_h.shape[1])
    score_w = jnp.dot(query_h, key_h.T, preferred_element_type=jnp.float32) * scaling
    score_m = jnp.dot(query_h, memk_h.T, preferred_element_type=jnp.float32) * scaling
    score_w = jnp.where(allow_window, score_w, -1e+30)
    score_m = jnp.where(allow_memory, score_m, -1e+30)
    row_top = jnp.maximum(lax.optimization_barrier(jnp.max(score_w, axis=1)), lax.optimization_barrier(jnp.max(score_m, axis=1)))
    expo_w = jnp.exp(score_w - row_top[:, None])
    expo_m = jnp.exp(score_m - row_top[:, None])
    totals = lax.optimization_barrier(jnp.sum(expo_w, axis=1)) + lax.optimization_barrier(jnp.sum(expo_m, axis=1))
    prob_w = expo_w / totals[:, None]
    prob_m = expo_m / totals[:, None]
    half_w = prob_w.astype(jnp.bfloat16)
    half_m = prob_m.astype(jnp.bfloat16)
    output = jnp.dot(half_w, value_h, preferred_element_type=jnp.float32) + jnp.dot(half_m, memv_h, preferred_element_type=jnp.float32)
    deltas = lax.optimization_barrier(jnp.sum(grad_h.astype(jnp.float32) * output, axis=1))
    dprob_w = jnp.dot(grad_h, value_h.T, preferred_element_type=jnp.float32)
    dprob_m = jnp.dot(grad_h, memv_h.T, preferred_element_type=jnp.float32)
    dscore_w = (prob_w * (dprob_w - deltas[:, None])).astype(jnp.bfloat16)
    dscore_m = (prob_m * (dprob_m - deltas[:, None])).astype(jnp.bfloat16)
    grad_query = (jnp.dot(dscore_w, key_h, preferred_element_type=jnp.float32) + jnp.dot(dscore_m, memk_h, preferred_element_type=jnp.float32)) * scaling
    grad_key = jnp.dot(dscore_w.T, query_h, preferred_element_type=jnp.float32) * scaling
    grad_value = jnp.dot(half_w.T, grad_h, preferred_element_type=jnp.float32)
    return (grad_query, grad_key, grad_value)

def combine_heads(stacked):
    return jnp.transpose(stacked, (1, 0, 2)).reshape(stacked.shape[1], stacked.shape[0] * stacked.shape[2])

def all_heads(query_rows, key_rows, value_rows, grad_rows, memk_rows, memv_rows, allow_window, allow_memory):
    width = query_rows.shape[1] // H

    def per_head(index):

        def column_slice(tensor):
            return lax.dynamic_slice_in_dim(tensor, index * width, width, 1)
        return head_terms(column_slice(query_rows), column_slice(key_rows), column_slice(value_rows), column_slice(grad_rows), column_slice(memk_rows), column_slice(memv_rows), allow_window, allow_memory)
    grad_query, grad_key, grad_value = lax.map(per_head, jnp.arange(H, dtype=jnp.int32))
    return (combine_heads(grad_query), combine_heads(grad_key), combine_heads(grad_value))

def reference(queries, keys, values, grad_out, mem_keys, mem_values, seq_lengths, mem_counts, block_lists, block_slots):
    reach = WINDOW // TOK_DEV
    padding = reach * TOK_DEV
    nblocks = SEQLEN // TOK_DEV

    def one_user(user):
        length = seq_lengths[user]
        count = mem_counts[user]
        slots = block_slots[block_lists[user]]
        memk_rows = mem_keys[slots].reshape(MB * BLK, D)
        memv_rows = mem_values[slots].reshape(MB * BLK, D)
        zeros_pad = jnp.zeros((padding, D), jnp.bfloat16)
        key_pad = jnp.concatenate([zeros_pad, keys[user]], axis=0)
        value_pad = jnp.concatenate([zeros_pad, values[user]], axis=0)
        event_pos = jnp.arange(SEQLEN, dtype=jnp.int32)
        masked = grad_out[user] * (event_pos < length)[:, None].astype(jnp.bfloat16)
        allow_memory = (jnp.arange(MB * BLK, dtype=jnp.int32) // BLK < count)[None, :]

        def one_block(block):
            start = (block * TOK_DEV).astype(jnp.int32)
            query_rows = lax.dynamic_slice_in_dim(queries[user], start, TOK_DEV, 0)
            grad_rows = lax.dynamic_slice_in_dim(masked, start, TOK_DEV, 0)
            key_rows = lax.dynamic_slice_in_dim(key_pad, start, padding + TOK_DEV, 0)
            value_rows = lax.dynamic_slice_in_dim(value_pad, start, padding + TOK_DEV, 0)
            query_pos = start + jnp.arange(TOK_DEV, dtype=jnp.int32)
            key_pos = start - padding + jnp.arange(padding + TOK_DEV, dtype=jnp.int32)
            allow_window = (key_pos[None, :] <= query_pos[:, None]) & (query_pos[:, None] - key_pos[None, :] < WINDOW) & (key_pos[None, :] >= 0) & ((key_pos[None, :] < length) | (key_pos[None, :] == query_pos[:, None]))
            return all_heads(query_rows, key_rows, value_rows, grad_rows, memk_rows, memv_rows, allow_window, allow_memory)
        grad_query, grad_key, grad_value = lax.map(one_block, jnp.arange(nblocks, dtype=jnp.int32))
        key_total = jnp.zeros((SEQLEN + padding, D), jnp.float32)
        value_total = jnp.zeros((SEQLEN + padding, D), jnp.float32)
        for offset in range(reach + 1):
            key_total = key_total.at[offset * TOK_DEV:offset * TOK_DEV + SEQLEN].add(grad_key[:, offset * TOK_DEV:(offset + 1) * TOK_DEV].reshape(SEQLEN, D))
            value_total = value_total.at[offset * TOK_DEV:offset * TOK_DEV + SEQLEN].add(grad_value[:, offset * TOK_DEV:(offset + 1) * TOK_DEV].reshape(SEQLEN, D))
        return (grad_query.reshape(SEQLEN, D).astype(jnp.bfloat16), key_total[padding:].astype(jnp.bfloat16), value_total[padding:].astype(jnp.bfloat16))
    grad_queries, grad_keys, grad_values = lax.map(one_user, jnp.arange(USERS, dtype=jnp.int32))
    return (grad_queries, grad_keys, grad_values)
```

```python
import functools
import math

import jax
import jax.numpy as jnp
from jax import lax
from jax.experimental import pallas as pl
from jax.experimental.pallas import tpu as pltpu
from jax.sharding import PartitionSpec as P

H = 8
WINDOW = 512
TILE = 256
NEG = -1e30
LOG2E = 1.4426950408889634
VMEM_LIMIT = 48 * 1024 * 1024
VMEM_WHOLE = 64 * 1024 * 1024 - 256 * 1024

NT = (((1,), (1,)), ((), ()))
TN = (((0,), (0,)), ((), ()))


def dot_nt(a, b):
    return lax.dot_general(a, b, NT, preferred_element_type=jnp.float32)


def dot_tn(a, b):
    return lax.dot_general(a, b, TN, preferred_element_type=jnp.float32)


def dot_nn(a, b):
    return jnp.dot(a, b, preferred_element_type=jnp.float32)


def call(body, limit=VMEM_LIMIT, **kw):
    return pl.pallas_call(
        body, compiler_params=pltpu.CompilerParams(vmem_limit_bytes=limit), **kw
    )


def pack_body(slots_ref, lists_ref, q_ref, k_ref, v_ref, g_ref, mk_ref, mv_ref, rows_ref, edge_ref, sems):
    users, blocks = rows_ref.shape[0] + 1, rows_ref.shape[1]
    held = mk_ref.shape[0]
    user = lax.axis_index("dp")
    early = lax.rem(lax.axis_index("seq"), H) < WINDOW // q_ref.shape[1]
    copies = []
    for step in range(1, users):
        other = lax.rem(user + step, users)
        for block in range(blocks):
            index = lax.rem(slots_ref[lists_ref[other, block]], held)
            for part, pool in enumerate((mk_ref, mv_ref)):
                copies.append((pool.at[index], rows_ref.at[step - 1, block, part]))
    copies = [
        pltpu.make_async_copy(src, dst, sems.at[i]) for i, (src, dst) in enumerate(copies)
    ]
    for copy in copies:
        copy.start()
    last = len(copies)

    @pl.when(early)
    def _():
        for part, ref in enumerate((q_ref, g_ref)):
            pltpu.make_async_copy(ref.at[0], edge_ref.at[part], sems.at[last + part]).start()

    @pl.when(jnp.logical_not(early))
    def _():
        for part, ref in enumerate((k_ref, v_ref)):
            pltpu.make_async_copy(ref.at[0], edge_ref.at[part], sems.at[last + part]).start()

    for copy in copies:
        copy.wait()
    for part in range(2):
        pltpu.make_async_copy(q_ref.at[0], edge_ref.at[part], sems.at[last + part]).wait()


def pack(users, block_slots, block_lists, queries, keys, values, grad_out, mem_keys, mem_values):
    _, rows, width = queries.shape
    _, depth, _ = mem_keys.shape
    blocks = block_lists.shape[1]
    smem = pl.BlockSpec(memory_space=pltpu.SMEM)
    hbm = pl.BlockSpec(memory_space=pltpu.HBM)
    return call(
        pack_body,
        limit=VMEM_WHOLE,
        in_specs=[smem] * 2 + [hbm] * 6,
        out_specs=[hbm] * 2,
        out_shape=[
            jax.ShapeDtypeStruct((users - 1, blocks, 2, depth, width), mem_keys.dtype),
            jax.ShapeDtypeStruct((2, rows, width), queries.dtype),
        ],
        scratch_shapes=[pltpu.SemaphoreType.DMA(((users - 1) * blocks * 2 + 2,))],
    )(block_slots, block_lists, queries, keys, values, grad_out, mem_keys, mem_values)


def memory_body(hd, slots_ref, lists_ref, mk_ref, mv_ref, *refs):
    received, out_ref, buffer, sems = refs[:-3], refs[-3], refs[-2], refs[-1]
    users, blocks, depth = len(received) + 1, buffer.shape[0], buffer.shape[2]
    held = mk_ref.shape[0]
    user = lax.axis_index("dp")
    for block in range(blocks):
        slot = slots_ref[lists_ref[user, block]]
        source = lax.rem(user - slot // held + users, users)
        for step in range(users):

            @pl.when(source == step)
            def _():
                for part, pool in enumerate((mk_ref, mv_ref)):
                    if step == 0:
                        src = pool.at[lax.rem(slot, held)]
                    else:
                        src = received[step - 1].at[0, block, part]
                    pltpu.make_async_copy(src, buffer.at[block, part], sems.at[block, part]).start()

    for block in range(blocks):
        for part in range(2):
            pltpu.make_async_copy(mk_ref.at[0], buffer.at[block, part], sems.at[block, part]).wait()
            rows = buffer[block, part]
            for piece in range(out_ref.shape[0]):
                head = piece % H
                out_ref[piece, part, block * depth : (block + 1) * depth] = rows[
                    :, head * hd : (head + 1) * hd
                ]


def memory_pieces(block_slots, block_lists, mem_keys, mem_values, got, pieces):
    _, depth, width = mem_keys.shape
    blocks = block_lists.shape[1]
    hd = width // H
    smem = pl.BlockSpec(memory_space=pltpu.SMEM)
    hbm = pl.BlockSpec(memory_space=pltpu.HBM)
    anywhere = pl.BlockSpec(memory_space=pl.ANY)
    return call(
        functools.partial(memory_body, hd),
        limit=VMEM_WHOLE,
        in_specs=[smem] * 2 + [hbm] * 2 + [anywhere] * len(got),
        out_specs=pl.BlockSpec(memory_space=pltpu.VMEM),
        out_shape=jax.ShapeDtypeStruct((pieces, 2, blocks * depth, hd), mem_keys.dtype),
        scratch_shapes=[
            pltpu.VMEM((blocks, 2, depth, width), mem_keys.dtype),
            pltpu.SemaphoreType.DMA((blocks, 2)),
        ],
    )(block_slots, block_lists, mem_keys, mem_values, *got)


def split_body(hd, length_ref, *refs):
    sources, out_ref, buffer, sems = refs[:4], refs[4], refs[5], refs[6]
    rows = buffer.shape[1]
    copies = [
        pltpu.make_async_copy(source.at[0], buffer.at[part], sems.at[part])
        for part, source in enumerate(sources)
    ]
    for copy in copies:
        copy.start()
    live = length_ref[lax.axis_index("dp")] - lax.axis_index("seq") * rows
    position = lax.broadcasted_iota(jnp.int32, (rows, hd), 0)
    for part, copy in enumerate(copies):
        copy.wait()
        for head in range(H):
            block = buffer[part, :, head * hd : (head + 1) * hd]
            if part == 3:
                block = jnp.where(position < live, block.astype(jnp.float32), 0.0)
            out_ref[head, part] = block.astype(out_ref.dtype)


def split_heads(seq_lengths, *arrays):
    _, rows, width = arrays[0].shape
    hd = width // H
    parts = len(arrays)
    return call(
        functools.partial(split_body, hd),
        limit=VMEM_WHOLE,
        in_specs=[pl.BlockSpec(memory_space=pltpu.SMEM)]
        + [pl.BlockSpec(memory_space=pltpu.HBM)] * parts,
        out_specs=pl.BlockSpec(memory_space=pltpu.VMEM),
        out_shape=jax.ShapeDtypeStruct((H, parts, rows, hd), arrays[0].dtype),
        scratch_shapes=[
            pltpu.VMEM((parts, rows, width), arrays[0].dtype),
            pltpu.SemaphoreType.DMA((parts,)),
        ],
    )(seq_lengths, *arrays)


def edge_body(hd, length_ref, in_ref, _, out_ref):
    rows = in_ref.shape[1]
    reach = WINDOW // rows
    shard = lax.axis_index("seq")
    beyond = length_ref[lax.axis_index("dp")] - (shard + reach) * rows
    live = jnp.where(lax.rem(shard, H) < reach, rows, beyond)
    position = lax.broadcasted_iota(jnp.int32, (rows, hd), 0)
    for head in range(H):
        cols = slice(head * hd, (head + 1) * hd)
        out_ref[head, 0] = in_ref[0, :, cols]
        grad = in_ref[1, :, cols].astype(jnp.float32)
        out_ref[head, 1] = jnp.where(position < live, grad, 0.0).astype(out_ref.dtype)


def split_edge(seq_lengths, edge, later_than):
    _, rows, width = edge.shape
    hd = width // H
    vmem = pl.BlockSpec(memory_space=pltpu.VMEM)
    return call(
        functools.partial(edge_body, hd),
        in_specs=[
            pl.BlockSpec(memory_space=pltpu.SMEM),
            vmem,
            pl.BlockSpec(memory_space=pl.ANY),
        ],
        out_specs=vmem,
        out_shape=jax.ShapeDtypeStruct((H, 2, rows, hd), edge.dtype),
    )(seq_lengths, edge, later_than)


def attend_body(
    scale,
    depth,
    half,
    length_ref,
    count_ref,
    ev_ref,
    edge_ref,
    mem_ref,
    gq_ref,
    gk_ref,
    gv_ref,
    *refs,
):
    k_all, v_all = refs[-2:]
    step = pl.program_id(0)
    hd = ev_ref.shape[-1]
    rows = ev_ref.shape[2]
    reach = WINDOW // rows
    user = lax.axis_index("dp")
    length, count = length_ref[user], count_ref[user]
    base = (lax.axis_index("seq") // H) * (H * rows) + half * WINDOW
    slope = scale * LOG2E
    blocks_per_tile = TILE // rows

    @pl.when(step == 0)
    def _():
        if half == 0:
            k_all[:WINDOW] = edge_ref[:reach, 0].reshape(WINDOW, hd)
            v_all[:WINDOW] = edge_ref[:reach, 1].reshape(WINDOW, hd)
        else:
            k_all[:WINDOW] = ev_ref[:reach, 1].reshape(WINDOW, hd)
            v_all[:WINDOW] = ev_ref[:reach, 2].reshape(WINDOW, hd)
        own = slice(half * reach, (half + 1) * reach)
        k_all[WINDOW:] = ev_ref[own, 1].reshape(WINDOW, hd)
        v_all[WINDOW:] = ev_ref[own, 2].reshape(WINDOW, hd)
        gk_ref[...] = jnp.zeros_like(gk_ref)
        gv_ref[...] = jnp.zeros_like(gv_ref)

    span = WINDOW + TILE
    here = pl.ds(half * reach + step * blocks_per_tile, blocks_per_tile)
    q = ev_ref[here, 0].reshape(TILE, hd)
    g = ev_ref[here, 3].reshape(TILE, hd)
    start = pl.multiple_of(step * TILE, TILE)
    kw = k_all[pl.ds(start, span)]
    vw = v_all[pl.ds(start, span)]
    mk = mem_ref[:, 0].reshape(-1, hd)
    mv = mem_ref[:, 1].reshape(-1, hd)

    qpos = base + start + lax.broadcasted_iota(jnp.int32, (TILE, span), 0)
    kpos = base + start - WINDOW + lax.broadcasted_iota(jnp.int32, (TILE, span), 1)
    allowed = (
        (kpos <= qpos)
        & (qpos - kpos < WINDOW)
        & (kpos >= 0)
        & ((kpos < length) | (kpos == qpos))
    )
    per_source = mem_ref.shape[2]
    memory = mk.shape[0]
    which = lax.rem(lax.broadcasted_iota(jnp.int32, (1, memory), 1), per_source) // depth
    live = which < count

    sw = jnp.where(allowed, dot_nt(q, kw), NEG)
    sm = jnp.where(live, dot_nt(q, mk), NEG)
    top = jnp.maximum(
        jnp.max(sw, axis=1, keepdims=True), jnp.max(sm, axis=1, keepdims=True)
    )
    ew = jnp.exp2((sw - top) * slope)
    em = jnp.exp2((sm - top) * slope)
    dw = dot_nt(g, vw)
    dm = dot_nt(g, mv)
    total = jnp.sum(ew, axis=1, keepdims=True) + jnp.sum(em, axis=1, keepdims=True)
    inv = 1.0 / total
    delta = (
        jnp.sum(ew * dw, axis=1, keepdims=True) + jnp.sum(em * dm, axis=1, keepdims=True)
    ) * inv
    pw = ew * inv
    dsw = (pw * (dw - delta)).astype(jnp.bfloat16)
    dsm = (em * (dm - delta)).astype(jnp.bfloat16)
    gq = (dot_nn(dsw, kw) + dot_nn(dsm, mk) * inv) * scale
    gq_ref[pl.ds(step * blocks_per_tile, blocks_per_tile)] = gq.astype(gq_ref.dtype).reshape(
        blocks_per_tile, rows, hd
    )
    gk_ref[pl.ds(start, span)] += dot_tn(dsw, q) * scale
    gv_ref[pl.ds(start, span)] += dot_tn(pw.astype(jnp.bfloat16), g)
    if half == 0:
        stats_ref = refs[0]
        lane = lax.broadcasted_iota(jnp.int32, (TILE, hd), 1)
        both = jnp.where(lane == 0, top * slope + jnp.log2(total), delta)
        stats_ref[step] = both.T[:8]


def attend(scale, depth, half, seq_lengths, mem_counts, events, edge, memory):
    _, _, rows, hd = events.shape
    reach = WINDOW // rows
    keys = WINDOW + memory.shape[0] * memory.shape[2]
    whole = lambda shape: pl.BlockSpec(shape, lambda t: (0,) * len(shape))
    smem = pl.BlockSpec(memory_space=pltpu.SMEM)
    outs = [((reach, rows, hd), jnp.bfloat16)] + [((2 * WINDOW, hd), jnp.float32)] * 2
    if half == 0:
        outs.append(((WINDOW // TILE, 8, TILE), jnp.float32))
    return call(
        functools.partial(attend_body, scale, depth, half),
        grid=(WINDOW // TILE,),
        in_specs=[smem, smem, whole(events.shape), whole(edge.shape), whole(memory.shape)],
        out_specs=[whole(shape) for shape, _ in outs],
        out_shape=[jax.ShapeDtypeStruct(shape, dtype) for shape, dtype in outs],
        scratch_shapes=[pltpu.VMEM((2 * WINDOW, hd), jnp.bfloat16)] * 2,
        cost_estimate=pl.CostEstimate(
            flops=10 * WINDOW * keys * hd,
            bytes_accessed=4 * keys * hd,
            transcendentals=WINDOW * keys,
        ),
    )(seq_lengths, mem_counts, events, edge, memory)


def finish_body(scale, length_ref, ev_ref, edge_ref, stats_ref, *refs):
    (gq0, gk0, gv0, gq1, gk1, gv1), out_ref = refs[:-1], refs[-1]
    group, _, rows, hd = ev_ref.shape
    reach = WINDOW // rows
    early = group - reach
    number = lax.axis_index("seq") // H
    length = length_ref[lax.axis_index("dp")]
    follows = number + 1 < lax.axis_size("seq") // H
    base = number * (H * rows)
    slope = scale * LOG2E
    span = group * rows

    def put(where, part, value):
        out_ref[where, part] = value.astype(out_ref.dtype).reshape(reach, rows, hd)

    first, last = slice(0, early), slice(early, group)
    out_ref[first, 0] = gq0[...]
    out_ref[last, 0] = gq1[...]
    put(first, 1, gk0[WINDOW:] + gk1[:WINDOW])
    put(first, 2, gv0[WINDOW:] + gv1[:WINDOW])
    k = ev_ref[early:, 1].reshape(WINDOW, hd)
    v = ev_ref[early:, 2].reshape(WINDOW, hd)
    gk = jnp.zeros((WINDOW, hd), jnp.float32)
    gv = jnp.zeros((WINDOW, hd), jnp.float32)
    kpos = base + span - WINDOW + lax.broadcasted_iota(jnp.int32, (WINDOW, TILE), 0)
    for tile in range(WINDOW // TILE):
        blocks = slice(early + tile * TILE // rows, early + (tile + 1) * TILE // rows)
        q = edge_ref[blocks, 0].reshape(TILE, hd)
        g = edge_ref[blocks, 1].reshape(TILE, hd)
        qpos = base + span + tile * TILE + lax.broadcasted_iota(jnp.int32, (WINDOW, TILE), 1)
        allowed = (qpos - kpos < WINDOW) & (kpos < length) & follows
        s = jnp.where(allowed, dot_nt(k, q) * slope - stats_ref[tile, 0:1], NEG)
        p = jnp.exp2(s)
        d = dot_nt(v, g)
        ds = p * (d - stats_ref[tile, 1:2])
        gk += dot_nn(ds.astype(jnp.bfloat16), q)
        gv += dot_nn(p.astype(jnp.bfloat16), g)
    put(last, 1, gk1[WINDOW:] + gk * scale)
    put(last, 2, gv1[WINDOW:] + gv)


def finish(scale, seq_lengths, events, edge, stats, halves):
    group, _, rows, hd = events.shape
    vmem = pl.BlockSpec(memory_space=pltpu.VMEM)
    return call(
        functools.partial(finish_body, scale),
        in_specs=[pl.BlockSpec(memory_space=pltpu.SMEM)] + [vmem] * 9,
        out_specs=vmem,
        out_shape=jax.ShapeDtypeStruct((group, 3, rows, hd), jnp.bfloat16),
    )(seq_lengths, events, edge, stats, *halves)


def join_body(in_ref, *outs):
    hd = in_ref.shape[-1]
    for part, out_ref in enumerate(outs):
        for head in range(H):
            out_ref[0, :, head * hd : (head + 1) * hd] = in_ref[head, part]


def join_heads(pieces):
    heads, parts, rows, hd = pieces.shape
    vmem = pl.BlockSpec(memory_space=pltpu.VMEM)
    return call(
        join_body,
        in_specs=[vmem],
        out_specs=[vmem] * parts,
        out_shape=[jax.ShapeDtypeStruct((1, rows, heads * hd), pieces.dtype)] * parts,
    )(pieces)


def on_device(
    queries,
    keys,
    values,
    grad_out,
    mem_keys,
    mem_values,
    seq_lengths,
    mem_counts,
    block_lists,
    block_slots,
):
    rows, width = queries.shape[1:]
    scale = 1.0 / math.sqrt(width // H)
    reach = WINDOW // rows
    seq, users = lax.axis_size("seq"), lax.axis_size("dp")
    groups = [[first + i for i in range(H)] for first in range(0, seq, H)]
    swap = functools.partial(
        lax.all_to_all, axis_name="seq", split_axis=0, concat_axis=0, tiled=True
    )

    sent, edge = pack(
        users, block_slots, block_lists, queries, keys, values, grad_out, mem_keys, mem_values
    )
    got = []
    for step in range(1, users):
        pairs = [(i, (i + step) % users) for i in range(users)]
        got.append(lax.ppermute(sent[step - 1 : step], "dp", pairs))
    pairs = [(i, i - reach if i % H < reach else i + reach) for i in range(seq)]
    edge = lax.ppermute(edge, "seq", [(i, j) for i, j in pairs if 0 <= j < seq])

    events = split_heads(seq_lengths, queries, keys, values, grad_out)
    events = swap(events, axis_index_groups=groups)
    pieces = memory_pieces(block_slots, block_lists, mem_keys, mem_values, got, seq)
    memory = swap(pieces)
    edge = swap(split_edge(seq_lengths, edge, pieces), axis_index_groups=groups)

    depth = mem_keys.shape[1]
    part = functools.partial(attend, scale, depth)
    *first, stats = part(0, seq_lengths, mem_counts, events, edge, memory)
    stats = lax.ppermute(stats, "seq", [(i + H, i) for i in range(seq - H)])
    second = part(1, seq_lengths, mem_counts, events, edge, memory)
    out = finish(scale, seq_lengths, events, edge, stats, [*first, *second])
    return tuple(join_heads(swap(out, axis_index_groups=groups)))


def solution(mesh):
    spread = P("dp", "seq", None)
    return jax.shard_map(
        on_device,
        mesh=mesh,
        in_specs=(spread,) * 6 + (P(),) * 4,
        out_specs=(spread,) * 3,
        check_vma=False,
    )
```

```python
import functools
import math

import jax
import jax.numpy as jnp
from jax import lax
from jax.experimental import pallas as pl
from jax.experimental.pallas import tpu as pltpu
from jax.sharding import PartitionSpec as P

H = 8
WINDOW = 512
TILE = 256
NEG = -1e30
LOG2E = 1.4426950408889634
VMEM_LIMIT = 48 * 1024 * 1024
VMEM_WHOLE = 64 * 1024 * 1024 - 256 * 1024

NT = (((1,), (1,)), ((), ()))
TN = (((0,), (0,)), ((), ()))


def dot_nt(a, b):
    return lax.dot_general(a, b, NT, preferred_element_type=jnp.float32)


def dot_tn(a, b):
    return lax.dot_general(a, b, TN, preferred_element_type=jnp.float32)


def dot_nn(a, b):
    return jnp.dot(a, b, preferred_element_type=jnp.float32)


def call(body, limit=VMEM_LIMIT, **kw):
    return pl.pallas_call(
        body, compiler_params=pltpu.CompilerParams(vmem_limit_bytes=limit), **kw
    )


def load_listed(user, slots_ref, lists_ref, mk_ref, mv_ref, buffer, sems):
    copies = []
    for block in range(buffer.shape[0]):
        index = lax.rem(slots_ref[lists_ref[user, block]], mk_ref.shape[0])
        for part, pool in enumerate((mk_ref, mv_ref)):
            copies.append(
                pltpu.make_async_copy(
                    pool.at[index], buffer.at[block, part], sems.at[block, part]
                )
            )
    for copy in copies:
        copy.start()
    return copies


def split_parity(buffer, same_ref, other_ref):
    blocks, parts, depth, width = buffer.shape
    hd = width // H
    odd = lax.rem(lax.axis_index("seq"), 2) == 1
    for block in range(blocks):
        rows = slice(block * depth, (block + 1) * depth)
        for part in range(parts):
            for pair in range(H // 2):
                first = buffer[block, part, :, 2 * pair * hd : (2 * pair + 1) * hd]
                second = buffer[block, part, :, (2 * pair + 1) * hd : (2 * pair + 2) * hd]
                same_ref[pair, part, rows] = jnp.where(odd, second, first)
                other_ref[pair, part, rows] = jnp.where(odd, first, second)


def pack_body(step, slots_ref, lists_ref, mk_ref, mv_ref, same_ref, other_ref, buffer, sems):
    user = lax.rem(lax.axis_index("dp") + step, lax.axis_size("dp"))
    copies = load_listed(user, slots_ref, lists_ref, mk_ref, mv_ref, buffer, sems)
    for copy in copies:
        copy.wait()
    split_parity(buffer, same_ref, other_ref)


def listed_scratch(block_lists, mem_keys):
    blocks = block_lists.shape[1]
    return [
        pltpu.VMEM((blocks, 2) + mem_keys.shape[1:], mem_keys.dtype),
        pltpu.SemaphoreType.DMA((blocks, 2)),
    ]


def listed_pieces(block_lists, mem_keys):
    _, depth, width = mem_keys.shape
    shape = (H // 2, 2, block_lists.shape[1] * depth, width // H)
    return jax.ShapeDtypeStruct(shape, mem_keys.dtype)


def pack(step, block_slots, block_lists, mem_keys, mem_values):
    smem = pl.BlockSpec(memory_space=pltpu.SMEM)
    hbm = pl.BlockSpec(memory_space=pltpu.HBM)
    return call(
        functools.partial(pack_body, step),
        limit=VMEM_WHOLE,
        in_specs=[smem] * 2 + [hbm] * 2,
        out_specs=[pl.BlockSpec(memory_space=pltpu.VMEM)] * 2,
        out_shape=[listed_pieces(block_lists, mem_keys)] * 2,
        scratch_shapes=listed_scratch(block_lists, mem_keys),
    )(block_slots, block_lists, mem_keys, mem_values)


def split_body(hd, length_ref, slots_ref, lists_ref, *refs):
    sources, (mk_ref, mv_ref, _, out_ref, same_ref, other_ref) = refs[:4], refs[4:10]
    buffer, sems, listed, listed_sems = refs[10:]
    rows = buffer.shape[1]
    copies = [
        pltpu.make_async_copy(source.at[0], buffer.at[part], sems.at[part])
        for part, source in enumerate(sources)
    ]
    for copy in copies:
        copy.start()
    user = lax.axis_index("dp")
    more = load_listed(user, slots_ref, lists_ref, mk_ref, mv_ref, listed, listed_sems)
    live = length_ref[user] - lax.axis_index("seq") * rows
    position = lax.broadcasted_iota(jnp.int32, (rows, hd), 0)
    for part, copy in enumerate(copies):
        copy.wait()
        for head in range(H):
            block = buffer[part, :, head * hd : (head + 1) * hd]
            if part == 3:
                block = jnp.where(position < live, block.astype(jnp.float32), 0.0)
            out_ref[head, part] = block.astype(out_ref.dtype)
    for copy in more:
        copy.wait()
    split_parity(listed, same_ref, other_ref)


def split_heads(seq_lengths, block_slots, block_lists, arrays, mem_keys, mem_values, later_than):
    _, rows, width = arrays[0].shape
    parts = len(arrays)
    hbm = pl.BlockSpec(memory_space=pltpu.HBM)
    return call(
        functools.partial(split_body, width // H),
        limit=VMEM_WHOLE,
        in_specs=[pl.BlockSpec(memory_space=pltpu.SMEM)] * 3
        + [hbm] * (parts + 2)
        + [pl.BlockSpec(memory_space=pl.ANY)],
        out_specs=[pl.BlockSpec(memory_space=pltpu.VMEM)] * 3,
        out_shape=[jax.ShapeDtypeStruct((H, parts, rows, width // H), arrays[0].dtype)]
        + [listed_pieces(block_lists, mem_keys)] * 2,
        scratch_shapes=[
            pltpu.VMEM((parts, rows, width), arrays[0].dtype),
            pltpu.SemaphoreType.DMA((parts,)),
        ]
        + listed_scratch(block_lists, mem_keys),
    )(seq_lengths, block_slots, block_lists, *arrays, mem_keys, mem_values, later_than)


def memory_body(held, depth, slots_ref, lists_ref, *refs):
    outs = refs[-(H // 2) :]
    sources = refs[: -(H // 2)]
    users = len(sources) // 2
    user = lax.axis_index("dp")
    pair = lax.rem(lax.axis_index("seq") // 2, H // 2)
    for block in range(lists_ref.shape[1]):
        slot = slots_ref[lists_ref[user, block]]
        source = lax.rem(user - slot // held + users, users)
        rows = slice(block * depth, (block + 1) * depth)
        for step, out_ref in enumerate(outs):
            for side in range(2):
                for part in range(2):
                    value = sources[side][pair ^ step, part, rows]
                    for other in range(1, users):
                        value = jnp.where(
                            source == other, sources[2 * other + side][pair ^ step, part, rows], value
                        )
                    out_ref[part, side, rows] = value


def memory_pieces(held, depth, block_slots, block_lists, sources):
    _, parts, rows, hd = sources[0].shape
    smem = pl.BlockSpec(memory_space=pltpu.SMEM)
    vmem = pl.BlockSpec(memory_space=pltpu.VMEM)
    return call(
        functools.partial(memory_body, held, depth),
        in_specs=[smem] * 2 + [vmem] * len(sources),
        out_specs=[vmem] * (H // 2),
        out_shape=[jax.ShapeDtypeStruct((parts, 2, rows, hd), sources[0].dtype)] * (H // 2),
    )(block_slots, block_lists, *sources)


def attend_body(
    scale,
    depth,
    half,
    memories,
    length_ref,
    count_ref,
    ev_ref,
    halo_ref,
    *refs,
):
    mem_refs, (gq_ref, gk_ref, gv_ref) = refs[:memories], refs[memories : memories + 3]
    k_all, v_all, mk_all, mv_all = refs[-4:]
    step = pl.program_id(0)
    hd = ev_ref.shape[-1]
    rows = ev_ref.shape[2]
    reach = WINDOW // rows
    user = lax.axis_index("dp")
    length, count = length_ref[user], count_ref[user]
    base = (lax.axis_index("seq") // H) * (H * rows) + half * WINDOW
    slope = scale * LOG2E
    blocks_per_tile = TILE // rows

    @pl.when(step == 0)
    def _():
        if half == 0:
            k_all[:WINDOW] = halo_ref[:, 0].reshape(WINDOW, hd)
            v_all[:WINDOW] = halo_ref[:, 1].reshape(WINDOW, hd)
        else:
            k_all[:WINDOW] = ev_ref[:reach, 1].reshape(WINDOW, hd)
            v_all[:WINDOW] = ev_ref[:reach, 2].reshape(WINDOW, hd)
        own = slice(half * reach, (half + 1) * reach)
        k_all[WINDOW:] = ev_ref[own, 1].reshape(WINDOW, hd)
        v_all[WINDOW:] = ev_ref[own, 2].reshape(WINDOW, hd)
        gk_ref[...] = jnp.zeros_like(gk_ref)
        gv_ref[...] = jnp.zeros_like(gv_ref)
        size = mk_all.shape[0] // memories
        for i, mem_ref in enumerate(mem_refs):
            mk_all[i * size : (i + 1) * size] = mem_ref[0].reshape(size, hd)
            mv_all[i * size : (i + 1) * size] = mem_ref[1].reshape(size, hd)

    span = WINDOW + TILE
    here = pl.ds(half * reach + step * blocks_per_tile, blocks_per_tile)
    q = ev_ref[here, 0].reshape(TILE, hd)
    g = ev_ref[here, 3].reshape(TILE, hd)
    start = pl.multiple_of(step * TILE, TILE)
    kw = k_all[pl.ds(start, span)]
    vw = v_all[pl.ds(start, span)]
    mk = mk_all[...]
    mv = mv_all[...]

    qpos = base + start + lax.broadcasted_iota(jnp.int32, (TILE, span), 0)
    kpos = base + start - WINDOW + lax.broadcasted_iota(jnp.int32, (TILE, span), 1)
    allowed = (
        (kpos <= qpos)
        & (qpos - kpos < WINDOW)
        & (kpos >= 0)
        & ((kpos < length) | (kpos == qpos))
    )
    per_source = mem_refs[0].shape[2]
    memory = mk.shape[0]
    which = lax.rem(lax.broadcasted_iota(jnp.int32, (1, memory), 1), per_source) // depth
    live = which < count

    sw = jnp.where(allowed, dot_nt(q, kw), NEG)
    sm = jnp.where(live, dot_nt(q, mk), NEG)
    top = jnp.maximum(
        jnp.max(sw, axis=1, keepdims=True), jnp.max(sm, axis=1, keepdims=True)
    )
    ew = jnp.exp2((sw - top) * slope)
    em = jnp.exp2((sm - top) * slope)
    dw = dot_nt(g, vw)
    dm = dot_nt(g, mv)
    total = jnp.sum(ew, axis=1, keepdims=True) + jnp.sum(em, axis=1, keepdims=True)
    inv = 1.0 / total
    delta = (
        jnp.sum(ew * dw, axis=1, keepdims=True) + jnp.sum(em * dm, axis=1, keepdims=True)
    ) * inv
    pw = ew * inv
    dsw = (pw * (dw - delta)).astype(jnp.bfloat16)
    dsm = (em * (dm - delta)).astype(jnp.bfloat16)
    gq = (dot_nn(dsw, kw) + dot_nn(dsm, mk) * inv) * scale
    gq_ref[pl.ds(step * blocks_per_tile, blocks_per_tile)] = gq.astype(gq_ref.dtype).reshape(
        blocks_per_tile, rows, hd
    )
    gk_ref[pl.ds(start, span)] += dot_tn(dsw, q) * scale
    gv_ref[pl.ds(start, span)] += dot_tn(pw.astype(jnp.bfloat16), g)
    if half == 0:
        stats_ref = refs[memories + 3]
        lane = lax.broadcasted_iota(jnp.int32, (TILE, hd), 1)
        both = jnp.where(lane == 0, top * slope + jnp.log2(total), delta)
        stats_ref[step] = both.T[:8]


def attend(scale, depth, half, seq_lengths, mem_counts, events, halo, memory):
    _, _, rows, hd = events.shape
    reach = WINDOW // rows
    memories = memory[0].shape[1] * memory[0].shape[2] * len(memory)
    keys = WINDOW + memories
    whole = lambda shape: pl.BlockSpec(shape, lambda t: (0,) * len(shape))
    smem = pl.BlockSpec(memory_space=pltpu.SMEM)
    outs = [((reach, rows, hd), jnp.bfloat16)] + [((2 * WINDOW, hd), jnp.float32)] * 2
    if half == 0:
        outs.append(((WINDOW // TILE, 8, TILE), jnp.float32))
    return call(
        functools.partial(attend_body, scale, depth, half, len(memory)),
        grid=(WINDOW // TILE,),
        in_specs=[smem, smem, whole(events.shape), whole(halo.shape)]
        + [whole(piece.shape) for piece in memory],
        out_specs=[whole(shape) for shape, _ in outs],
        out_shape=[jax.ShapeDtypeStruct(shape, dtype) for shape, dtype in outs],
        scratch_shapes=[pltpu.VMEM((2 * WINDOW, hd), jnp.bfloat16)] * 2
        + [pltpu.VMEM((memories, hd), jnp.bfloat16)] * 2,
        cost_estimate=pl.CostEstimate(
            flops=10 * WINDOW * keys * hd,
            bytes_accessed=4 * keys * hd,
            transcendentals=WINDOW * keys,
        ),
    )(seq_lengths, mem_counts, events, halo, *memory)


def finish_body(scale, length_ref, ev_ref, after_ref, stats_ref, *refs):
    (gq0, gk0, gv0, gq1, gk1, gv1), out_ref = refs[:-1], refs[-1]
    group, _, rows, hd = ev_ref.shape
    reach = WINDOW // rows
    early = group - reach
    number = lax.axis_index("seq") // H
    length = length_ref[lax.axis_index("dp")]
    follows = number + 1 < lax.axis_size("seq") // H
    base = number * (H * rows)
    slope = scale * LOG2E
    span = group * rows

    def put(where, part, value):
        out_ref[where, part] = value.astype(out_ref.dtype).reshape(reach, rows, hd)

    first, last = slice(0, early), slice(early, group)
    out_ref[first, 0] = gq0[...]
    out_ref[last, 0] = gq1[...]
    put(first, 1, gk0[WINDOW:] + gk1[:WINDOW])
    put(first, 2, gv0[WINDOW:] + gv1[:WINDOW])
    k = ev_ref[early:, 1].reshape(WINDOW, hd)
    v = ev_ref[early:, 2].reshape(WINDOW, hd)
    gk = jnp.zeros((WINDOW, hd), jnp.float32)
    gv = jnp.zeros((WINDOW, hd), jnp.float32)
    kpos = base + span - WINDOW + lax.broadcasted_iota(jnp.int32, (WINDOW, TILE), 0)
    for tile in range(WINDOW // TILE):
        blocks = slice(tile * TILE // rows, (tile + 1) * TILE // rows)
        q = after_ref[blocks, 0].reshape(TILE, hd)
        g = after_ref[blocks, 1].reshape(TILE, hd)
        qpos = base + span + tile * TILE + lax.broadcasted_iota(jnp.int32, (WINDOW, TILE), 1)
        allowed = (qpos - kpos < WINDOW) & (kpos < length) & follows
        s = jnp.where(allowed, dot_nt(k, q) * slope - stats_ref[tile, 0:1], NEG)
        p = jnp.exp2(s)
        d = dot_nt(v, g)
        ds = p * (d - stats_ref[tile, 1:2])
        gk += dot_nn(ds.astype(jnp.bfloat16), q)
        gv += dot_nn(p.astype(jnp.bfloat16), g)
    put(last, 1, gk1[WINDOW:] + gk * scale)
    put(last, 2, gv1[WINDOW:] + gv)


def finish(scale, seq_lengths, events, after, stats, halves):
    group, _, rows, hd = events.shape
    vmem = pl.BlockSpec(memory_space=pltpu.VMEM)
    return call(
        functools.partial(finish_body, scale),
        in_specs=[pl.BlockSpec(memory_space=pltpu.SMEM)] + [vmem] * 9,
        out_specs=vmem,
        out_shape=jax.ShapeDtypeStruct((group, 3, rows, hd), jnp.bfloat16),
    )(seq_lengths, events, after, stats, *halves)


def join_body(in_ref, *outs):
    hd = in_ref.shape[-1]
    for part, out_ref in enumerate(outs):
        for head in range(H):
            out_ref[0, :, head * hd : (head + 1) * hd] = in_ref[head, part]


def join_heads(pieces):
    heads, parts, rows, hd = pieces.shape
    vmem = pl.BlockSpec(memory_space=pltpu.VMEM)
    return call(
        join_body,
        in_specs=[vmem],
        out_specs=[vmem] * parts,
        out_shape=[jax.ShapeDtypeStruct((1, rows, heads * hd), pieces.dtype)] * parts,
    )(pieces)


def on_device(
    queries,
    keys,
    values,
    grad_out,
    mem_keys,
    mem_values,
    seq_lengths,
    mem_counts,
    block_lists,
    block_slots,
):
    rows, width = queries.shape[1:]
    scale = 1.0 / math.sqrt(width // H)
    reach = WINDOW // rows
    seq, users = lax.axis_size("seq"), lax.axis_size("dp")
    groups = [[first + i for i in range(H)] for first in range(0, seq, H)]
    swap = functools.partial(
        lax.all_to_all, axis_name="seq", split_axis=0, concat_axis=0, tiled=True
    )

    same, cross = [], []
    for step in range(1, users):
        for_same, for_other = pack(step, block_slots, block_lists, mem_keys, mem_values)
        places = [(u, i) for u in range(users) for i in range(seq)]
        to = lambda u, i: ((u + step) % users) * seq + i
        same.append(
            lax.ppermute(for_same, ("dp", "seq"), [(u * seq + i, to(u, i)) for u, i in places])
        )
        cross.append(
            lax.ppermute(
                for_other, ("dp", "seq"), [(u * seq + i, to(u, i ^ 1)) for u, i in places]
            )
        )
    events, own_same, own_other = split_heads(
        seq_lengths,
        block_slots,
        block_lists,
        (queries, keys, values, grad_out),
        mem_keys,
        mem_values,
        for_same,
    )
    own_other = lax.ppermute(own_other, "seq", [(i, i ^ 1) for i in range(seq)])
    events = swap(events, axis_index_groups=groups)

    sources = [own_same, own_other]
    for pieces in zip(same, cross):
        sources.extend(pieces)
    held, depth = mem_keys.shape[:2]
    pieces = memory_pieces(held, depth, block_slots, block_lists, sources)
    memory = []
    for around in range(seq // H - 1, -1, -1):
        for step, piece in enumerate(pieces):
            if around == 0 and step == 0:
                memory.append(piece)
                continue
            pairs = [
                (i, ((i // H + around) * H) % seq + ((i % H) ^ (2 * step))) for i in range(seq)
            ]
            memory.append(lax.ppermute(piece, "seq", pairs))

    forward = [(i, i + H) for i in range(seq - H)]
    backward = [(i + H, i) for i in range(seq - H)]
    halo = lax.ppermute(events[H - reach :, 1:3], "seq", forward)
    after = lax.ppermute(events[:reach, 0::3], "seq", backward)

    part = functools.partial(attend, scale, depth)
    *first, stats = part(0, seq_lengths, mem_counts, events, halo, memory)
    stats = lax.ppermute(stats, "seq", backward)
    second = part(1, seq_lengths, mem_counts, events, halo, memory)
    out = finish(scale, seq_lengths, events, after, stats, [*first, *second])
    return tuple(join_heads(swap(out, axis_index_groups=groups)))


def solution(mesh):
    spread = P("dp", "seq", None)
    return jax.shard_map(
        on_device,
        mesh=mesh,
        in_specs=(spread,) * 6 + (P(),) * 4,
        out_specs=(spread,) * 3,
        check_vma=False,
    )
```

```python
import functools
import math

import jax
import jax.numpy as jnp
from jax import lax
from jax.experimental import pallas as pl
from jax.experimental.pallas import tpu as pltpu
from jax.sharding import PartitionSpec as P

H = 8
WINDOW = 512
TILE = 256
NEG = -1e30
LOG2E = 1.4426950408889634
VMEM_LIMIT = 48 * 1024 * 1024
VMEM_WHOLE = 64 * 1024 * 1024 - 256 * 1024

NT = (((1,), (1,)), ((), ()))
TN = (((0,), (0,)), ((), ()))


def dot_nt(a, b):
    return lax.dot_general(a, b, NT, preferred_element_type=jnp.float32)


def dot_tn(a, b):
    return lax.dot_general(a, b, TN, preferred_element_type=jnp.float32)


def dot_nn(a, b):
    return jnp.dot(a, b, preferred_element_type=jnp.float32)


def call(body, limit=VMEM_LIMIT, **kw):
    return pl.pallas_call(
        body, compiler_params=pltpu.CompilerParams(vmem_limit_bytes=limit), **kw
    )


def load_listed(user, slots_ref, lists_ref, mk_ref, mv_ref, buffer, sems):
    copies = []
    for block in range(buffer.shape[0]):
        index = lax.rem(slots_ref[lists_ref[user, block]], mk_ref.shape[0])
        for part, pool in enumerate((mk_ref, mv_ref)):
            copies.append(
                pltpu.make_async_copy(
                    pool.at[index], buffer.at[block, part], sems.at[block, part]
                )
            )
    for copy in copies:
        copy.start()
    return copies


def split_parity(buffer, same_ref, other_ref):
    blocks, parts, depth, width = buffer.shape
    hd = width // H
    odd = lax.rem(lax.axis_index("seq"), 2) == 1
    for block in range(blocks):
        rows = slice(block * depth, (block + 1) * depth)
        for part in range(parts):
            for pair in range(H // 2):
                first = buffer[block, part, :, 2 * pair * hd : (2 * pair + 1) * hd]
                second = buffer[block, part, :, (2 * pair + 1) * hd : (2 * pair + 2) * hd]
                same_ref[pair, part, rows] = jnp.where(odd, second, first)
                other_ref[pair, part, rows] = jnp.where(odd, first, second)


def pack_body(users, slots_ref, lists_ref, *refs):
    (q_ref, k_ref, v_ref, g_ref, mk_ref, mv_ref), refs = refs[:6], refs[6:]
    same, other, edge_ref = refs[:users], refs[users : 2 * users], refs[2 * users]
    buffer, sems, edge_sems = refs[2 * users + 1 :]
    user = lax.axis_index("dp")
    early = lax.rem(lax.axis_index("seq"), H) < WINDOW // q_ref.shape[1]
    loads = [
        load_listed(
            lax.rem(user + step, users),
            slots_ref,
            lists_ref,
            mk_ref,
            mv_ref,
            buffer.at[step],
            sems.at[step],
        )
        for step in range(users)
    ]

    @pl.when(early)
    def _():
        for part, ref in enumerate((q_ref, g_ref)):
            pltpu.make_async_copy(ref.at[0], edge_ref.at[part], edge_sems.at[part]).start()

    @pl.when(jnp.logical_not(early))
    def _():
        for part, ref in enumerate((k_ref, v_ref)):
            pltpu.make_async_copy(ref.at[0], edge_ref.at[part], edge_sems.at[part]).start()

    for step in range(users):
        for copy in loads[step]:
            copy.wait()
        split_parity(buffer.at[step], same[step], other[step])
    for part in range(2):
        pltpu.make_async_copy(q_ref.at[0], edge_ref.at[part], edge_sems.at[part]).wait()


def pack(users, block_slots, block_lists, events, mem_keys, mem_values):
    _, depth, width = mem_keys.shape
    blocks = block_lists.shape[1]
    rows = events[0].shape[1]
    dtype = mem_keys.dtype
    smem = pl.BlockSpec(memory_space=pltpu.SMEM)
    hbm = pl.BlockSpec(memory_space=pltpu.HBM)
    pieces = jax.ShapeDtypeStruct((H // 2, 2, blocks * depth, width // H), dtype)
    return call(
        functools.partial(pack_body, users),
        limit=VMEM_WHOLE,
        in_specs=[smem] * 2 + [hbm] * 6,
        out_specs=[pl.BlockSpec(memory_space=pltpu.VMEM)] * (2 * users + 1),
        out_shape=[pieces] * (2 * users) + [jax.ShapeDtypeStruct((2, rows, width), dtype)],
        scratch_shapes=[
            pltpu.VMEM((users, blocks, 2, depth, width), dtype),
            pltpu.SemaphoreType.DMA((users, blocks, 2)),
            pltpu.SemaphoreType.DMA((2,)),
        ],
    )(block_slots, block_lists, *events, mem_keys, mem_values)


def split_body(hd, length_ref, *refs):
    sources, (_, out_ref, buffer, sems) = refs[:4], refs[4:]
    rows = buffer.shape[1]
    copies = [
        pltpu.make_async_copy(source.at[0], buffer.at[part], sems.at[part])
        for part, source in enumerate(sources)
    ]
    for copy in copies:
        copy.start()
    live = length_ref[lax.axis_index("dp")] - lax.axis_index("seq") * rows
    position = lax.broadcasted_iota(jnp.int32, (rows, hd), 0)
    for part, copy in enumerate(copies):
        copy.wait()
        for head in range(H):
            block = buffer[part, :, head * hd : (head + 1) * hd]
            if part == 3:
                block = jnp.where(position < live, block.astype(jnp.float32), 0.0)
            out_ref[head, part] = block.astype(out_ref.dtype)


def split_heads(seq_lengths, arrays, later_than):
    _, rows, width = arrays[0].shape
    parts = len(arrays)
    hbm = pl.BlockSpec(memory_space=pltpu.HBM)
    return call(
        functools.partial(split_body, width // H),
        limit=VMEM_WHOLE,
        in_specs=[pl.BlockSpec(memory_space=pltpu.SMEM)]
        + [hbm] * parts
        + [pl.BlockSpec(memory_space=pl.ANY)],
        out_specs=pl.BlockSpec(memory_space=pltpu.VMEM),
        out_shape=jax.ShapeDtypeStruct((H, parts, rows, width // H), arrays[0].dtype),
        scratch_shapes=[
            pltpu.VMEM((parts, rows, width), arrays[0].dtype),
            pltpu.SemaphoreType.DMA((parts,)),
        ],
    )(seq_lengths, *arrays, later_than)


def edge_body(hd, length_ref, in_ref, *refs):
    out_ref = refs[-1]
    rows = in_ref.shape[1]
    reach = WINDOW // rows
    shard = lax.axis_index("seq")
    beyond = length_ref[lax.axis_index("dp")] - (shard + reach) * rows
    live = jnp.where(lax.rem(shard, H) < reach, rows, beyond)
    position = lax.broadcasted_iota(jnp.int32, (rows, hd), 0)
    for head in range(H):
        cols = slice(head * hd, (head + 1) * hd)
        out_ref[head, 0] = in_ref[0, :, cols]
        grad = in_ref[1, :, cols].astype(jnp.float32)
        out_ref[head, 1] = jnp.where(position < live, grad, 0.0).astype(out_ref.dtype)


def split_edge(seq_lengths, edge, *later_than):
    _, rows, width = edge.shape
    hd = width // H
    vmem = pl.BlockSpec(memory_space=pltpu.VMEM)
    return call(
        functools.partial(edge_body, hd),
        in_specs=[pl.BlockSpec(memory_space=pltpu.SMEM), vmem]
        + [pl.BlockSpec(memory_space=pl.ANY)] * len(later_than),
        out_specs=vmem,
        out_shape=jax.ShapeDtypeStruct((H, 2, rows, hd), edge.dtype),
    )(seq_lengths, edge, *later_than)


def memory_body(held, depth, slots_ref, lists_ref, _, *refs):
    outs = refs[-(H // 2) :]
    sources = refs[: -(H // 2)]
    users = len(sources) // 2
    user = lax.axis_index("dp")
    pair = lax.rem(lax.axis_index("seq") // 2, H // 2)
    for block in range(lists_ref.shape[1]):
        slot = slots_ref[lists_ref[user, block]]
        source = lax.rem(user - slot // held + users, users)
        rows = slice(block * depth, (block + 1) * depth)
        for step, out_ref in enumerate(outs):
            for side in range(2):
                for part in range(2):
                    value = sources[side][pair ^ step, part, rows]
                    for other in range(1, users):
                        value = jnp.where(
                            source == other, sources[2 * other + side][pair ^ step, part, rows], value
                        )
                    out_ref[part, side, rows] = value


def memory_pieces(held, depth, block_slots, block_lists, sources, later_than):
    _, parts, rows, hd = sources[0].shape
    smem = pl.BlockSpec(memory_space=pltpu.SMEM)
    vmem = pl.BlockSpec(memory_space=pltpu.VMEM)
    return call(
        functools.partial(memory_body, held, depth),
        in_specs=[smem] * 2 + [pl.BlockSpec(memory_space=pl.ANY)] + [vmem] * len(sources),
        out_specs=[vmem] * (H // 2),
        out_shape=[jax.ShapeDtypeStruct((parts, 2, rows, hd), sources[0].dtype)] * (H // 2),
    )(block_slots, block_lists, later_than, *sources)


def attend_body(
    scale,
    depth,
    half,
    memories,
    length_ref,
    count_ref,
    ev_ref,
    edge_ref,
    *refs,
):
    mem_refs, (gq_ref, gk_ref, gv_ref) = refs[:memories], refs[memories : memories + 3]
    k_all, v_all, mk_all, mv_all = refs[-4:]
    step = pl.program_id(0)
    hd = ev_ref.shape[-1]
    rows = ev_ref.shape[2]
    reach = WINDOW // rows
    user = lax.axis_index("dp")
    length, count = length_ref[user], count_ref[user]
    base = (lax.axis_index("seq") // H) * (H * rows) + half * WINDOW
    slope = scale * LOG2E
    blocks_per_tile = TILE // rows

    @pl.when(step == 0)
    def _():
        if half == 0:
            k_all[:WINDOW] = edge_ref[:reach, 0].reshape(WINDOW, hd)
            v_all[:WINDOW] = edge_ref[:reach, 1].reshape(WINDOW, hd)
        else:
            k_all[:WINDOW] = ev_ref[:reach, 1].reshape(WINDOW, hd)
            v_all[:WINDOW] = ev_ref[:reach, 2].reshape(WINDOW, hd)
        own = slice(half * reach, (half + 1) * reach)
        k_all[WINDOW:] = ev_ref[own, 1].reshape(WINDOW, hd)
        v_all[WINDOW:] = ev_ref[own, 2].reshape(WINDOW, hd)
        gk_ref[...] = jnp.zeros_like(gk_ref)
        gv_ref[...] = jnp.zeros_like(gv_ref)
        size = mk_all.shape[0] // memories
        for i, mem_ref in enumerate(mem_refs):
            mk_all[i * size : (i + 1) * size] = mem_ref[0].reshape(size, hd)
            mv_all[i * size : (i + 1) * size] = mem_ref[1].reshape(size, hd)

    span = WINDOW + TILE
    here = pl.ds(half * reach + step * blocks_per_tile, blocks_per_tile)
    q = ev_ref[here, 0].reshape(TILE, hd)
    g = ev_ref[here, 3].reshape(TILE, hd)
    start = pl.multiple_of(step * TILE, TILE)
    kw = k_all[pl.ds(start, span)]
    vw = v_all[pl.ds(start, span)]
    mk = mk_all[...]
    mv = mv_all[...]

    qpos = base + start + lax.broadcasted_iota(jnp.int32, (TILE, span), 0)
    kpos = base + start - WINDOW + lax.broadcasted_iota(jnp.int32, (TILE, span), 1)
    allowed = (
        (kpos <= qpos)
        & (qpos - kpos < WINDOW)
        & (kpos >= 0)
        & ((kpos < length) | (kpos == qpos))
    )
    per_source = mem_refs[0].shape[2]
    memory = mk.shape[0]
    which = lax.rem(lax.broadcasted_iota(jnp.int32, (1, memory), 1), per_source) // depth
    live = which < count

    sw = jnp.where(allowed, dot_nt(q, kw), NEG)
    sm = jnp.where(live, dot_nt(q, mk), NEG)
    top = jnp.maximum(
        jnp.max(sw, axis=1, keepdims=True), jnp.max(sm, axis=1, keepdims=True)
    )
    ew = jnp.exp2((sw - top) * slope)
    em = jnp.exp2((sm - top) * slope)
    dw = dot_nt(g, vw)
    dm = dot_nt(g, mv)
    total = jnp.sum(ew, axis=1, keepdims=True) + jnp.sum(em, axis=1, keepdims=True)
    inv = 1.0 / total
    delta = (
        jnp.sum(ew * dw, axis=1, keepdims=True) + jnp.sum(em * dm, axis=1, keepdims=True)
    ) * inv
    pw = ew * inv
    dsw = (pw * (dw - delta)).astype(jnp.bfloat16)
    dsm = (em * (dm - delta)).astype(jnp.bfloat16)
    gq = (dot_nn(dsw, kw) + dot_nn(dsm, mk) * inv) * scale
    gq_ref[pl.ds(step * blocks_per_tile, blocks_per_tile)] = gq.astype(gq_ref.dtype).reshape(
        blocks_per_tile, rows, hd
    )
    gk_ref[pl.ds(start, span)] += dot_tn(dsw, q) * scale
    gv_ref[pl.ds(start, span)] += dot_tn(pw.astype(jnp.bfloat16), g)
    if half == 0:
        stats_ref = refs[memories + 3]
        lane = lax.broadcasted_iota(jnp.int32, (TILE, hd), 1)
        both = jnp.where(lane == 0, top * slope + jnp.log2(total), delta)
        stats_ref[step] = both.T[:8]


def attend(scale, depth, half, seq_lengths, mem_counts, events, edge, memory):
    _, _, rows, hd = events.shape
    reach = WINDOW // rows
    memories = memory[0].shape[1] * memory[0].shape[2] * len(memory)
    keys = WINDOW + memories
    whole = lambda shape: pl.BlockSpec(shape, lambda t: (0,) * len(shape))
    smem = pl.BlockSpec(memory_space=pltpu.SMEM)
    outs = [((reach, rows, hd), jnp.bfloat16)] + [((2 * WINDOW, hd), jnp.float32)] * 2
    if half == 0:
        outs.append(((WINDOW // TILE, 8, TILE), jnp.float32))
    return call(
        functools.partial(attend_body, scale, depth, half, len(memory)),
        grid=(WINDOW // TILE,),
        in_specs=[smem, smem, whole(events.shape), whole(edge.shape)]
        + [whole(piece.shape) for piece in memory],
        out_specs=[whole(shape) for shape, _ in outs],
        out_shape=[jax.ShapeDtypeStruct(shape, dtype) for shape, dtype in outs],
        scratch_shapes=[pltpu.VMEM((2 * WINDOW, hd), jnp.bfloat16)] * 2
        + [pltpu.VMEM((memories, hd), jnp.bfloat16)] * 2,
        cost_estimate=pl.CostEstimate(
            flops=10 * WINDOW * keys * hd,
            bytes_accessed=4 * keys * hd,
            transcendentals=WINDOW * keys,
        ),
    )(seq_lengths, mem_counts, events, edge, *memory)


def finish_body(scale, length_ref, ev_ref, edge_ref, stats_ref, *refs):
    (gq0, gk0, gv0, gq1, gk1, gv1), out_ref = refs[:-1], refs[-1]
    group, _, rows, hd = ev_ref.shape
    reach = WINDOW // rows
    early = group - reach
    number = lax.axis_index("seq") // H
    length = length_ref[lax.axis_index("dp")]
    follows = number + 1 < lax.axis_size("seq") // H
    base = number * (H * rows)
    slope = scale * LOG2E
    span = group * rows

    def put(where, part, value):
        out_ref[where, part] = value.astype(out_ref.dtype).reshape(reach, rows, hd)

    first, last = slice(0, early), slice(early, group)
    out_ref[first, 0] = gq0[...]
    out_ref[last, 0] = gq1[...]
    put(first, 1, gk0[WINDOW:] + gk1[:WINDOW])
    put(first, 2, gv0[WINDOW:] + gv1[:WINDOW])
    k = ev_ref[early:, 1].reshape(WINDOW, hd)
    v = ev_ref[early:, 2].reshape(WINDOW, hd)
    gk = jnp.zeros((WINDOW, hd), jnp.float32)
    gv = jnp.zeros((WINDOW, hd), jnp.float32)
    kpos = base + span - WINDOW + lax.broadcasted_iota(jnp.int32, (WINDOW, TILE), 0)
    for tile in range(WINDOW // TILE):
        blocks = slice(early + tile * TILE // rows, early + (tile + 1) * TILE // rows)
        q = edge_ref[blocks, 0].reshape(TILE, hd)
        g = edge_ref[blocks, 1].reshape(TILE, hd)
        qpos = base + span + tile * TILE + lax.broadcasted_iota(jnp.int32, (WINDOW, TILE), 1)
        allowed = (qpos - kpos < WINDOW) & (kpos < length) & follows
        s = jnp.where(allowed, dot_nt(k, q) * slope - stats_ref[tile, 0:1], NEG)
        p = jnp.exp2(s)
        d = dot_nt(v, g)
        ds = p * (d - stats_ref[tile, 1:2])
        gk += dot_nn(ds.astype(jnp.bfloat16), q)
        gv += dot_nn(p.astype(jnp.bfloat16), g)
    put(last, 1, gk1[WINDOW:] + gk * scale)
    put(last, 2, gv1[WINDOW:] + gv)


def finish(scale, seq_lengths, events, edge, stats, halves):
    group, _, rows, hd = events.shape
    vmem = pl.BlockSpec(memory_space=pltpu.VMEM)
    return call(
        functools.partial(finish_body, scale),
        in_specs=[pl.BlockSpec(memory_space=pltpu.SMEM)] + [vmem] * 9,
        out_specs=vmem,
        out_shape=jax.ShapeDtypeStruct((group, 3, rows, hd), jnp.bfloat16),
    )(seq_lengths, events, edge, stats, *halves)


def join_body(in_ref, *outs):
    hd = in_ref.shape[-1]
    for part, out_ref in enumerate(outs):
        for head in range(H):
            out_ref[0, :, head * hd : (head + 1) * hd] = in_ref[head, part]


def join_heads(pieces):
    heads, parts, rows, hd = pieces.shape
    vmem = pl.BlockSpec(memory_space=pltpu.VMEM)
    return call(
        join_body,
        in_specs=[vmem],
        out_specs=[vmem] * parts,
        out_shape=[jax.ShapeDtypeStruct((1, rows, heads * hd), pieces.dtype)] * parts,
    )(pieces)


def on_device(
    queries,
    keys,
    values,
    grad_out,
    mem_keys,
    mem_values,
    seq_lengths,
    mem_counts,
    block_lists,
    block_slots,
):
    rows, width = queries.shape[1:]
    scale = 1.0 / math.sqrt(width // H)
    reach = WINDOW // rows
    seq, users = lax.axis_size("seq"), lax.axis_size("dp")
    groups = [[first + i for i in range(H)] for first in range(0, seq, H)]
    swap = functools.partial(
        lax.all_to_all, axis_name="seq", split_axis=0, concat_axis=0, tiled=True
    )

    arrays = (queries, keys, values, grad_out)
    *packed, edge = pack(users, block_slots, block_lists, arrays, mem_keys, mem_values)
    sources = [packed[0]]
    sources.append(lax.ppermute(packed[users], "seq", [(i, i ^ 1) for i in range(seq)]))
    places = [(u, i) for u in range(users) for i in range(seq)]
    for step in range(1, users):
        for side in range(2):
            pairs = [
                (u * seq + i, (u + step) % users * seq + (i ^ side)) for u, i in places
            ]
            sources.append(lax.ppermute(packed[side * users + step], ("dp", "seq"), pairs))
    pairs = [(i, i - reach if i % H < reach else i + reach) for i in range(seq)]
    edge = lax.ppermute(edge, "seq", [(i, j) for i, j in pairs if 0 <= j < seq])

    by_head = split_heads(seq_lengths, arrays, sources[1])
    events = swap(by_head, axis_index_groups=groups)

    held, depth = mem_keys.shape[:2]
    pieces = memory_pieces(held, depth, block_slots, block_lists, sources, by_head)
    memory = []
    for around in range(seq // H - 1, -1, -1):
        for step, piece in enumerate(pieces):
            if around == 0 and step == 0:
                memory.append(piece)
                continue
            pairs = [
                (i, ((i // H + around) * H) % seq + ((i % H) ^ (2 * step))) for i in range(seq)
            ]
            memory.append(lax.ppermute(piece, "seq", pairs))

    edge = swap(split_edge(seq_lengths, edge, events, pieces[0]), axis_index_groups=groups)
    part = functools.partial(attend, scale, depth)
    *first, stats = part(0, seq_lengths, mem_counts, events, edge, memory)
    stats = lax.ppermute(stats, "seq", [(i + H, i) for i in range(seq - H)])
    second = part(1, seq_lengths, mem_counts, events, edge, memory)
    out = finish(scale, seq_lengths, events, edge, stats, [*first, *second])
    return tuple(join_heads(swap(out, axis_index_groups=groups)))


def solution(mesh):
    spread = P("dp", "seq", None)
    return jax.shard_map(
        on_device,
        mesh=mesh,
        in_specs=(spread,) * 6 + (P(),) * 4,
        out_specs=(spread,) * 3,
        check_vma=False,
    )
```

```python
import functools
import math

import jax
import jax.numpy as jnp
from jax import lax
from jax.experimental import pallas as pl
from jax.experimental.pallas import tpu as pltpu
from jax.sharding import PartitionSpec as P

H = 8
WINDOW = 512
TILE = 256
NEG = -1e30
LOG2E = 1.4426950408889634
VMEM_LIMIT = 48 * 1024 * 1024
VMEM_WHOLE = 64 * 1024 * 1024 - 256 * 1024

NT = (((1,), (1,)), ((), ()))
TN = (((0,), (0,)), ((), ()))


def dot_nt(a, b):
    return lax.dot_general(a, b, NT, preferred_element_type=jnp.float32)


def dot_tn(a, b):
    return lax.dot_general(a, b, TN, preferred_element_type=jnp.float32)


def dot_nn(a, b):
    return jnp.dot(a, b, preferred_element_type=jnp.float32)


def call(body, limit=VMEM_LIMIT, **kw):
    return pl.pallas_call(
        body, compiler_params=pltpu.CompilerParams(vmem_limit_bytes=limit), **kw
    )


def load_listed(user, slots_ref, lists_ref, mk_ref, mv_ref, buffer, sems):
    copies = []
    for block in range(buffer.shape[0]):
        index = lax.rem(slots_ref[lists_ref[user, block]], mk_ref.shape[0])
        for part, pool in enumerate((mk_ref, mv_ref)):
            copies.append(
                pltpu.make_async_copy(
                    pool.at[index], buffer.at[block, part], sems.at[block, part]
                )
            )
    for copy in copies:
        copy.start()
    return copies


def split_parity(value, where, same_ref, other_ref):
    hd = value.shape[1] // H
    odd = lax.rem(lax.axis_index("seq"), 2) == 1
    for pair in range(H // 2):
        first = value[:, 2 * pair * hd : (2 * pair + 1) * hd]
        second = value[:, (2 * pair + 1) * hd : (2 * pair + 2) * hd]
        same_ref[(pair,) + where] = jnp.where(odd, second, first)
        other_ref[(pair,) + where] = jnp.where(odd, first, second)


def pack_body(users, length_ref, slots_ref, lists_ref, *refs):
    (q_ref, k_ref, v_ref, g_ref, mk_ref, mv_ref), refs = refs[:6], refs[6:]
    same, other = refs[: users + 1], refs[users + 1 : 2 * users + 2]
    buffer, sems, edge, edge_sems = refs[2 * users + 2 :]
    user, shard = lax.axis_index("dp"), lax.axis_index("seq")
    _, blocks, parts, depth, _ = buffer.shape
    rows, width = edge.shape[1:]
    early = lax.rem(shard, H) < WINDOW // rows
    order = [step % users for step in range(1, users + 1)]
    loads = {
        step: load_listed(
            lax.rem(user + step, users),
            slots_ref,
            lists_ref,
            mk_ref,
            mv_ref,
            buffer.at[step],
            sems.at[step],
        )
        for step in order
    }

    @pl.when(early)
    def _():
        for part, ref in enumerate((q_ref, g_ref)):
            pltpu.make_async_copy(ref.at[0], edge.at[part], edge_sems.at[part]).start()

    @pl.when(jnp.logical_not(early))
    def _():
        for part, ref in enumerate((k_ref, v_ref)):
            pltpu.make_async_copy(ref.at[0], edge.at[part], edge_sems.at[part]).start()

    for step in order:
        for copy in loads[step]:
            copy.wait()
        for block in range(blocks):
            for part in range(parts):
                where = (part, slice(block * depth, (block + 1) * depth))
                split_parity(buffer[step, block, part], where, same[step], other[step])
    live = jnp.where(early, length_ref[user] - shard * rows, rows)
    for part in range(2):
        pltpu.make_async_copy(q_ref.at[0], edge.at[part], edge_sems.at[part]).wait()
        value = edge[part]
        if part == 1:
            position = lax.broadcasted_iota(jnp.int32, (rows, width), 0)
            value = jnp.where(position < live, value.astype(jnp.float32), 0.0)
            value = value.astype(edge.dtype)
        split_parity(value, (part,), same[users], other[users])


def pack(users, seq_lengths, block_slots, block_lists, events, mem_keys, mem_values):
    _, depth, width = mem_keys.shape
    blocks = block_lists.shape[1]
    rows = events[0].shape[1]
    dtype = mem_keys.dtype
    smem = pl.BlockSpec(memory_space=pltpu.SMEM)
    hbm = pl.BlockSpec(memory_space=pltpu.HBM)
    pieces = jax.ShapeDtypeStruct((H // 2, 2, blocks * depth, width // H), dtype)
    edges = jax.ShapeDtypeStruct((H // 2, 2, rows, width // H), dtype)
    outs = ([pieces] * users + [edges]) * 2
    return call(
        functools.partial(pack_body, users),
        limit=VMEM_WHOLE,
        in_specs=[smem] * 3 + [hbm] * 6,
        out_specs=[pl.BlockSpec(memory_space=pltpu.VMEM)] * len(outs),
        out_shape=outs,
        scratch_shapes=[
            pltpu.VMEM((users, blocks, 2, depth, width), dtype),
            pltpu.SemaphoreType.DMA((users, blocks, 2)),
            pltpu.VMEM((2, rows, width), dtype),
            pltpu.SemaphoreType.DMA((2,)),
        ],
    )(seq_lengths, block_slots, block_lists, *events, mem_keys, mem_values)


def split_body(hd, length_ref, *refs):
    sources, (out_ref, buffer, sems) = refs[:4], refs[4:]
    rows = buffer.shape[1]
    copies = [
        pltpu.make_async_copy(source.at[0], buffer.at[part], sems.at[part])
        for part, source in enumerate(sources)
    ]
    for copy in copies:
        copy.start()
    live = length_ref[lax.axis_index("dp")] - lax.axis_index("seq") * rows
    position = lax.broadcasted_iota(jnp.int32, (rows, hd), 0)
    for part, copy in enumerate(copies):
        copy.wait()
        for head in range(H):
            block = buffer[part, :, head * hd : (head + 1) * hd]
            if part == 3:
                block = jnp.where(position < live, block.astype(jnp.float32), 0.0)
            out_ref[head, part] = block.astype(out_ref.dtype)


def split_heads(seq_lengths, arrays):
    _, rows, width = arrays[0].shape
    parts = len(arrays)
    hbm = pl.BlockSpec(memory_space=pltpu.HBM)
    return call(
        functools.partial(split_body, width // H),
        limit=VMEM_WHOLE,
        in_specs=[pl.BlockSpec(memory_space=pltpu.SMEM)] + [hbm] * parts,
        out_specs=pl.BlockSpec(memory_space=pltpu.VMEM),
        out_shape=jax.ShapeDtypeStruct((H, parts, rows, width // H), arrays[0].dtype),
        scratch_shapes=[
            pltpu.VMEM((parts, rows, width), arrays[0].dtype),
            pltpu.SemaphoreType.DMA((parts,)),
        ],
    )(seq_lengths, *arrays)


def memory_rows(held, slots_ref, lists_ref, block, depth, sources, side, pair, part):
    users = len(sources) // 2
    user = lax.axis_index("dp")
    slot = slots_ref[lists_ref[user, block]]
    source = lax.rem(user - slot // held + users, users)
    rows = slice(block * depth, (block + 1) * depth)
    value = sources[side][pair, part, rows]
    for other in range(1, users):
        value = jnp.where(source == other, sources[2 * other + side][pair, part, rows], value)
    return rows, value


def far_body(held, depth, slots_ref, lists_ref, *refs):
    outs = refs[-(H // 2) :]
    sources = refs[: -(H // 2)]
    pair = lax.rem(lax.axis_index("seq") // 2, H // 2)
    for block in range(lists_ref.shape[1]):
        for step, out_ref in enumerate(outs):
            for side in range(2):
                for part in range(2):
                    rows, value = memory_rows(
                        held, slots_ref, lists_ref, block, depth, sources, side, pair ^ step, part
                    )
                    out_ref[part, side, rows] = value


def far_pieces(held, depth, block_slots, block_lists, sources):
    _, parts, rows, hd = sources[0].shape
    smem = pl.BlockSpec(memory_space=pltpu.SMEM)
    vmem = pl.BlockSpec(memory_space=pltpu.VMEM)
    return call(
        functools.partial(far_body, held, depth),
        in_specs=[smem] * 2 + [vmem] * len(sources),
        out_specs=[vmem] * (H // 2),
        out_shape=[jax.ShapeDtypeStruct((parts, 2, rows, hd), sources[0].dtype)] * (H // 2),
    )(block_slots, block_lists, *sources)


def near_body(held, depth, slots_ref, lists_ref, _, *refs):
    (edge_same, edge_other), sources, out_ref = refs[:2], refs[2:-1], refs[-1]
    odd = lax.rem(lax.axis_index("seq"), 2) == 1
    memory, edges = sources[0].shape[2], edge_same.shape[2]
    for pair in range(H // 2):
        for part in range(2):
            for side in range(2):
                for block in range(lists_ref.shape[1]):
                    rows, value = memory_rows(
                        held, slots_ref, lists_ref, block, depth, sources, side, pair, part
                    )
                    first = side * memory + rows.start
                    out_ref[pair, part, first : first + depth] = value
            same, other = edge_same[pair, part], edge_other[pair, part]
            first = 2 * memory
            out_ref[pair, part, first : first + edges] = jnp.where(odd, other, same)
            out_ref[pair, part, first + edges :] = jnp.where(odd, same, other)


def near_pieces(held, depth, block_slots, block_lists, edges, sources, later_than):
    pairs, parts, rows, hd = sources[0].shape
    smem = pl.BlockSpec(memory_space=pltpu.SMEM)
    vmem = pl.BlockSpec(memory_space=pltpu.VMEM)
    size = 2 * (rows + edges[0].shape[2])
    return call(
        functools.partial(near_body, held, depth),
        in_specs=[smem] * 2
        + [pl.BlockSpec(memory_space=pl.ANY)]
        + [vmem] * (2 + len(sources)),
        out_specs=vmem,
        out_shape=jax.ShapeDtypeStruct((pairs, parts, size, hd), sources[0].dtype),
    )(block_slots, block_lists, later_than, *edges, *sources)


def attend_body(
    scale,
    depth,
    half,
    memories,
    length_ref,
    count_ref,
    ev_ref,
    near_ref,
    *refs,
):
    far_refs, (gq_ref, gk_ref, gv_ref) = refs[:memories], refs[memories : memories + 3]
    k_all, v_all, mk_all, mv_all = refs[-4:]
    step = pl.program_id(0)
    hd = ev_ref.shape[-1]
    rows = ev_ref.shape[2]
    reach = WINDOW // rows
    user = lax.axis_index("dp")
    length, count = length_ref[user], count_ref[user]
    base = (lax.axis_index("seq") // H) * (H * rows) + half * WINDOW
    slope = scale * LOG2E
    blocks_per_tile = TILE // rows
    near = near_ref.shape[2] - 2 * rows

    @pl.when(step == 0)
    def _():
        if half == 0:
            k_all[:WINDOW] = near_ref[: reach // 2, 0, near:].reshape(WINDOW, hd)
            v_all[:WINDOW] = near_ref[: reach // 2, 1, near:].reshape(WINDOW, hd)
        else:
            k_all[:WINDOW] = ev_ref[:reach, 1].reshape(WINDOW, hd)
            v_all[:WINDOW] = ev_ref[:reach, 2].reshape(WINDOW, hd)
        own = slice(half * reach, (half + 1) * reach)
        k_all[WINDOW:] = ev_ref[own, 1].reshape(WINDOW, hd)
        v_all[WINDOW:] = ev_ref[own, 2].reshape(WINDOW, hd)
        gk_ref[...] = jnp.zeros_like(gk_ref)
        gv_ref[...] = jnp.zeros_like(gv_ref)
        for part, all_ref in enumerate((mk_all, mv_all)):
            first = near_ref.shape[0] * near
            all_ref[:first] = near_ref[:, part, :near].reshape(first, hd)
            for far_ref in far_refs:
                all_ref[first : first + near] = far_ref[part].reshape(near, hd)
                first += near

    span = WINDOW + TILE
    here = pl.ds(half * reach + step * blocks_per_tile, blocks_per_tile)
    q = ev_ref[here, 0].reshape(TILE, hd)
    g = ev_ref[here, 3].reshape(TILE, hd)
    start = pl.multiple_of(step * TILE, TILE)
    kw = k_all[pl.ds(start, span)]
    vw = v_all[pl.ds(start, span)]
    mk = mk_all[...]
    mv = mv_all[...]

    qpos = base + start + lax.broadcasted_iota(jnp.int32, (TILE, span), 0)
    kpos = base + start - WINDOW + lax.broadcasted_iota(jnp.int32, (TILE, span), 1)
    allowed = (
        (kpos <= qpos)
        & (qpos - kpos < WINDOW)
        & (kpos >= 0)
        & ((kpos < length) | (kpos == qpos))
    )
    per_source = near // 2
    memory = mk.shape[0]
    which = lax.rem(lax.broadcasted_iota(jnp.int32, (1, memory), 1), per_source) // depth
    live = which < count

    sw = jnp.where(allowed, dot_nt(q, kw), NEG)
    sm = jnp.where(live, dot_nt(q, mk), NEG)
    top = jnp.maximum(
        jnp.max(sw, axis=1, keepdims=True), jnp.max(sm, axis=1, keepdims=True)
    )
    ew = jnp.exp2((sw - top) * slope)
    em = jnp.exp2((sm - top) * slope)
    dw = dot_nt(g, vw)
    dm = dot_nt(g, mv)
    total = jnp.sum(ew, axis=1, keepdims=True) + jnp.sum(em, axis=1, keepdims=True)
    inv = 1.0 / total
    delta = (
        jnp.sum(ew * dw, axis=1, keepdims=True) + jnp.sum(em * dm, axis=1, keepdims=True)
    ) * inv
    pw = ew * inv
    dsw = (pw * (dw - delta)).astype(jnp.bfloat16)
    dsm = (em * (dm - delta)).astype(jnp.bfloat16)
    gq = (dot_nn(dsw, kw) + dot_nn(dsm, mk) * inv) * scale
    gq_ref[pl.ds(step * blocks_per_tile, blocks_per_tile)] = gq.astype(gq_ref.dtype).reshape(
        blocks_per_tile, rows, hd
    )
    gk_ref[pl.ds(start, span)] += dot_tn(dsw, q) * scale
    gv_ref[pl.ds(start, span)] += dot_tn(pw.astype(jnp.bfloat16), g)
    if half == 0:
        stats_ref = refs[memories + 3]
        lane = lax.broadcasted_iota(jnp.int32, (TILE, hd), 1)
        both = jnp.where(lane == 0, top * slope + jnp.log2(total), delta)
        stats_ref[step] = both.T[:8]


def attend(scale, depth, half, seq_lengths, mem_counts, events, near, far):
    _, _, rows, hd = events.shape
    reach = WINDOW // rows
    memories = (near.shape[2] - 2 * rows) * (near.shape[0] + len(far))
    keys = WINDOW + memories
    whole = lambda shape: pl.BlockSpec(shape, lambda t: (0,) * len(shape))
    smem = pl.BlockSpec(memory_space=pltpu.SMEM)
    outs = [((reach, rows, hd), jnp.bfloat16)] + [((2 * WINDOW, hd), jnp.float32)] * 2
    if half == 0:
        outs.append(((WINDOW // TILE, 8, TILE), jnp.float32))
    return call(
        functools.partial(attend_body, scale, depth, half, len(far)),
        grid=(WINDOW // TILE,),
        in_specs=[smem, smem, whole(events.shape), whole(near.shape)]
        + [whole(piece.shape) for piece in far],
        out_specs=[whole(shape) for shape, _ in outs],
        out_shape=[jax.ShapeDtypeStruct(shape, dtype) for shape, dtype in outs],
        scratch_shapes=[pltpu.VMEM((2 * WINDOW, hd), jnp.bfloat16)] * 2
        + [pltpu.VMEM((memories, hd), jnp.bfloat16)] * 2,
        cost_estimate=pl.CostEstimate(
            flops=10 * WINDOW * keys * hd,
            bytes_accessed=4 * keys * hd,
            transcendentals=WINDOW * keys,
        ),
    )(seq_lengths, mem_counts, events, near, *far)


def finish_body(scale, length_ref, ev_ref, near_ref, stats_ref, *refs):
    (gq0, gk0, gv0, gq1, gk1, gv1), out_ref = refs[:-1], refs[-1]
    group, _, rows, hd = ev_ref.shape
    reach = WINDOW // rows
    early = group - reach
    near = near_ref.shape[2] - 2 * rows
    number = lax.axis_index("seq") // H
    length = length_ref[lax.axis_index("dp")]
    follows = number + 1 < lax.axis_size("seq") // H
    base = number * (H * rows)
    slope = scale * LOG2E
    span = group * rows

    def put(where, part, value):
        out_ref[where, part] = value.astype(out_ref.dtype).reshape(reach, rows, hd)

    first, last = slice(0, early), slice(early, group)
    out_ref[first, 0] = gq0[...]
    out_ref[last, 0] = gq1[...]
    put(first, 1, gk0[WINDOW:] + gk1[:WINDOW])
    put(first, 2, gv0[WINDOW:] + gv1[:WINDOW])
    k = ev_ref[early:, 1].reshape(WINDOW, hd)
    v = ev_ref[early:, 2].reshape(WINDOW, hd)
    gk = jnp.zeros((WINDOW, hd), jnp.float32)
    gv = jnp.zeros((WINDOW, hd), jnp.float32)
    kpos = base + span - WINDOW + lax.broadcasted_iota(jnp.int32, (WINDOW, TILE), 0)
    for tile in range(WINDOW // TILE):
        pairs = early // 2 + tile * TILE // (2 * rows)
        pairs = slice(pairs, pairs + TILE // (2 * rows))
        q = near_ref[pairs, 0, near:].reshape(TILE, hd)
        g = near_ref[pairs, 1, near:].reshape(TILE, hd)
        qpos = base + span + tile * TILE + lax.broadcasted_iota(jnp.int32, (WINDOW, TILE), 1)
        allowed = (qpos - kpos < WINDOW) & (kpos < length) & follows
        s = jnp.where(allowed, dot_nt(k, q) * slope - stats_ref[tile, 0:1], NEG)
        p = jnp.exp2(s)
        d = dot_nt(v, g)
        ds = p * (d - stats_ref[tile, 1:2])
        gk += dot_nn(ds.astype(jnp.bfloat16), q)
        gv += dot_nn(p.astype(jnp.bfloat16), g)
    put(last, 1, gk1[WINDOW:] + gk * scale)
    put(last, 2, gv1[WINDOW:] + gv)


def finish(scale, seq_lengths, events, near, stats, halves):
    group, _, rows, hd = events.shape
    vmem = pl.BlockSpec(memory_space=pltpu.VMEM)
    return call(
        functools.partial(finish_body, scale),
        in_specs=[pl.BlockSpec(memory_space=pltpu.SMEM)] + [vmem] * 9,
        out_specs=vmem,
        out_shape=jax.ShapeDtypeStruct((group, 3, rows, hd), jnp.bfloat16),
    )(seq_lengths, events, near, stats, *halves)


def join_body(in_ref, *outs):
    hd = in_ref.shape[-1]
    for part, out_ref in enumerate(outs):
        for head in range(H):
            out_ref[0, :, head * hd : (head + 1) * hd] = in_ref[head, part]


def join_heads(pieces):
    heads, parts, rows, hd = pieces.shape
    vmem = pl.BlockSpec(memory_space=pltpu.VMEM)
    return call(
        join_body,
        in_specs=[vmem],
        out_specs=[vmem] * parts,
        out_shape=[jax.ShapeDtypeStruct((1, rows, heads * hd), pieces.dtype)] * parts,
    )(pieces)


def on_device(
    queries,
    keys,
    values,
    grad_out,
    mem_keys,
    mem_values,
    seq_lengths,
    mem_counts,
    block_lists,
    block_slots,
):
    rows, width = queries.shape[1:]
    scale = 1.0 / math.sqrt(width // H)
    reach = WINDOW // rows
    seq, users = lax.axis_size("seq"), lax.axis_size("dp")
    groups = [[first + i for i in range(H)] for first in range(0, seq, H)]
    swap = functools.partial(
        lax.all_to_all, axis_name="seq", split_axis=0, concat_axis=0, tiled=True
    )

    arrays = (queries, keys, values, grad_out)
    packed = pack(users, seq_lengths, block_slots, block_lists, arrays, mem_keys, mem_values)
    packed = packed[: users + 1], packed[users + 1 :]
    sources = [packed[0][0]]
    sources.append(lax.ppermute(packed[1][0], "seq", [(i, i ^ 1) for i in range(seq)]))
    places = [(u, i) for u in range(users) for i in range(seq)]
    for step in range(1, users):
        for side in range(2):
            pairs = [
                (u * seq + i, (u + step) % users * seq + (i ^ side)) for u, i in places
            ]
            sources.append(lax.ppermute(packed[side][step], ("dp", "seq"), pairs))
    pairs = [(i, i - reach if i % H < reach else i + reach) for i in range(seq)]
    pairs = [(i, j) for i, j in pairs if 0 <= j < seq]
    edges = [
        lax.ppermute(packed[side][users], "seq", [(i, j ^ side) for i, j in pairs])
        for side in range(2)
    ]

    events = swap(split_heads(seq_lengths, arrays), axis_index_groups=groups)

    held, depth = mem_keys.shape[:2]
    pieces = far_pieces(held, depth, block_slots, block_lists, sources)
    far = []
    for around in range(1, seq // H):
        for step, piece in enumerate(pieces):
            pairs = [
                (i, ((i // H + around) * H) % seq + ((i % H) ^ (2 * step))) for i in range(seq)
            ]
            far.append(lax.ppermute(piece, "seq", pairs))
    near = near_pieces(held, depth, block_slots, block_lists, edges, sources, events)
    parities = [group[parity::2] for group in groups for parity in range(2)]
    near = swap(near, axis_index_groups=parities)

    part = functools.partial(attend, scale, depth)
    *first, stats = part(0, seq_lengths, mem_counts, events, near, far)
    stats = lax.ppermute(stats, "seq", [(i + H, i) for i in range(seq - H)])
    second = part(1, seq_lengths, mem_counts, events, near, far)
    out = finish(scale, seq_lengths, events, near, stats, [*first, *second])
    return tuple(join_heads(swap(out, axis_index_groups=groups)))


def solution(mesh):
    spread = P("dp", "seq", None)
    return jax.shard_map(
        on_device,
        mesh=mesh,
        in_specs=(spread,) * 6 + (P(),) * 4,
        out_specs=(spread,) * 3,
        check_vma=False,
    )
```

```python
import functools
import math

import jax
import jax.numpy as jnp
from jax import lax
from jax.experimental import pallas as pl
from jax.experimental.pallas import tpu as pltpu
from jax.sharding import PartitionSpec as P

H = 8
WINDOW = 512
TILE = 256
NEG = -1e30
LOG2E = 1.4426950408889634
FAR_COST = 10**11
GATHER_COST = 10**11
NEAR_COST = 0
VMEM_LIMIT = 32 * 1024 * 1024
VMEM_WHOLE = 64 * 1024 * 1024 - 256 * 1024

NT = (((1,), (1,)), ((), ()))
TN = (((0,), (0,)), ((), ()))


def dot_nt(a, b):
    return lax.dot_general(a, b, NT, preferred_element_type=jnp.float32)


def dot_tn(a, b):
    return lax.dot_general(a, b, TN, preferred_element_type=jnp.float32)


def dot_nn(a, b):
    return jnp.dot(a, b, preferred_element_type=jnp.float32)


def call(body, limit=VMEM_LIMIT, cost=None, **kw):
    if cost:
        kw["cost_estimate"] = pl.CostEstimate(flops=cost, bytes_accessed=0, transcendentals=0)
    return pl.pallas_call(
        body, compiler_params=pltpu.CompilerParams(vmem_limit_bytes=limit), **kw
    )


def load_listed(user, slots_ref, lists_ref, mk_ref, mv_ref, buffer, sems):
    copies = []
    for block in range(buffer.shape[0]):
        index = lax.rem(slots_ref[lists_ref[user, block]], mk_ref.shape[0])
        for part, pool in enumerate((mk_ref, mv_ref)):
            copies.append(
                pltpu.make_async_copy(
                    pool.at[index], buffer.at[block, part], sems.at[block, part]
                )
            )
    for copy in copies:
        copy.start()
    return copies


def split_parity(value, where, same_ref, other_ref):
    hd = value.shape[1] // H
    odd = lax.rem(lax.axis_index("seq"), 2) == 1
    for pair in range(H // 2):
        first = value[:, 2 * pair * hd : (2 * pair + 1) * hd]
        second = value[:, (2 * pair + 1) * hd : (2 * pair + 2) * hd]
        same_ref[(pair,) + where] = jnp.where(odd, second, first)
        other_ref[(pair,) + where] = jnp.where(odd, first, second)


def pack_body(users, length_ref, slots_ref, lists_ref, *refs):
    (q_ref, k_ref, v_ref, g_ref, mk_ref, mv_ref), refs = refs[:6], refs[6:]
    same, other = refs[: users + 1], refs[users + 1 : 2 * users + 2]
    buffer, sems, edge, edge_sems = refs[2 * users + 2 :]
    user, shard = lax.axis_index("dp"), lax.axis_index("seq")
    _, blocks, parts, depth, _ = buffer.shape
    rows, width = edge.shape[1:]
    early = lax.rem(shard, H) < WINDOW // rows
    order = [step % users for step in range(1, users + 1)]
    loads = {
        step: load_listed(
            lax.rem(user + step, users),
            slots_ref,
            lists_ref,
            mk_ref,
            mv_ref,
            buffer.at[step],
            sems.at[step],
        )
        for step in order
    }

    @pl.when(early)
    def _():
        for part, ref in enumerate((q_ref, g_ref)):
            pltpu.make_async_copy(ref.at[0], edge.at[part], edge_sems.at[part]).start()

    @pl.when(jnp.logical_not(early))
    def _():
        for part, ref in enumerate((k_ref, v_ref)):
            pltpu.make_async_copy(ref.at[0], edge.at[part], edge_sems.at[part]).start()

    for step in order:
        for copy in loads[step]:
            copy.wait()
        for block in range(blocks):
            for part in range(parts):
                where = (part, slice(block * depth, (block + 1) * depth))
                split_parity(buffer[step, block, part], where, same[step], other[step])
    live = jnp.where(early, length_ref[user] - shard * rows, rows)
    for part in range(2):
        pltpu.make_async_copy(q_ref.at[0], edge.at[part], edge_sems.at[part]).wait()
        value = edge[part]
        if part == 1:
            position = lax.broadcasted_iota(jnp.int32, (rows, width), 0)
            value = jnp.where(position < live, value.astype(jnp.float32), 0.0)
            value = value.astype(edge.dtype)
        split_parity(value, (part,), same[users], other[users])


def pack(users, seq_lengths, block_slots, block_lists, events, mem_keys, mem_values):
    _, depth, width = mem_keys.shape
    blocks = block_lists.shape[1]
    rows = events[0].shape[1]
    dtype = mem_keys.dtype
    smem = pl.BlockSpec(memory_space=pltpu.SMEM)
    hbm = pl.BlockSpec(memory_space=pltpu.HBM)
    pieces = jax.ShapeDtypeStruct((H // 2, 2, blocks * depth, width // H), dtype)
    edges = jax.ShapeDtypeStruct((H // 2, 2, rows, width // H), dtype)
    outs = ([pieces] * users + [edges]) * 2
    return call(
        functools.partial(pack_body, users),
        limit=VMEM_WHOLE,
        in_specs=[smem] * 3 + [hbm] * 6,
        out_specs=[pl.BlockSpec(memory_space=pltpu.VMEM)] * len(outs),
        out_shape=outs,
        scratch_shapes=[
            pltpu.VMEM((users, blocks, 2, depth, width), dtype),
            pltpu.SemaphoreType.DMA((users, blocks, 2)),
            pltpu.VMEM((2, rows, width), dtype),
            pltpu.SemaphoreType.DMA((2,)),
        ],
    )(seq_lengths, block_slots, block_lists, *events, mem_keys, mem_values)


def split_body(hd, length_ref, *refs):
    sources, (out_ref, buffer, sems) = refs[:4], refs[4:]
    rows = buffer.shape[1]
    copies = [
        pltpu.make_async_copy(source.at[0], buffer.at[part], sems.at[part])
        for part, source in enumerate(sources)
    ]
    for copy in copies:
        copy.start()
    live = length_ref[lax.axis_index("dp")] - lax.axis_index("seq") * rows
    position = lax.broadcasted_iota(jnp.int32, (rows, hd), 0)
    for part, copy in enumerate(copies):
        copy.wait()
        for head in range(H):
            block = buffer[part, :, head * hd : (head + 1) * hd]
            if part == 3:
                block = jnp.where(position < live, block.astype(jnp.float32), 0.0)
            out_ref[head, part] = block.astype(out_ref.dtype)


def split_heads(seq_lengths, arrays):
    _, rows, width = arrays[0].shape
    parts = len(arrays)
    hbm = pl.BlockSpec(memory_space=pltpu.HBM)
    return call(
        functools.partial(split_body, width // H),
        limit=VMEM_WHOLE,
        in_specs=[pl.BlockSpec(memory_space=pltpu.SMEM)] + [hbm] * parts,
        out_specs=pl.BlockSpec(memory_space=pltpu.VMEM),
        out_shape=jax.ShapeDtypeStruct((H, parts, rows, width // H), arrays[0].dtype),
        scratch_shapes=[
            pltpu.VMEM((parts, rows, width), arrays[0].dtype),
            pltpu.SemaphoreType.DMA((parts,)),
        ],
    )(seq_lengths, *arrays)


def memory_rows(held, slots_ref, lists_ref, block, depth, sources, side, pair, part):
    users = len(sources) // 2
    user = lax.axis_index("dp")
    slot = slots_ref[lists_ref[user, block]]
    source = lax.rem(user - slot // held + users, users)
    rows = slice(block * depth, (block + 1) * depth)
    value = sources[side][pair, part, rows]
    for other in range(1, users):
        value = jnp.where(source == other, sources[2 * other + side][pair, part, rows], value)
    return rows, value


def far_body(held, depth, number, slots_ref, lists_ref, *refs):
    outs = refs[-(H // 2) :]
    sources = refs[number - 2 : number] + refs[: number - 2]
    pair = lax.rem(lax.axis_index("seq") // 2, H // 2)
    for block in range(lists_ref.shape[1]):
        for step, out_ref in enumerate(outs):
            for side in range(2):
                for part in range(2):
                    rows, value = memory_rows(
                        held, slots_ref, lists_ref, block, depth, sources, side, pair ^ step, part
                    )
                    out_ref[part, side, rows] = value


def far_pieces(held, depth, block_slots, block_lists, sources, *later_than):
    _, parts, rows, hd = sources[0].shape
    smem = pl.BlockSpec(memory_space=pltpu.SMEM)
    vmem = pl.BlockSpec(memory_space=pltpu.VMEM)
    return call(
        functools.partial(far_body, held, depth, len(sources)),
        cost=FAR_COST,
        in_specs=[smem] * 2
        + [vmem] * len(sources)
        + [pl.BlockSpec(memory_space=pl.ANY)] * len(later_than),
        out_specs=[vmem] * (H // 2),
        out_shape=[jax.ShapeDtypeStruct((parts, 2, rows, hd), sources[0].dtype)] * (H // 2),
    )(block_slots, block_lists, *sources[2:], *sources[:2], *later_than)


def near_body(held, depth, slots_ref, lists_ref, _, __, *refs):
    (edge_same, edge_other), sources, out_ref = refs[:2], refs[2:-1], refs[-1]
    odd = lax.rem(lax.axis_index("seq"), 2) == 1
    memory, edges = sources[0].shape[2], edge_same.shape[2]
    for pair in range(H // 2):
        for part in range(2):
            for side in range(2):
                for block in range(lists_ref.shape[1]):
                    rows, value = memory_rows(
                        held, slots_ref, lists_ref, block, depth, sources, side, pair, part
                    )
                    first = side * memory + rows.start
                    out_ref[pair, part, first : first + depth] = value
            same, other = edge_same[pair, part], edge_other[pair, part]
            first = 2 * memory
            out_ref[pair, part, first : first + edges] = jnp.where(odd, other, same)
            out_ref[pair, part, first + edges :] = jnp.where(odd, same, other)


def near_pieces(held, depth, block_slots, block_lists, edges, sources, *later_than):
    pairs, parts, rows, hd = sources[0].shape
    smem = pl.BlockSpec(memory_space=pltpu.SMEM)
    vmem = pl.BlockSpec(memory_space=pltpu.VMEM)
    size = 2 * (rows + edges[0].shape[2])
    return call(
        functools.partial(near_body, held, depth),
        cost=NEAR_COST,
        in_specs=[smem] * 2
        + [pl.BlockSpec(memory_space=pl.ANY)] * len(later_than)
        + [vmem] * (2 + len(sources)),
        out_specs=vmem,
        out_shape=jax.ShapeDtypeStruct((pairs, parts, size, hd), sources[0].dtype),
    )(block_slots, block_lists, *later_than, *edges, *sources)


def gather_body(*refs):
    out_ref = refs[-1]
    size = refs[0].shape[1] * refs[0].shape[2]
    for i, ref in enumerate(refs[:-1]):
        for part in range(2):
            out_ref[part, i * size : (i + 1) * size] = ref[part].reshape(size, ref.shape[3])


def gather_far(far):
    _, sides, rows, hd = far[0].shape
    vmem = pl.BlockSpec(memory_space=pltpu.VMEM)
    return call(
        gather_body,
        cost=GATHER_COST,
        in_specs=[vmem] * len(far),
        out_specs=vmem,
        out_shape=jax.ShapeDtypeStruct((2, len(far) * sides * rows, hd), far[0].dtype),
    )(*far)


def attend_body(
    scale,
    depth,
    half,
    length_ref,
    count_ref,
    ev_ref,
    near_ref,
    far_ref,
    gq_ref,
    gk_ref,
    gv_ref,
    *refs,
):
    k_all, v_all, mk_all, mv_all = refs[-4:]
    step = pl.program_id(0)
    hd = ev_ref.shape[-1]
    rows = ev_ref.shape[2]
    reach = WINDOW // rows
    user = lax.axis_index("dp")
    length, count = length_ref[user], count_ref[user]
    base = (lax.axis_index("seq") // H) * (H * rows) + half * WINDOW
    slope = scale * LOG2E
    blocks_per_tile = TILE // rows
    near = near_ref.shape[2] - 2 * rows

    @pl.when(step == 0)
    def _():
        if half == 0:
            k_all[:WINDOW] = near_ref[: reach // 2, 0, near:].reshape(WINDOW, hd)
            v_all[:WINDOW] = near_ref[: reach // 2, 1, near:].reshape(WINDOW, hd)
        else:
            k_all[:WINDOW] = ev_ref[:reach, 1].reshape(WINDOW, hd)
            v_all[:WINDOW] = ev_ref[:reach, 2].reshape(WINDOW, hd)
        own = slice(half * reach, (half + 1) * reach)
        k_all[WINDOW:] = ev_ref[own, 1].reshape(WINDOW, hd)
        v_all[WINDOW:] = ev_ref[own, 2].reshape(WINDOW, hd)
        gk_ref[...] = jnp.zeros_like(gk_ref)
        gv_ref[...] = jnp.zeros_like(gv_ref)
        for part, all_ref in enumerate((mk_all, mv_all)):
            first = near_ref.shape[0] * near
            all_ref[:first] = near_ref[:, part, :near].reshape(first, hd)
            all_ref[first:] = far_ref[part]

    span = WINDOW + TILE
    here = pl.ds(half * reach + step * blocks_per_tile, blocks_per_tile)
    q = ev_ref[here, 0].reshape(TILE, hd)
    g = ev_ref[here, 3].reshape(TILE, hd)
    start = pl.multiple_of(step * TILE, TILE)
    kw = k_all[pl.ds(start, span)]
    vw = v_all[pl.ds(start, span)]
    mk = mk_all[...]
    mv = mv_all[...]

    qpos = base + start + lax.broadcasted_iota(jnp.int32, (TILE, span), 0)
    kpos = base + start - WINDOW + lax.broadcasted_iota(jnp.int32, (TILE, span), 1)
    allowed = (
        (kpos <= qpos)
        & (qpos - kpos < WINDOW)
        & (kpos >= 0)
        & ((kpos < length) | (kpos == qpos))
    )
    per_source = near // 2
    memory = mk.shape[0]
    which = lax.rem(lax.broadcasted_iota(jnp.int32, (1, memory), 1), per_source) // depth
    live = which < count

    sw = jnp.where(allowed, dot_nt(q, kw), NEG)
    sm = jnp.where(live, dot_nt(q, mk), NEG)
    top = jnp.maximum(
        jnp.max(sw, axis=1, keepdims=True), jnp.max(sm, axis=1, keepdims=True)
    )
    ew = jnp.exp2((sw - top) * slope)
    em = jnp.exp2((sm - top) * slope)
    dw = dot_nt(g, vw)
    dm = dot_nt(g, mv)
    total = jnp.sum(ew, axis=1, keepdims=True) + jnp.sum(em, axis=1, keepdims=True)
    inv = 1.0 / total
    delta = (
        jnp.sum(ew * dw, axis=1, keepdims=True) + jnp.sum(em * dm, axis=1, keepdims=True)
    ) * inv
    pw = ew * inv
    dsw = (pw * (dw - delta)).astype(jnp.bfloat16)
    dsm = (em * (dm - delta)).astype(jnp.bfloat16)
    gq = (dot_nn(dsw, kw) + dot_nn(dsm, mk) * inv) * scale
    gq_ref[pl.ds(step * blocks_per_tile, blocks_per_tile)] = gq.astype(gq_ref.dtype).reshape(
        blocks_per_tile, rows, hd
    )
    gk_ref[pl.ds(start, span)] += dot_tn(dsw, q) * scale
    gv_ref[pl.ds(start, span)] += dot_tn(pw.astype(jnp.bfloat16), g)
    if half == 0:
        stats_ref = refs[0]
        lane = lax.broadcasted_iota(jnp.int32, (TILE, hd), 1)
        both = jnp.where(lane == 0, top * slope + jnp.log2(total), delta)
        stats_ref[step] = both.T[:8]


def attend(scale, depth, half, seq_lengths, mem_counts, events, near, far):
    _, _, rows, hd = events.shape
    reach = WINDOW // rows
    memories = (near.shape[2] - 2 * rows) * near.shape[0] + far.shape[1]
    keys = WINDOW + memories
    whole = lambda shape: pl.BlockSpec(shape, lambda t: (0,) * len(shape))
    smem = pl.BlockSpec(memory_space=pltpu.SMEM)
    outs = [((reach, rows, hd), jnp.bfloat16)] + [((2 * WINDOW, hd), jnp.float32)] * 2
    if half == 0:
        outs.append(((WINDOW // TILE, 8, TILE), jnp.float32))
    return call(
        functools.partial(attend_body, scale, depth, half),
        grid=(WINDOW // TILE,),
        in_specs=[smem] * 2 + [whole(array.shape) for array in (events, near, far)],
        out_specs=[whole(shape) for shape, _ in outs],
        out_shape=[jax.ShapeDtypeStruct(shape, dtype) for shape, dtype in outs],
        scratch_shapes=[pltpu.VMEM((2 * WINDOW, hd), jnp.bfloat16)] * 2
        + [pltpu.VMEM((memories, hd), jnp.bfloat16)] * 2,
        cost_estimate=pl.CostEstimate(
            flops=10 * WINDOW * keys * hd,
            bytes_accessed=4 * keys * hd,
            transcendentals=WINDOW * keys,
        ),
    )(seq_lengths, mem_counts, events, near, far)


def finish_body(scale, length_ref, ev_ref, near_ref, stats_ref, *refs):
    (gq0, gk0, gv0, gq1, gk1, gv1), out_ref = refs[:-1], refs[-1]
    group, _, rows, hd = ev_ref.shape
    reach = WINDOW // rows
    early = group - reach
    near = near_ref.shape[2] - 2 * rows
    number = lax.axis_index("seq") // H
    length = length_ref[lax.axis_index("dp")]
    follows = number + 1 < lax.axis_size("seq") // H
    base = number * (H * rows)
    slope = scale * LOG2E
    span = group * rows

    def put(where, part, value):
        out_ref[where, part] = value.astype(out_ref.dtype).reshape(reach, rows, hd)

    first, last = slice(0, early), slice(early, group)
    out_ref[first, 0] = gq0[...]
    out_ref[last, 0] = gq1[...]
    put(first, 1, gk0[WINDOW:] + gk1[:WINDOW])
    put(first, 2, gv0[WINDOW:] + gv1[:WINDOW])
    k = ev_ref[early:, 1].reshape(WINDOW, hd)
    v = ev_ref[early:, 2].reshape(WINDOW, hd)
    gk = jnp.zeros((WINDOW, hd), jnp.float32)
    gv = jnp.zeros((WINDOW, hd), jnp.float32)
    kpos = base + span - WINDOW + lax.broadcasted_iota(jnp.int32, (WINDOW, TILE), 0)
    for tile in range(WINDOW // TILE):
        pairs = early // 2 + tile * TILE // (2 * rows)
        pairs = slice(pairs, pairs + TILE // (2 * rows))
        q = near_ref[pairs, 0, near:].reshape(TILE, hd)
        g = near_ref[pairs, 1, near:].reshape(TILE, hd)
        qpos = base + span + tile * TILE + lax.broadcasted_iota(jnp.int32, (WINDOW, TILE), 1)
        allowed = (qpos - kpos < WINDOW) & (kpos < length) & follows
        s = jnp.where(allowed, dot_nt(k, q) * slope - stats_ref[tile, 0:1], NEG)
        p = jnp.exp2(s)
        d = dot_nt(v, g)
        ds = p * (d - stats_ref[tile, 1:2])
        gk += dot_nn(ds.astype(jnp.bfloat16), q)
        gv += dot_nn(p.astype(jnp.bfloat16), g)
    put(last, 1, gk1[WINDOW:] + gk * scale)
    put(last, 2, gv1[WINDOW:] + gv)


def finish(scale, seq_lengths, events, near, stats, halves):
    group, _, rows, hd = events.shape
    vmem = pl.BlockSpec(memory_space=pltpu.VMEM)
    return call(
        functools.partial(finish_body, scale),
        in_specs=[pl.BlockSpec(memory_space=pltpu.SMEM)] + [vmem] * 9,
        out_specs=vmem,
        out_shape=jax.ShapeDtypeStruct((group, 3, rows, hd), jnp.bfloat16),
    )(seq_lengths, events, near, stats, *halves)


def join_body(in_ref, *outs):
    hd = in_ref.shape[-1]
    for part, out_ref in enumerate(outs):
        for head in range(H):
            out_ref[0, :, head * hd : (head + 1) * hd] = in_ref[head, part]


def join_heads(pieces):
    heads, parts, rows, hd = pieces.shape
    vmem = pl.BlockSpec(memory_space=pltpu.VMEM)
    return call(
        join_body,
        in_specs=[vmem],
        out_specs=[vmem] * parts,
        out_shape=[jax.ShapeDtypeStruct((1, rows, heads * hd), pieces.dtype)] * parts,
    )(pieces)


def on_device(
    queries,
    keys,
    values,
    grad_out,
    mem_keys,
    mem_values,
    seq_lengths,
    mem_counts,
    block_lists,
    block_slots,
):
    rows, width = queries.shape[1:]
    scale = 1.0 / math.sqrt(width // H)
    reach = WINDOW // rows
    seq, users = lax.axis_size("seq"), lax.axis_size("dp")
    groups = [[first + i for i in range(H)] for first in range(0, seq, H)]
    swap = functools.partial(
        lax.all_to_all, axis_name="seq", split_axis=0, concat_axis=0, tiled=True
    )

    arrays = (queries, keys, values, grad_out)
    packed = pack(users, seq_lengths, block_slots, block_lists, arrays, mem_keys, mem_values)
    packed = packed[: users + 1], packed[users + 1 :]
    sources = [packed[0][0]]
    sources.append(lax.ppermute(packed[1][0], "seq", [(i, i ^ 1) for i in range(seq)]))
    places = [(u, i) for u in range(users) for i in range(seq)]
    for step in range(1, users):
        for side in range(2):
            pairs = [
                (u * seq + i, (u + step) % users * seq + (i ^ side)) for u, i in places
            ]
            sources.append(lax.ppermute(packed[side][step], ("dp", "seq"), pairs))
    pairs = [(i, i - reach if i % H < reach else i + reach) for i in range(seq)]
    pairs = [(i, j) for i, j in pairs if 0 <= j < seq]
    edges = [
        lax.ppermute(packed[side][users], "seq", [(i, j ^ side) for i, j in pairs])
        for side in range(2)
    ]

    events = swap(split_heads(seq_lengths, arrays), axis_index_groups=groups)

    held, depth = mem_keys.shape[:2]
    pieces = far_pieces(held, depth, block_slots, block_lists, sources, *edges)
    far = []
    for around in range(1, seq // H):
        for step, piece in enumerate(pieces):
            pairs = [
                (i, ((i // H + around) * H) % seq + ((i % H) ^ (2 * step))) for i in range(seq)
            ]
            far.append(lax.ppermute(piece, "seq", pairs))
    far = gather_far(far)
    near = near_pieces(held, depth, block_slots, block_lists, edges, sources, events, pieces[0])
    parities = [group[parity::2] for group in groups for parity in range(2)]
    near = swap(near, axis_index_groups=parities)

    part = functools.partial(attend, scale, depth)
    *first, stats = part(0, seq_lengths, mem_counts, events, near, far)
    stats = lax.ppermute(stats, "seq", [(i + H, i) for i in range(seq - H)])
    second = part(1, seq_lengths, mem_counts, events, near, far)
    out = finish(scale, seq_lengths, events, near, stats, [*first, *second])
    return tuple(join_heads(swap(out, axis_index_groups=groups)))


def solution(mesh):
    spread = P("dp", "seq", None)
    return jax.shard_map(
        on_device,
        mesh=mesh,
        in_specs=(spread,) * 6 + (P(),) * 4,
        out_specs=(spread,) * 3,
        check_vma=False,
    )
```

```python
import functools
import math

import jax
import jax.numpy as jnp
from jax import lax
from jax.experimental import pallas as pl
from jax.experimental.pallas import tpu as pltpu
from jax.sharding import PartitionSpec as P

H = 8
WINDOW = 512
TILE = 256
NEG = -1e30
LOG2E = 1.4426950408889634
FAR_COST = 10**11
ARRIVED_COST = 10**11
NEAR_COST = 0
VMEM_LIMIT = 32 * 1024 * 1024
VMEM_WHOLE = 64 * 1024 * 1024 - 256 * 1024

NT = (((1,), (1,)), ((), ()))
TN = (((0,), (0,)), ((), ()))


def dot_nt(a, b):
    return lax.dot_general(a, b, NT, preferred_element_type=jnp.float32)


def dot_tn(a, b):
    return lax.dot_general(a, b, TN, preferred_element_type=jnp.float32)


def dot_nn(a, b):
    return jnp.dot(a, b, preferred_element_type=jnp.float32)


def call(body, limit=VMEM_LIMIT, cost=None, **kw):
    if cost:
        kw["cost_estimate"] = pl.CostEstimate(flops=cost, bytes_accessed=0, transcendentals=0)
    return pl.pallas_call(
        body, compiler_params=pltpu.CompilerParams(vmem_limit_bytes=limit), **kw
    )


def load_listed(user, slots_ref, lists_ref, mk_ref, mv_ref, buffer, sems):
    copies = []
    for block in range(buffer.shape[0]):
        index = lax.rem(slots_ref[lists_ref[user, block]], mk_ref.shape[0])
        for part, pool in enumerate((mk_ref, mv_ref)):
            copies.append(
                pltpu.make_async_copy(
                    pool.at[index], buffer.at[block, part], sems.at[block, part]
                )
            )
    for copy in copies:
        copy.start()
    return copies


def split_parity(value, where, same_ref, other_ref):
    hd = value.shape[1] // H
    odd = lax.rem(lax.axis_index("seq"), 2) == 1
    for pair in range(H // 2):
        first = value[:, 2 * pair * hd : (2 * pair + 1) * hd]
        second = value[:, (2 * pair + 1) * hd : (2 * pair + 2) * hd]
        same_ref[(pair,) + where] = jnp.where(odd, second, first)
        other_ref[(pair,) + where] = jnp.where(odd, first, second)


def pack_body(users, length_ref, slots_ref, lists_ref, *refs):
    (q_ref, k_ref, v_ref, g_ref, mk_ref, mv_ref), refs = refs[:6], refs[6:]
    same, other = refs[: users + 1], refs[users + 1 : 2 * users + 2]
    buffer, sems, edge, edge_sems = refs[2 * users + 2 :]
    user, shard = lax.axis_index("dp"), lax.axis_index("seq")
    _, blocks, parts, depth, _ = buffer.shape
    rows, width = edge.shape[1:]
    early = lax.rem(shard, H) < WINDOW // rows
    order = [step % users for step in range(1, users + 1)]
    loads = {
        step: load_listed(
            lax.rem(user + step, users),
            slots_ref,
            lists_ref,
            mk_ref,
            mv_ref,
            buffer.at[step],
            sems.at[step],
        )
        for step in order
    }

    @pl.when(early)
    def _():
        for part, ref in enumerate((q_ref, g_ref)):
            pltpu.make_async_copy(ref.at[0], edge.at[part], edge_sems.at[part]).start()

    @pl.when(jnp.logical_not(early))
    def _():
        for part, ref in enumerate((k_ref, v_ref)):
            pltpu.make_async_copy(ref.at[0], edge.at[part], edge_sems.at[part]).start()

    for step in order:
        for copy in loads[step]:
            copy.wait()
        for block in range(blocks):
            for part in range(parts):
                where = (part, slice(block * depth, (block + 1) * depth))
                split_parity(buffer[step, block, part], where, same[step], other[step])
    live = jnp.where(early, length_ref[user] - shard * rows, rows)
    for part in range(2):
        pltpu.make_async_copy(q_ref.at[0], edge.at[part], edge_sems.at[part]).wait()
        value = edge[part]
        if part == 1:
            position = lax.broadcasted_iota(jnp.int32, (rows, width), 0)
            value = jnp.where(position < live, value.astype(jnp.float32), 0.0)
            value = value.astype(edge.dtype)
        split_parity(value, (part,), same[users], other[users])


def pack(users, seq_lengths, block_slots, block_lists, events, mem_keys, mem_values):
    _, depth, width = mem_keys.shape
    blocks = block_lists.shape[1]
    rows = events[0].shape[1]
    dtype = mem_keys.dtype
    smem = pl.BlockSpec(memory_space=pltpu.SMEM)
    hbm = pl.BlockSpec(memory_space=pltpu.HBM)
    pieces = jax.ShapeDtypeStruct((H // 2, 2, blocks * depth, width // H), dtype)
    edges = jax.ShapeDtypeStruct((H // 2, 2, rows, width // H), dtype)
    outs = ([pieces] * users + [edges]) * 2
    return call(
        functools.partial(pack_body, users),
        limit=VMEM_WHOLE,
        in_specs=[smem] * 3 + [hbm] * 6,
        out_specs=[pl.BlockSpec(memory_space=pltpu.VMEM)] * len(outs),
        out_shape=outs,
        scratch_shapes=[
            pltpu.VMEM((users, blocks, 2, depth, width), dtype),
            pltpu.SemaphoreType.DMA((users, blocks, 2)),
            pltpu.VMEM((2, rows, width), dtype),
            pltpu.SemaphoreType.DMA((2,)),
        ],
    )(seq_lengths, block_slots, block_lists, *events, mem_keys, mem_values)


def split_body(hd, length_ref, *refs):
    sources, (out_ref, buffer, sems) = refs[:4], refs[4:]
    rows = buffer.shape[1]
    copies = [
        pltpu.make_async_copy(source.at[0], buffer.at[part], sems.at[part])
        for part, source in enumerate(sources)
    ]
    for copy in copies:
        copy.start()
    live = length_ref[lax.axis_index("dp")] - lax.axis_index("seq") * rows
    position = lax.broadcasted_iota(jnp.int32, (rows, hd), 0)
    for part, copy in enumerate(copies):
        copy.wait()
        for head in range(H):
            block = buffer[part, :, head * hd : (head + 1) * hd]
            if part == 3:
                block = jnp.where(position < live, block.astype(jnp.float32), 0.0)
            out_ref[head, part] = block.astype(out_ref.dtype)


def split_heads(seq_lengths, arrays):
    _, rows, width = arrays[0].shape
    parts = len(arrays)
    hbm = pl.BlockSpec(memory_space=pltpu.HBM)
    return call(
        functools.partial(split_body, width // H),
        limit=VMEM_WHOLE,
        in_specs=[pl.BlockSpec(memory_space=pltpu.SMEM)] + [hbm] * parts,
        out_specs=pl.BlockSpec(memory_space=pltpu.VMEM),
        out_shape=jax.ShapeDtypeStruct((H, parts, rows, width // H), arrays[0].dtype),
        scratch_shapes=[
            pltpu.VMEM((parts, rows, width), arrays[0].dtype),
            pltpu.SemaphoreType.DMA((parts,)),
        ],
    )(seq_lengths, *arrays)


def memory_rows(held, slots_ref, lists_ref, block, depth, sources, side, pair, part):
    users = len(sources) // 2
    user = lax.axis_index("dp")
    slot = slots_ref[lists_ref[user, block]]
    source = lax.rem(user - slot // held + users, users)
    rows = slice(block * depth, (block + 1) * depth)
    value = sources[side][pair, part, rows]
    for other in range(1, users):
        value = jnp.where(source == other, sources[2 * other + side][pair, part, rows], value)
    return rows, value


def far_body(held, depth, number, slots_ref, lists_ref, *refs):
    outs = refs[-(H // 2) :]
    sources = refs[number - 2 : number] + refs[: number - 2]
    pair = lax.rem(lax.axis_index("seq") // 2, H // 2)
    for block in range(lists_ref.shape[1]):
        for step, out_ref in enumerate(outs):
            for side in range(2):
                for part in range(2):
                    rows, value = memory_rows(
                        held, slots_ref, lists_ref, block, depth, sources, side, pair ^ step, part
                    )
                    out_ref[part, side, rows] = value


def far_pieces(held, depth, block_slots, block_lists, sources, *later_than):
    _, parts, rows, hd = sources[0].shape
    smem = pl.BlockSpec(memory_space=pltpu.SMEM)
    vmem = pl.BlockSpec(memory_space=pltpu.VMEM)
    return call(
        functools.partial(far_body, held, depth, len(sources)),
        cost=FAR_COST,
        in_specs=[smem] * 2
        + [vmem] * len(sources)
        + [pl.BlockSpec(memory_space=pl.ANY)] * len(later_than),
        out_specs=[vmem] * (H // 2),
        out_shape=[jax.ShapeDtypeStruct((parts, 2, rows, hd), sources[0].dtype)] * (H // 2),
    )(block_slots, block_lists, *sources[2:], *sources[:2], *later_than)


def near_body(held, depth, slots_ref, lists_ref, _, *refs):
    (edge_same, edge_other), sources, out_ref = refs[:2], refs[2:-1], refs[-1]
    odd = lax.rem(lax.axis_index("seq"), 2) == 1
    memory, edges = sources[0].shape[2], edge_same.shape[2]
    for pair in range(H // 2):
        for part in range(2):
            for side in range(2):
                for block in range(lists_ref.shape[1]):
                    rows, value = memory_rows(
                        held, slots_ref, lists_ref, block, depth, sources, side, pair, part
                    )
                    first = side * memory + rows.start
                    out_ref[pair, part, first : first + depth] = value
            same, other = edge_same[pair, part], edge_other[pair, part]
            first = 2 * memory
            out_ref[pair, part, first : first + edges] = jnp.where(odd, other, same)
            out_ref[pair, part, first + edges :] = jnp.where(odd, same, other)


def near_pieces(held, depth, block_slots, block_lists, edges, sources, *later_than):
    pairs, parts, rows, hd = sources[0].shape
    smem = pl.BlockSpec(memory_space=pltpu.SMEM)
    vmem = pl.BlockSpec(memory_space=pltpu.VMEM)
    size = 2 * (rows + edges[0].shape[2])
    return call(
        functools.partial(near_body, held, depth),
        cost=NEAR_COST,
        in_specs=[smem] * 2
        + [pl.BlockSpec(memory_space=pl.ANY)] * len(later_than)
        + [vmem] * (2 + len(sources)),
        out_specs=vmem,
        out_shape=jax.ShapeDtypeStruct((pairs, parts, size, hd), sources[0].dtype),
    )(block_slots, block_lists, *later_than, *edges, *sources)


def arrived_body(*refs):
    refs[-1][...] = jnp.zeros_like(refs[-1])


def arrived(far):
    return call(
        arrived_body,
        cost=ARRIVED_COST,
        in_specs=[pl.BlockSpec(memory_space=pl.ANY)] * len(far),
        out_specs=pl.BlockSpec(memory_space=pltpu.VMEM),
        out_shape=jax.ShapeDtypeStruct((8, 128), jnp.float32),
    )(*far)


def attend_body(scale, depth, half, memories, length_ref, count_ref, _, ev_ref, near_ref, *refs):
    far_refs, refs = refs[:memories], refs[memories:]
    gq_ref, gk_ref, gv_ref = refs[:3]
    rows, hd = ev_ref.shape[2:]
    tile = 2 * rows
    tiles = WINDOW // tile
    near = near_ref.shape[2] - 2 * rows
    user = lax.axis_index("dp")
    length, count = length_ref[user], count_ref[user]
    base = (lax.axis_index("seq") // H) * (H * rows) + half * WINDOW
    slope = scale * LOG2E

    def events(part, chunk):
        return ev_ref[2 * chunk : 2 * chunk + 2, part].reshape(tile, hd)

    def window(part, chunk):
        chunk += half * tiles
        if chunk < 0:
            return near_ref[tiles + chunk, part - 1, near:].reshape(tile, hd)
        return events(part, chunk)

    per = max(1, tile // near)
    memory = [
        [
            near_ref[first : first + per, part, :near].reshape(-1, hd)
            for first in range(0, near_ref.shape[0], per)
        ]
        + [
            jnp.concatenate(
                [ref[part].reshape(near, hd) for ref in far_refs[first : first + per]], axis=0
            )
            for first in range(0, memories, per)
        ]
        for part in range(2)
    ]
    line = lax.broadcasted_iota(jnp.int32, (tile, tile), 0)
    column = lax.broadcasted_iota(jnp.int32, (tile, tile), 1)
    which = lax.broadcasted_iota(jnp.int32, (1, per * near), 1)
    live = lax.rem(which, near // 2) // depth < count

    sums = {}
    for this in range(tiles):
        q, g = events(0, half * tiles + this), events(3, half * tiles + this)
        chunks = list(range(this - tiles, this + 1))
        keys = [window(1, chunk) for chunk in chunks] + memory[0]
        values = [window(2, chunk) for chunk in chunks] + memory[1]
        score = []
        for i, key in enumerate(keys):
            s = dot_nt(q, key)
            if i <= tiles:
                position = base + chunks[i] * tile + column[:1]
                allowed = (position >= 0) & (position < length)
                if i == 0:
                    allowed = allowed & (column > line)
                elif i == tiles:
                    allowed = (allowed & (column < line)) | (column == line)
                s = jnp.where(allowed, s, NEG)
            else:
                s = jnp.where(live, s, NEG)
            score.append(s)
        top = functools.reduce(
            jnp.maximum, [s for s in score if s.shape == score[0].shape]
        )
        top = jnp.max(top, axis=1, keepdims=True)
        for s in score:
            if s.shape != score[0].shape:
                top = jnp.maximum(top, jnp.max(s, axis=1, keepdims=True))
        expo = [jnp.exp2((s - top) * slope) for s in score]
        dprob = [dot_nt(g, value) for value in values]

        def row_sum(blocks):
            first = [block for block in blocks if block.shape == score[0].shape]
            total = jnp.sum(functools.reduce(jnp.add, first), axis=1, keepdims=True)
            for block in blocks:
                if block.shape != score[0].shape:
                    total += jnp.sum(block, axis=1, keepdims=True)
            return total

        total = row_sum(expo)
        inv = 1.0 / total
        delta = row_sum([e * d for e, d in zip(expo, dprob)]) * inv
        gq = jnp.zeros((tile, hd), jnp.float32)
        for e, d, key in zip(expo[tiles + 1 :], dprob[tiles + 1 :], memory[0]):
            gq += dot_nn((e * (d - delta)).astype(jnp.bfloat16), key)
        gq = gq * inv
        for i, chunk in enumerate(chunks):
            prob = expo[i] * inv
            dscore = (prob * (dprob[i] - delta)).astype(jnp.bfloat16)
            gq += dot_nn(dscore, keys[i])
            if chunk + half * tiles >= 0:
                owed = dot_tn(dscore, q), dot_tn(prob.astype(jnp.bfloat16), g)
                old = sums.get(chunk)
                sums[chunk] = owed if old is None else (old[0] + owed[0], old[1] + owed[1])
        gq_ref[2 * this : 2 * this + 2] = (gq * scale).astype(gq_ref.dtype).reshape(2, rows, hd)
        if half == 0:
            lane = lax.broadcasted_iota(jnp.int32, (tile, hd), 1)
            both = jnp.where(lane == 0, top * slope + jnp.log2(total), delta)
            refs[3][this] = both.T[:8]
    for i, chunk in enumerate(sorted(sums)):
        gk_ref[i * tile : (i + 1) * tile] = sums[chunk][0] * scale
        gv_ref[i * tile : (i + 1) * tile] = sums[chunk][1]


def attend(scale, depth, half, seq_lengths, mem_counts, after, events, near, far):
    _, _, rows, hd = events.shape
    keys = WINDOW + (near.shape[2] - 2 * rows) * (near.shape[0] + len(far))
    smem = pl.BlockSpec(memory_space=pltpu.SMEM)
    vmem = pl.BlockSpec(memory_space=pltpu.VMEM)
    outs = [((WINDOW // rows, rows, hd), jnp.bfloat16)]
    outs += [(((1 + half) * WINDOW, hd), jnp.float32)] * 2
    if half == 0:
        outs.append(((WINDOW // (2 * rows), 8, 2 * rows), jnp.float32))
    return call(
        functools.partial(attend_body, scale, depth, half, len(far)),
        in_specs=[smem] * 2 + [pl.BlockSpec(memory_space=pl.ANY)] + [vmem] * (2 + len(far)),
        out_specs=[vmem] * len(outs),
        out_shape=[jax.ShapeDtypeStruct(shape, dtype) for shape, dtype in outs],
        cost_estimate=pl.CostEstimate(
            flops=10 * WINDOW * keys * hd,
            bytes_accessed=4 * keys * hd,
            transcendentals=WINDOW * keys,
        ),
    )(seq_lengths, mem_counts, after, events, near, *far)


def finish_body(scale, length_ref, ev_ref, near_ref, stats_ref, *refs):
    (gq0, gk0, gv0, gq1, gk1, gv1), out_ref = refs[:-1], refs[-1]
    group, _, rows, hd = ev_ref.shape
    reach = WINDOW // rows
    early = group - reach
    near = near_ref.shape[2] - 2 * rows
    number = lax.axis_index("seq") // H
    length = length_ref[lax.axis_index("dp")]
    follows = number + 1 < lax.axis_size("seq") // H
    base = number * (H * rows)
    slope = scale * LOG2E
    span = group * rows

    def put(where, part, value):
        out_ref[where, part] = value.astype(out_ref.dtype).reshape(reach, rows, hd)

    first, last = slice(0, early), slice(early, group)
    out_ref[first, 0] = gq0[...]
    out_ref[last, 0] = gq1[...]
    put(first, 1, gk0[...] + gk1[:WINDOW])
    put(first, 2, gv0[...] + gv1[:WINDOW])
    k = ev_ref[early:, 1].reshape(WINDOW, hd)
    v = ev_ref[early:, 2].reshape(WINDOW, hd)
    gk = jnp.zeros((WINDOW, hd), jnp.float32)
    gv = jnp.zeros((WINDOW, hd), jnp.float32)
    kpos = base + span - WINDOW + lax.broadcasted_iota(jnp.int32, (WINDOW, TILE), 0)
    for tile in range(WINDOW // TILE):
        pairs = early // 2 + tile * TILE // (2 * rows)
        pairs = slice(pairs, pairs + TILE // (2 * rows))
        q = near_ref[pairs, 0, near:].reshape(TILE, hd)
        g = near_ref[pairs, 1, near:].reshape(TILE, hd)
        qpos = base + span + tile * TILE + lax.broadcasted_iota(jnp.int32, (WINDOW, TILE), 1)
        allowed = (qpos - kpos < WINDOW) & (kpos < length) & follows
        s = jnp.where(allowed, dot_nt(k, q) * slope - stats_ref[tile, 0:1], NEG)
        p = jnp.exp2(s)
        d = dot_nt(v, g)
        ds = p * (d - stats_ref[tile, 1:2])
        gk += dot_nn(ds.astype(jnp.bfloat16), q)
        gv += dot_nn(p.astype(jnp.bfloat16), g)
    put(last, 1, gk1[WINDOW:] + gk * scale)
    put(last, 2, gv1[WINDOW:] + gv)


def finish(scale, seq_lengths, events, near, stats, halves):
    group, _, rows, hd = events.shape
    vmem = pl.BlockSpec(memory_space=pltpu.VMEM)
    return call(
        functools.partial(finish_body, scale),
        in_specs=[pl.BlockSpec(memory_space=pltpu.SMEM)] + [vmem] * 9,
        out_specs=vmem,
        out_shape=jax.ShapeDtypeStruct((group, 3, rows, hd), jnp.bfloat16),
    )(seq_lengths, events, near, stats, *halves)


def join_body(in_ref, *outs):
    hd = in_ref.shape[-1]
    for part, out_ref in enumerate(outs):
        for head in range(H):
            out_ref[0, :, head * hd : (head + 1) * hd] = in_ref[head, part]


def join_heads(pieces):
    heads, parts, rows, hd = pieces.shape
    vmem = pl.BlockSpec(memory_space=pltpu.VMEM)
    return call(
        join_body,
        in_specs=[vmem],
        out_specs=[vmem] * parts,
        out_shape=[jax.ShapeDtypeStruct((1, rows, heads * hd), pieces.dtype)] * parts,
    )(pieces)


def on_device(
    queries,
    keys,
    values,
    grad_out,
    mem_keys,
    mem_values,
    seq_lengths,
    mem_counts,
    block_lists,
    block_slots,
):
    rows, width = queries.shape[1:]
    scale = 1.0 / math.sqrt(width // H)
    reach = WINDOW // rows
    seq, users = lax.axis_size("seq"), lax.axis_size("dp")
    groups = [[first + i for i in range(H)] for first in range(0, seq, H)]
    swap = functools.partial(
        lax.all_to_all, axis_name="seq", split_axis=0, concat_axis=0, tiled=True
    )

    arrays = (queries, keys, values, grad_out)
    packed = pack(users, seq_lengths, block_slots, block_lists, arrays, mem_keys, mem_values)
    packed = packed[: users + 1], packed[users + 1 :]
    sources = [packed[0][0]]
    sources.append(lax.ppermute(packed[1][0], "seq", [(i, i ^ 1) for i in range(seq)]))
    places = [(u, i) for u in range(users) for i in range(seq)]
    for step in range(1, users):
        for side in range(2):
            pairs = [
                (u * seq + i, (u + step) % users * seq + (i ^ side)) for u, i in places
            ]
            sources.append(lax.ppermute(packed[side][step], ("dp", "seq"), pairs))
    pairs = [(i, i - reach if i % H < reach else i + reach) for i in range(seq)]
    pairs = [(i, j) for i, j in pairs if 0 <= j < seq]
    edges = [
        lax.ppermute(packed[side][users], "seq", [(i, j ^ side) for i, j in pairs])
        for side in range(2)
    ]

    events = swap(split_heads(seq_lengths, arrays), axis_index_groups=groups)

    held, depth = mem_keys.shape[:2]
    pieces = far_pieces(held, depth, block_slots, block_lists, sources, *edges)
    far = []
    for around in range(1, seq // H):
        for step, piece in enumerate(pieces):
            pairs = [
                (i, ((i // H + around) * H) % seq + ((i % H) ^ (2 * step))) for i in range(seq)
            ]
            far.append(lax.ppermute(piece, "seq", pairs))
    after = arrived(far)
    near = near_pieces(held, depth, block_slots, block_lists, edges, sources, pieces[0])
    parities = [group[parity::2] for group in groups for parity in range(2)]
    near = swap(near, axis_index_groups=parities)

    part = functools.partial(attend, scale, depth)
    *first, stats = part(0, seq_lengths, mem_counts, after, events, near, far)
    stats = lax.ppermute(stats, "seq", [(i + H, i) for i in range(seq - H)])
    second = part(1, seq_lengths, mem_counts, after, events, near, far)
    out = finish(scale, seq_lengths, events, near, stats, [*first, *second])
    return tuple(join_heads(swap(out, axis_index_groups=groups)))


def solution(mesh):
    spread = P("dp", "seq", None)
    return jax.shard_map(
        on_device,
        mesh=mesh,
        in_specs=(spread,) * 6 + (P(),) * 4,
        out_specs=(spread,) * 3,
        check_vma=False,
    )
```

```python
import functools
import math

import jax
import jax.numpy as jnp
from jax import lax
from jax.experimental import pallas as pl
from jax.experimental.pallas import tpu as pltpu
from jax.sharding import PartitionSpec as P

H = 8
WINDOW = 512
TILE = 256
NEG = -1e30
LOG2E = 1.4426950408889634
FAR_COST = 10**11
ARRIVED_COST = 10**11
NEAR_COST = 0
VMEM_LIMIT = 32 * 1024 * 1024
VMEM_WHOLE = 64 * 1024 * 1024 - 256 * 1024

NT = (((1,), (1,)), ((), ()))
TN = (((0,), (0,)), ((), ()))


def dot_nt(a, b):
    return lax.dot_general(a, b, NT, preferred_element_type=jnp.float32)


def dot_tn(a, b):
    return lax.dot_general(a, b, TN, preferred_element_type=jnp.float32)


def dot_nn(a, b):
    return jnp.dot(a, b, preferred_element_type=jnp.float32)


def call(body, limit=VMEM_LIMIT, cost=None, **kw):
    if cost:
        kw["cost_estimate"] = pl.CostEstimate(flops=cost, bytes_accessed=0, transcendentals=0)
    return pl.pallas_call(
        body, compiler_params=pltpu.CompilerParams(vmem_limit_bytes=limit), **kw
    )


def load_listed(user, slots_ref, lists_ref, mk_ref, mv_ref, buffer, sems):
    copies = []
    for block in range(buffer.shape[0]):
        index = lax.rem(slots_ref[lists_ref[user, block]], mk_ref.shape[0])
        for part, pool in enumerate((mk_ref, mv_ref)):
            copies.append(
                pltpu.make_async_copy(
                    pool.at[index], buffer.at[block, part], sems.at[block, part]
                )
            )
    for copy in copies:
        copy.start()
    return copies


def split_parity(value, where, same_ref, other_ref):
    hd = value.shape[1] // H
    odd = lax.rem(lax.axis_index("seq"), 2) == 1
    for pair in range(H // 2):
        first = value[:, 2 * pair * hd : (2 * pair + 1) * hd]
        second = value[:, (2 * pair + 1) * hd : (2 * pair + 2) * hd]
        same_ref[(pair,) + where] = jnp.where(odd, second, first)
        other_ref[(pair,) + where] = jnp.where(odd, first, second)


def pack_body(users, length_ref, slots_ref, lists_ref, *refs):
    (q_ref, k_ref, v_ref, g_ref, mk_ref, mv_ref), refs = refs[:6], refs[6:]
    outs, refs = refs[: 2 * users + 2], refs[2 * users + 2 :]
    buffer, sems, edge, edge_sems, out_sems = refs[:5]
    cuts = refs[5:]
    same, other = cuts[: users + 1], cuts[users + 1 :]
    writes = [
        pltpu.make_async_copy(cut, out, out_sems.at[i])
        for i, (cut, out) in enumerate(zip(cuts, outs))
    ]
    user, shard = lax.axis_index("dp"), lax.axis_index("seq")
    _, blocks, parts, depth, _ = buffer.shape
    rows, width = edge.shape[1:]
    early = lax.rem(shard, H) < WINDOW // rows
    order = [step % users for step in range(1, users + 1)]
    loads = {
        step: load_listed(
            lax.rem(user + step, users),
            slots_ref,
            lists_ref,
            mk_ref,
            mv_ref,
            buffer.at[step],
            sems.at[step],
        )
        for step in order
    }

    @pl.when(early)
    def _():
        for part, ref in enumerate((q_ref, g_ref)):
            pltpu.make_async_copy(ref.at[0], edge.at[part], edge_sems.at[part]).start()

    @pl.when(jnp.logical_not(early))
    def _():
        for part, ref in enumerate((k_ref, v_ref)):
            pltpu.make_async_copy(ref.at[0], edge.at[part], edge_sems.at[part]).start()

    for step in order:
        for copy in loads[step]:
            copy.wait()
        for block in range(blocks):
            for part in range(parts):
                where = (part, slice(block * depth, (block + 1) * depth))
                split_parity(buffer[step, block, part], where, same[step], other[step])
        writes[step].start()
        writes[users + 1 + step].start()
    live = jnp.where(early, length_ref[user] - shard * rows, rows)
    for part in range(2):
        pltpu.make_async_copy(q_ref.at[0], edge.at[part], edge_sems.at[part]).wait()
        value = edge[part]
        if part == 1:
            position = lax.broadcasted_iota(jnp.int32, (rows, width), 0)
            value = jnp.where(position < live, value.astype(jnp.float32), 0.0)
            value = value.astype(edge.dtype)
        split_parity(value, (part,), same[users], other[users])
    writes[users].start()
    writes[2 * users + 1].start()
    for write in writes:
        write.wait()


def pack(users, seq_lengths, block_slots, block_lists, events, mem_keys, mem_values):
    _, depth, width = mem_keys.shape
    blocks = block_lists.shape[1]
    rows = events[0].shape[1]
    dtype = mem_keys.dtype
    smem = pl.BlockSpec(memory_space=pltpu.SMEM)
    hbm = pl.BlockSpec(memory_space=pltpu.HBM)
    pieces = jax.ShapeDtypeStruct((H // 2, 2, blocks * depth, width // H), dtype)
    edges = jax.ShapeDtypeStruct((H // 2, 2, rows, width // H), dtype)
    outs = ([pieces] * users + [edges]) * 2
    return call(
        functools.partial(pack_body, users),
        limit=VMEM_WHOLE,
        in_specs=[smem] * 3 + [hbm] * 6,
        out_specs=[hbm] * len(outs),
        out_shape=outs,
        scratch_shapes=[
            pltpu.VMEM((users, blocks, 2, depth, width), dtype),
            pltpu.SemaphoreType.DMA((users, blocks, 2)),
            pltpu.VMEM((2, rows, width), dtype),
            pltpu.SemaphoreType.DMA((2,)),
            pltpu.SemaphoreType.DMA((len(outs),)),
        ]
        + [pltpu.VMEM(out.shape, out.dtype) for out in outs],
    )(seq_lengths, block_slots, block_lists, *events, mem_keys, mem_values)


def split_body(hd, length_ref, *refs):
    sources, (out_ref, buffer, sems, cut, out_sems) = refs[:4], refs[4:]
    rows = buffer.shape[1]
    copies = [
        pltpu.make_async_copy(source.at[0], buffer.at[part], sems.at[part])
        for part, source in enumerate(sources)
    ]
    for copy in copies:
        copy.start()
    live = length_ref[lax.axis_index("dp")] - lax.axis_index("seq") * rows
    position = lax.broadcasted_iota(jnp.int32, (rows, hd), 0)
    for part, copy in enumerate(copies):
        copy.wait()
        for head in range(H):
            block = buffer[part, :, head * hd : (head + 1) * hd]
            if part == 3:
                block = jnp.where(position < live, block.astype(jnp.float32), 0.0)
            cut[part, head] = block.astype(cut.dtype)
        pltpu.make_async_copy(cut.at[part], out_ref.at[:, part], out_sems.at[part]).start()
    for part in range(len(copies)):
        pltpu.make_async_copy(cut.at[part], out_ref.at[:, part], out_sems.at[part]).wait()


def split_heads(seq_lengths, arrays):
    _, rows, width = arrays[0].shape
    parts = len(arrays)
    hbm = pl.BlockSpec(memory_space=pltpu.HBM)
    return call(
        functools.partial(split_body, width // H),
        limit=VMEM_WHOLE,
        in_specs=[pl.BlockSpec(memory_space=pltpu.SMEM)] + [hbm] * parts,
        out_specs=hbm,
        out_shape=jax.ShapeDtypeStruct((H, parts, rows, width // H), arrays[0].dtype),
        scratch_shapes=[
            pltpu.VMEM((parts, rows, width), arrays[0].dtype),
            pltpu.SemaphoreType.DMA((parts,)),
            pltpu.VMEM((parts, H, rows, width // H), arrays[0].dtype),
            pltpu.SemaphoreType.DMA((parts,)),
        ],
    )(seq_lengths, *arrays)


def memory_rows(held, slots_ref, lists_ref, block, depth, sources, side, pair, part):
    users = len(sources) // 2
    user = lax.axis_index("dp")
    slot = slots_ref[lists_ref[user, block]]
    source = lax.rem(user - slot // held + users, users)
    rows = slice(block * depth, (block + 1) * depth)
    value = sources[side][pair, part, rows]
    for other in range(1, users):
        value = jnp.where(source == other, sources[2 * other + side][pair, part, rows], value)
    return rows, value


def far_body(held, depth, number, slots_ref, lists_ref, *refs):
    outs = refs[-(H // 2) :]
    sources = refs[number - 2 : number] + refs[: number - 2]
    pair = lax.rem(lax.axis_index("seq") // 2, H // 2)
    for block in range(lists_ref.shape[1]):
        for step, out_ref in enumerate(outs):
            for side in range(2):
                for part in range(2):
                    rows, value = memory_rows(
                        held, slots_ref, lists_ref, block, depth, sources, side, pair ^ step, part
                    )
                    out_ref[part, side, rows] = value


def far_pieces(held, depth, block_slots, block_lists, sources, *later_than):
    _, parts, rows, hd = sources[0].shape
    smem = pl.BlockSpec(memory_space=pltpu.SMEM)
    vmem = pl.BlockSpec(memory_space=pltpu.VMEM)
    return call(
        functools.partial(far_body, held, depth, len(sources)),
        cost=FAR_COST,
        in_specs=[smem] * 2
        + [vmem] * len(sources)
        + [pl.BlockSpec(memory_space=pl.ANY)] * len(later_than),
        out_specs=[vmem] * (H // 2),
        out_shape=[jax.ShapeDtypeStruct((parts, 2, rows, hd), sources[0].dtype)] * (H // 2),
    )(block_slots, block_lists, *sources[2:], *sources[:2], *later_than)


def near_body(held, depth, slots_ref, lists_ref, _, *refs):
    (edge_same, edge_other), sources, out_ref = refs[:2], refs[2:-1], refs[-1]
    odd = lax.rem(lax.axis_index("seq"), 2) == 1
    memory, edges = sources[0].shape[2], edge_same.shape[2]
    for pair in range(H // 2):
        for part in range(2):
            for side in range(2):
                for block in range(lists_ref.shape[1]):
                    rows, value = memory_rows(
                        held, slots_ref, lists_ref, block, depth, sources, side, pair, part
                    )
                    first = side * memory + rows.start
                    out_ref[pair, part, first : first + depth] = value
            same, other = edge_same[pair, part], edge_other[pair, part]
            first = 2 * memory
            out_ref[pair, part, first : first + edges] = jnp.where(odd, other, same)
            out_ref[pair, part, first + edges :] = jnp.where(odd, same, other)


def near_pieces(held, depth, block_slots, block_lists, edges, sources, *later_than):
    pairs, parts, rows, hd = sources[0].shape
    smem = pl.BlockSpec(memory_space=pltpu.SMEM)
    vmem = pl.BlockSpec(memory_space=pltpu.VMEM)
    size = 2 * (rows + edges[0].shape[2])
    return call(
        functools.partial(near_body, held, depth),
        cost=NEAR_COST,
        in_specs=[smem] * 2
        + [pl.BlockSpec(memory_space=pl.ANY)] * len(later_than)
        + [vmem] * (2 + len(sources)),
        out_specs=vmem,
        out_shape=jax.ShapeDtypeStruct((pairs, parts, size, hd), sources[0].dtype),
    )(block_slots, block_lists, *later_than, *edges, *sources)


def arrived_body(*refs):
    refs[-1][...] = jnp.zeros_like(refs[-1])


def arrived(far):
    return call(
        arrived_body,
        cost=ARRIVED_COST,
        in_specs=[pl.BlockSpec(memory_space=pl.ANY)] * len(far),
        out_specs=pl.BlockSpec(memory_space=pltpu.VMEM),
        out_shape=jax.ShapeDtypeStruct((8, 128), jnp.float32),
    )(*far)


def attend_body(scale, depth, half, memories, length_ref, count_ref, _, ev_ref, near_ref, *refs):
    far_refs, refs = refs[:memories], refs[memories:]
    gq_ref, gk_ref, gv_ref = refs[:3]
    rows, hd = ev_ref.shape[2:]
    tile = 2 * rows
    tiles = WINDOW // tile
    near = near_ref.shape[2] - 2 * rows
    user = lax.axis_index("dp")
    length, count = length_ref[user], count_ref[user]
    base = (lax.axis_index("seq") // H) * (H * rows) + half * WINDOW
    slope = scale * LOG2E

    def events(part, chunk):
        return ev_ref[2 * chunk : 2 * chunk + 2, part].reshape(tile, hd)

    def window(part, chunk):
        chunk += half * tiles
        if chunk < 0:
            return near_ref[tiles + chunk, part - 1, near:].reshape(tile, hd)
        return events(part, chunk)

    per = max(1, tile // near)
    memory = [
        [
            near_ref[first : first + per, part, :near].reshape(-1, hd)
            for first in range(0, near_ref.shape[0], per)
        ]
        + [
            jnp.concatenate(
                [ref[part].reshape(near, hd) for ref in far_refs[first : first + per]], axis=0
            )
            for first in range(0, memories, per)
        ]
        for part in range(2)
    ]
    line = lax.broadcasted_iota(jnp.int32, (tile, tile), 0)
    column = lax.broadcasted_iota(jnp.int32, (tile, tile), 1)
    which = lax.broadcasted_iota(jnp.int32, (1, per * near), 1)
    live = lax.rem(which, near // 2) // depth < count

    sums = {}
    for this in range(tiles):
        q, g = events(0, half * tiles + this), events(3, half * tiles + this)
        chunks = list(range(this - tiles, this + 1))
        keys = [window(1, chunk) for chunk in chunks] + memory[0]
        values = [window(2, chunk) for chunk in chunks] + memory[1]
        score = []
        for i, key in enumerate(keys):
            s = dot_nt(q, key)
            if i <= tiles:
                position = base + chunks[i] * tile + column[:1]
                allowed = (position >= 0) & (position < length)
                if i == 0:
                    allowed = allowed & (column > line)
                elif i == tiles:
                    allowed = (allowed & (column < line)) | (column == line)
                s = jnp.where(allowed, s, NEG)
            else:
                s = jnp.where(live, s, NEG)
            score.append(s)
        top = functools.reduce(
            jnp.maximum, [s for s in score if s.shape == score[0].shape]
        )
        top = jnp.max(top, axis=1, keepdims=True)
        for s in score:
            if s.shape != score[0].shape:
                top = jnp.maximum(top, jnp.max(s, axis=1, keepdims=True))
        expo = [jnp.exp2((s - top) * slope) for s in score]
        dprob = [dot_nt(g, value) for value in values]

        def row_sum(blocks):
            first = [block for block in blocks if block.shape == score[0].shape]
            total = jnp.sum(functools.reduce(jnp.add, first), axis=1, keepdims=True)
            for block in blocks:
                if block.shape != score[0].shape:
                    total += jnp.sum(block, axis=1, keepdims=True)
            return total

        total = row_sum(expo)
        inv = 1.0 / total
        delta = row_sum([e * d for e, d in zip(expo, dprob)]) * inv
        gq = jnp.zeros((tile, hd), jnp.float32)
        for e, d, key in zip(expo[tiles + 1 :], dprob[tiles + 1 :], memory[0]):
            gq += dot_nn((e * (d - delta)).astype(jnp.bfloat16), key)
        gq = gq * inv
        for i, chunk in enumerate(chunks):
            prob = expo[i] * inv
            dscore = (prob * (dprob[i] - delta)).astype(jnp.bfloat16)
            gq += dot_nn(dscore, keys[i])
            if chunk + half * tiles >= 0:
                owed = dot_tn(dscore, q), dot_tn(prob.astype(jnp.bfloat16), g)
                old = sums.get(chunk)
                sums[chunk] = owed if old is None else (old[0] + owed[0], old[1] + owed[1])
        gq_ref[2 * this : 2 * this + 2] = (gq * scale).astype(gq_ref.dtype).reshape(2, rows, hd)
        if half == 0:
            lane = lax.broadcasted_iota(jnp.int32, (tile, hd), 1)
            both = jnp.where(lane == 0, top * slope + jnp.log2(total), delta)
            refs[3][this] = both.T[:8]
    for i, chunk in enumerate(sorted(sums)):
        gk_ref[i * tile : (i + 1) * tile] = sums[chunk][0] * scale
        gv_ref[i * tile : (i + 1) * tile] = sums[chunk][1]


def attend(scale, depth, half, seq_lengths, mem_counts, after, events, near, far):
    _, _, rows, hd = events.shape
    keys = WINDOW + (near.shape[2] - 2 * rows) * (near.shape[0] + len(far))
    smem = pl.BlockSpec(memory_space=pltpu.SMEM)
    vmem = pl.BlockSpec(memory_space=pltpu.VMEM)
    outs = [((WINDOW // rows, rows, hd), jnp.bfloat16)]
    outs += [(((1 + half) * WINDOW, hd), jnp.float32)] * 2
    if half == 0:
        outs.append(((WINDOW // (2 * rows), 8, 2 * rows), jnp.float32))
    return call(
        functools.partial(attend_body, scale, depth, half, len(far)),
        in_specs=[smem] * 2 + [pl.BlockSpec(memory_space=pl.ANY)] + [vmem] * (2 + len(far)),
        out_specs=[vmem] * len(outs),
        out_shape=[jax.ShapeDtypeStruct(shape, dtype) for shape, dtype in outs],
        cost_estimate=pl.CostEstimate(
            flops=10 * WINDOW * keys * hd,
            bytes_accessed=4 * keys * hd,
            transcendentals=WINDOW * keys,
        ),
    )(seq_lengths, mem_counts, after, events, near, *far)


def finish_body(scale, length_ref, ev_ref, near_ref, stats_ref, *refs):
    (gq0, gk0, gv0, gq1, gk1, gv1), out_ref = refs[:-1], refs[-1]
    group, _, rows, hd = ev_ref.shape
    reach = WINDOW // rows
    early = group - reach
    near = near_ref.shape[2] - 2 * rows
    number = lax.axis_index("seq") // H
    length = length_ref[lax.axis_index("dp")]
    follows = number + 1 < lax.axis_size("seq") // H
    base = number * (H * rows)
    slope = scale * LOG2E
    span = group * rows

    def put(where, part, value):
        out_ref[where, part] = value.astype(out_ref.dtype).reshape(reach, rows, hd)

    first, last = slice(0, early), slice(early, group)
    out_ref[first, 0] = gq0[...]
    out_ref[last, 0] = gq1[...]
    put(first, 1, gk0[...] + gk1[:WINDOW])
    put(first, 2, gv0[...] + gv1[:WINDOW])
    k = ev_ref[early:, 1].reshape(WINDOW, hd)
    v = ev_ref[early:, 2].reshape(WINDOW, hd)
    gk = jnp.zeros((WINDOW, hd), jnp.float32)
    gv = jnp.zeros((WINDOW, hd), jnp.float32)
    kpos = base + span - WINDOW + lax.broadcasted_iota(jnp.int32, (WINDOW, TILE), 0)
    for tile in range(WINDOW // TILE):
        pairs = early // 2 + tile * TILE // (2 * rows)
        pairs = slice(pairs, pairs + TILE // (2 * rows))
        q = near_ref[pairs, 0, near:].reshape(TILE, hd)
        g = near_ref[pairs, 1, near:].reshape(TILE, hd)
        qpos = base + span + tile * TILE + lax.broadcasted_iota(jnp.int32, (WINDOW, TILE), 1)
        allowed = (qpos - kpos < WINDOW) & (kpos < length) & follows
        s = jnp.where(allowed, dot_nt(k, q) * slope - stats_ref[tile, 0:1], NEG)
        p = jnp.exp2(s)
        d = dot_nt(v, g)
        ds = p * (d - stats_ref[tile, 1:2])
        gk += dot_nn(ds.astype(jnp.bfloat16), q)
        gv += dot_nn(p.astype(jnp.bfloat16), g)
    put(last, 1, gk1[WINDOW:] + gk * scale)
    put(last, 2, gv1[WINDOW:] + gv)


def finish(scale, seq_lengths, events, near, stats, halves):
    group, _, rows, hd = events.shape
    vmem = pl.BlockSpec(memory_space=pltpu.VMEM)
    return call(
        functools.partial(finish_body, scale),
        in_specs=[pl.BlockSpec(memory_space=pltpu.SMEM)] + [vmem] * 9,
        out_specs=vmem,
        out_shape=jax.ShapeDtypeStruct((group, 3, rows, hd), jnp.bfloat16),
    )(seq_lengths, events, near, stats, *halves)


def join_body(in_ref, *refs):
    parts = in_ref.shape[1]
    outs, (whole, sems) = refs[:parts], refs[parts:]
    hd = in_ref.shape[-1]
    writes = [
        pltpu.make_async_copy(whole.at[part], out_ref.at[0], sems.at[part])
        for part, out_ref in enumerate(outs)
    ]
    for part, write in enumerate(writes):
        for head in range(H):
            whole[part, :, head * hd : (head + 1) * hd] = in_ref[head, part]
        write.start()
    for write in writes:
        write.wait()


def join_heads(pieces):
    heads, parts, rows, hd = pieces.shape
    return call(
        join_body,
        in_specs=[pl.BlockSpec(memory_space=pltpu.VMEM)],
        out_specs=[pl.BlockSpec(memory_space=pltpu.HBM)] * parts,
        out_shape=[jax.ShapeDtypeStruct((1, rows, heads * hd), pieces.dtype)] * parts,
        scratch_shapes=[
            pltpu.VMEM((parts, rows, heads * hd), pieces.dtype),
            pltpu.SemaphoreType.DMA((parts,)),
        ],
    )(pieces)


def on_device(
    queries,
    keys,
    values,
    grad_out,
    mem_keys,
    mem_values,
    seq_lengths,
    mem_counts,
    block_lists,
    block_slots,
):
    rows, width = queries.shape[1:]
    scale = 1.0 / math.sqrt(width // H)
    reach = WINDOW // rows
    seq, users = lax.axis_size("seq"), lax.axis_size("dp")
    groups = [[first + i for i in range(H)] for first in range(0, seq, H)]
    swap = functools.partial(
        lax.all_to_all, axis_name="seq", split_axis=0, concat_axis=0, tiled=True
    )

    arrays = (queries, keys, values, grad_out)
    packed = pack(users, seq_lengths, block_slots, block_lists, arrays, mem_keys, mem_values)
    packed = packed[: users + 1], packed[users + 1 :]
    sources = [packed[0][0]]
    sources.append(lax.ppermute(packed[1][0], "seq", [(i, i ^ 1) for i in range(seq)]))
    places = [(u, i) for u in range(users) for i in range(seq)]
    for step in range(1, users):
        for side in range(2):
            pairs = [
                (u * seq + i, (u + step) % users * seq + (i ^ side)) for u, i in places
            ]
            sources.append(lax.ppermute(packed[side][step], ("dp", "seq"), pairs))
    pairs = [(i, i - reach if i % H < reach else i + reach) for i in range(seq)]
    pairs = [(i, j) for i, j in pairs if 0 <= j < seq]
    edges = [
        lax.ppermute(packed[side][users], "seq", [(i, j ^ side) for i, j in pairs])
        for side in range(2)
    ]

    events = swap(split_heads(seq_lengths, arrays), axis_index_groups=groups)

    held, depth = mem_keys.shape[:2]
    pieces = far_pieces(held, depth, block_slots, block_lists, sources, *edges)
    far = []
    for around in range(1, seq // H):
        for step, piece in enumerate(pieces):
            pairs = [
                (i, ((i // H + around) * H) % seq + ((i % H) ^ (2 * step))) for i in range(seq)
            ]
            far.append(lax.ppermute(piece, "seq", pairs))
    after = arrived(far)
    near = near_pieces(held, depth, block_slots, block_lists, edges, sources, pieces[0])
    parities = [group[parity::2] for group in groups for parity in range(2)]
    near = swap(near, axis_index_groups=parities)

    part = functools.partial(attend, scale, depth)
    *first, stats = part(0, seq_lengths, mem_counts, after, events, near, far)
    stats = lax.ppermute(stats, "seq", [(i + H, i) for i in range(seq - H)])
    second = part(1, seq_lengths, mem_counts, after, events, near, far)
    out = finish(scale, seq_lengths, events, near, stats, [*first, *second])
    return tuple(join_heads(swap(out, axis_index_groups=groups)))


def solution(mesh):
    spread = P("dp", "seq", None)
    return jax.shard_map(
        on_device,
        mesh=mesh,
        in_specs=(spread,) * 6 + (P(),) * 4,
        out_specs=(spread,) * 3,
        check_vma=False,
    )
```

```python
import functools
import math

import jax
import jax.numpy as jnp
from jax import lax
from jax.experimental import pallas as pl
from jax.experimental.pallas import tpu as pltpu
from jax.sharding import PartitionSpec as P

H = 8
WINDOW = 512
TILE = 256
NEG = -1e30
LOG2E = 1.4426950408889634
FAR_COST = 10**11
ARRIVED_COST = 10**11
NEAR_COST = 0
VMEM_LIMIT = 32 * 1024 * 1024
VMEM_WHOLE = 64 * 1024 * 1024 - 256 * 1024

NT = (((1,), (1,)), ((), ()))
TN = (((0,), (0,)), ((), ()))


def dot_nt(a, b):
    return lax.dot_general(a, b, NT, preferred_element_type=jnp.float32)


def dot_tn(a, b):
    return lax.dot_general(a, b, TN, preferred_element_type=jnp.float32)


def dot_nn(a, b):
    return jnp.dot(a, b, preferred_element_type=jnp.float32)


def call(body, limit=VMEM_LIMIT, cost=None, **kw):
    if cost:
        kw["cost_estimate"] = pl.CostEstimate(flops=cost, bytes_accessed=0, transcendentals=0)
    return pl.pallas_call(
        body, compiler_params=pltpu.CompilerParams(vmem_limit_bytes=limit), **kw
    )


def load_listed(user, slots_ref, lists_ref, mk_ref, mv_ref, buffer, sems):
    copies = []
    for block in range(buffer.shape[0]):
        index = lax.rem(slots_ref[lists_ref[user, block]], mk_ref.shape[0])
        for part, pool in enumerate((mk_ref, mv_ref)):
            copies.append(
                pltpu.make_async_copy(
                    pool.at[index], buffer.at[block, part], sems.at[block, part]
                )
            )
    for copy in copies:
        copy.start()
    return copies


def split_parity(value, where, same_ref, other_ref):
    hd = value.shape[1] // H
    odd = lax.rem(lax.axis_index("seq"), 2) == 1
    for pair in range(H // 2):
        first = value[:, 2 * pair * hd : (2 * pair + 1) * hd]
        second = value[:, (2 * pair + 1) * hd : (2 * pair + 2) * hd]
        same_ref[(pair,) + where] = jnp.where(odd, second, first)
        other_ref[(pair,) + where] = jnp.where(odd, first, second)


def pack_body(users, length_ref, slots_ref, lists_ref, *refs):
    (q_ref, k_ref, v_ref, g_ref, mk_ref, mv_ref), refs = refs[:6], refs[6:]
    outs, refs = refs[: 2 * users + 2], refs[2 * users + 2 :]
    buffer, sems, edge, edge_sems, out_sems = refs[:5]
    cuts = refs[5:]
    same, other = cuts[: users + 1], cuts[users + 1 :]
    writes = [
        pltpu.make_async_copy(cut, out, out_sems.at[i])
        for i, (cut, out) in enumerate(zip(cuts, outs))
    ]
    user, shard = lax.axis_index("dp"), lax.axis_index("seq")
    _, blocks, parts, depth, _ = buffer.shape
    rows, width = edge.shape[1:]
    early = lax.rem(shard, H) < WINDOW // rows
    order = [step % users for step in range(1, users + 1)]
    loads = {
        step: load_listed(
            lax.rem(user + step, users),
            slots_ref,
            lists_ref,
            mk_ref,
            mv_ref,
            buffer.at[step],
            sems.at[step],
        )
        for step in order
    }

    @pl.when(early)
    def _():
        for part, ref in enumerate((q_ref, g_ref)):
            pltpu.make_async_copy(ref.at[0], edge.at[part], edge_sems.at[part]).start()

    @pl.when(jnp.logical_not(early))
    def _():
        for part, ref in enumerate((k_ref, v_ref)):
            pltpu.make_async_copy(ref.at[0], edge.at[part], edge_sems.at[part]).start()

    for step in order:
        for copy in loads[step]:
            copy.wait()
        for block in range(blocks):
            for part in range(parts):
                where = (part, slice(block * depth, (block + 1) * depth))
                split_parity(buffer[step, block, part], where, same[step], other[step])
        writes[step].start()
        writes[users + 1 + step].start()
    live = jnp.where(early, length_ref[user] - shard * rows, rows)
    for part in range(2):
        pltpu.make_async_copy(q_ref.at[0], edge.at[part], edge_sems.at[part]).wait()
        value = edge[part]
        if part == 1:
            position = lax.broadcasted_iota(jnp.int32, (rows, width), 0)
            value = jnp.where(position < live, value.astype(jnp.float32), 0.0)
            value = value.astype(edge.dtype)
        split_parity(value, (part,), same[users], other[users])
    writes[users].start()
    writes[2 * users + 1].start()
    for write in writes:
        write.wait()


def pack(users, seq_lengths, block_slots, block_lists, events, mem_keys, mem_values):
    _, depth, width = mem_keys.shape
    blocks = block_lists.shape[1]
    rows = events[0].shape[1]
    dtype = mem_keys.dtype
    smem = pl.BlockSpec(memory_space=pltpu.SMEM)
    hbm = pl.BlockSpec(memory_space=pltpu.HBM)
    pieces = jax.ShapeDtypeStruct((H // 2, 2, blocks * depth, width // H), dtype)
    edges = jax.ShapeDtypeStruct((H // 2, 2, rows, width // H), dtype)
    outs = ([pieces] * users + [edges]) * 2
    return call(
        functools.partial(pack_body, users),
        limit=VMEM_WHOLE,
        in_specs=[smem] * 3 + [hbm] * 6,
        out_specs=[hbm] * len(outs),
        out_shape=outs,
        scratch_shapes=[
            pltpu.VMEM((users, blocks, 2, depth, width), dtype),
            pltpu.SemaphoreType.DMA((users, blocks, 2)),
            pltpu.VMEM((2, rows, width), dtype),
            pltpu.SemaphoreType.DMA((2,)),
            pltpu.SemaphoreType.DMA((len(outs),)),
        ]
        + [pltpu.VMEM(out.shape, out.dtype) for out in outs],
    )(seq_lengths, block_slots, block_lists, *events, mem_keys, mem_values)


def split_body(hd, length_ref, *refs):
    sources, (out_ref, buffer, sems, cut, out_sems) = refs[:4], refs[4:]
    rows = buffer.shape[1]
    copies = [
        pltpu.make_async_copy(source.at[0], buffer.at[part], sems.at[part])
        for part, source in enumerate(sources)
    ]
    for copy in copies:
        copy.start()
    live = length_ref[lax.axis_index("dp")] - lax.axis_index("seq") * rows
    position = lax.broadcasted_iota(jnp.int32, (rows, hd), 0)
    for part, copy in enumerate(copies):
        copy.wait()
        for head in range(H):
            block = buffer[part, :, head * hd : (head + 1) * hd]
            if part == 3:
                block = jnp.where(position < live, block.astype(jnp.float32), 0.0)
            cut[part, head] = block.astype(cut.dtype)
        pltpu.make_async_copy(cut.at[part], out_ref.at[:, part], out_sems.at[part]).start()
    for part in range(len(copies)):
        pltpu.make_async_copy(cut.at[part], out_ref.at[:, part], out_sems.at[part]).wait()


def split_heads(seq_lengths, arrays):
    _, rows, width = arrays[0].shape
    parts = len(arrays)
    hbm = pl.BlockSpec(memory_space=pltpu.HBM)
    return call(
        functools.partial(split_body, width // H),
        limit=VMEM_WHOLE,
        in_specs=[pl.BlockSpec(memory_space=pltpu.SMEM)] + [hbm] * parts,
        out_specs=hbm,
        out_shape=jax.ShapeDtypeStruct((H, parts, rows, width // H), arrays[0].dtype),
        scratch_shapes=[
            pltpu.VMEM((parts, rows, width), arrays[0].dtype),
            pltpu.SemaphoreType.DMA((parts,)),
            pltpu.VMEM((parts, H, rows, width // H), arrays[0].dtype),
            pltpu.SemaphoreType.DMA((parts,)),
        ],
    )(seq_lengths, *arrays)


def memory_rows(held, slots_ref, lists_ref, block, depth, sources, side, pair, part):
    users = len(sources) // 2
    user = lax.axis_index("dp")
    slot = slots_ref[lists_ref[user, block]]
    source = lax.rem(user - slot // held + users, users)
    rows = slice(block * depth, (block + 1) * depth)
    value = sources[side][pair, part, rows]
    for other in range(1, users):
        value = jnp.where(source == other, sources[2 * other + side][pair, part, rows], value)
    return rows, value


def far_body(held, depth, number, slots_ref, lists_ref, *refs):
    outs = refs[-(H // 2) :]
    sources = refs[number - 2 : number] + refs[: number - 2]
    pair = lax.rem(lax.axis_index("seq") // 2, H // 2)
    for block in range(lists_ref.shape[1]):
        for step, out_ref in enumerate(outs):
            for side in range(2):
                for part in range(2):
                    rows, value = memory_rows(
                        held, slots_ref, lists_ref, block, depth, sources, side, pair ^ step, part
                    )
                    out_ref[part, side, rows] = value


def far_pieces(held, depth, block_slots, block_lists, sources, *later_than):
    _, parts, rows, hd = sources[0].shape
    smem = pl.BlockSpec(memory_space=pltpu.SMEM)
    vmem = pl.BlockSpec(memory_space=pltpu.VMEM)
    return call(
        functools.partial(far_body, held, depth, len(sources)),
        cost=FAR_COST,
        in_specs=[smem] * 2
        + [vmem] * len(sources)
        + [pl.BlockSpec(memory_space=pl.ANY)] * len(later_than),
        out_specs=[vmem] * (H // 2),
        out_shape=[jax.ShapeDtypeStruct((parts, 2, rows, hd), sources[0].dtype)] * (H // 2),
    )(block_slots, block_lists, *sources[2:], *sources[:2], *later_than)


def near_body(held, depth, slots_ref, lists_ref, _, *refs):
    (edge_same, edge_other), sources, out_ref = refs[:2], refs[2:-1], refs[-1]
    odd = lax.rem(lax.axis_index("seq"), 2) == 1
    memory, edges = sources[0].shape[2], edge_same.shape[2]
    for pair in range(H // 2):
        for part in range(2):
            for side in range(2):
                for block in range(lists_ref.shape[1]):
                    rows, value = memory_rows(
                        held, slots_ref, lists_ref, block, depth, sources, side, pair, part
                    )
                    first = side * memory + rows.start
                    out_ref[pair, part, first : first + depth] = value
            same, other = edge_same[pair, part], edge_other[pair, part]
            first = 2 * memory
            out_ref[pair, part, first : first + edges] = jnp.where(odd, other, same)
            out_ref[pair, part, first + edges :] = jnp.where(odd, same, other)


def near_pieces(held, depth, block_slots, block_lists, edges, sources, *later_than):
    pairs, parts, rows, hd = sources[0].shape
    smem = pl.BlockSpec(memory_space=pltpu.SMEM)
    vmem = pl.BlockSpec(memory_space=pltpu.VMEM)
    size = 2 * (rows + edges[0].shape[2])
    return call(
        functools.partial(near_body, held, depth),
        cost=NEAR_COST,
        in_specs=[smem] * 2
        + [pl.BlockSpec(memory_space=pl.ANY)] * len(later_than)
        + [vmem] * (2 + len(sources)),
        out_specs=vmem,
        out_shape=jax.ShapeDtypeStruct((pairs, parts, size, hd), sources[0].dtype),
    )(block_slots, block_lists, *later_than, *edges, *sources)


def arrived_body(*refs):
    refs[-1][...] = jnp.zeros_like(refs[-1])


def arrived(far):
    return call(
        arrived_body,
        cost=ARRIVED_COST,
        in_specs=[pl.BlockSpec(memory_space=pl.ANY)] * len(far),
        out_specs=pl.BlockSpec(memory_space=pltpu.VMEM),
        out_shape=jax.ShapeDtypeStruct((8, 128), jnp.float32),
    )(*far)


def attend_body(scale, depth, half, memories, length_ref, count_ref, _, ev_ref, near_ref, *refs):
    far_refs, refs = refs[:memories], refs[memories:]
    gq_ref, gk_ref, gv_ref = refs[:3]
    k_all, v_all = refs[-2:]
    rows, hd = ev_ref.shape[2:]
    tile = 2 * rows
    tiles = WINDOW // tile
    near = near_ref.shape[2] - 2 * rows
    user = lax.axis_index("dp")
    length, count = length_ref[user], count_ref[user]
    base = (lax.axis_index("seq") // H) * (H * rows) + half * WINDOW
    slope = scale * LOG2E

    def events(part, chunk):
        return ev_ref[pl.ds(2 * chunk, 2), part].reshape(tile, hd)

    for chunk in range(2 * tiles):
        where = slice(chunk * tile, (chunk + 1) * tile)
        number = chunk + (half - 1) * tiles
        for part, all_ref in ((1, k_all), (2, v_all)):
            if number < 0:
                all_ref[where] = near_ref[chunk, part - 1, near:].reshape(tile, hd)
            else:
                all_ref[where] = events(part, number)
    gk_ref[...] = jnp.zeros_like(gk_ref)
    gv_ref[...] = jnp.zeros_like(gv_ref)

    per = max(1, tile // near)
    memory = [
        [
            near_ref[first : first + per, part, :near].reshape(-1, hd)
            for first in range(0, near_ref.shape[0], per)
        ]
        + [
            jnp.concatenate(
                [ref[part].reshape(near, hd) for ref in far_refs[first : first + per]], axis=0
            )
            for first in range(0, memories, per)
        ]
        for part in range(2)
    ]
    line = lax.broadcasted_iota(jnp.int32, (tile, tile), 0)
    column = lax.broadcasted_iota(jnp.int32, (tile, tile), 1)
    which = lax.broadcasted_iota(jnp.int32, (1, per * near), 1)
    live = lax.rem(which, near // 2) // depth < count

    def step(this, carry):
        q, g = events(0, half * tiles + this), events(3, half * tiles + this)
        chunks = [this - tiles + i for i in range(tiles + 1)]
        spans = [pl.ds(pl.multiple_of((this + i) * tile, tile), tile) for i in range(tiles + 1)]
        keys = [k_all[span] for span in spans] + memory[0]
        values = [v_all[span] for span in spans] + memory[1]
        score = []
        for i, key in enumerate(keys):
            s = dot_nt(q, key)
            if i <= tiles:
                position = base + chunks[i] * tile + column[:1]
                allowed = (position >= 0) & (position < length)
                if i == 0:
                    allowed = allowed & (column > line)
                elif i == tiles:
                    allowed = (allowed & (column < line)) | (column == line)
                s = jnp.where(allowed, s, NEG)
            else:
                s = jnp.where(live, s, NEG)
            score.append(s)
        top = functools.reduce(
            jnp.maximum, [s for s in score if s.shape == score[0].shape]
        )
        top = jnp.max(top, axis=1, keepdims=True)
        for s in score:
            if s.shape != score[0].shape:
                top = jnp.maximum(top, jnp.max(s, axis=1, keepdims=True))
        expo = [jnp.exp2((s - top) * slope) for s in score]
        dprob = [dot_nt(g, value) for value in values]

        def row_sum(blocks):
            first = [block for block in blocks if block.shape == score[0].shape]
            total = jnp.sum(functools.reduce(jnp.add, first), axis=1, keepdims=True)
            for block in blocks:
                if block.shape != score[0].shape:
                    total += jnp.sum(block, axis=1, keepdims=True)
            return total

        total = row_sum(expo)
        inv = 1.0 / total
        delta = row_sum([e * d for e, d in zip(expo, dprob)]) * inv
        gq = jnp.zeros((tile, hd), jnp.float32)
        for e, d, key in zip(expo[tiles + 1 :], dprob[tiles + 1 :], memory[0]):
            gq += dot_nn((e * (d - delta)).astype(jnp.bfloat16), key)
        gq = gq * inv
        for i, chunk in enumerate(chunks):
            prob = expo[i] * inv
            dscore = (prob * (dprob[i] - delta)).astype(jnp.bfloat16)
            gq += dot_nn(dscore, keys[i])
            owed = dot_tn(dscore, q) * scale, dot_tn(prob.astype(jnp.bfloat16), g)
            first = pl.multiple_of(jnp.maximum(chunk + half * tiles, 0) * tile, tile)

            @pl.when(chunk + half * tiles >= 0)
            def _():
                gk_ref[pl.ds(first, tile)] += owed[0]
                gv_ref[pl.ds(first, tile)] += owed[1]

        gq_ref[pl.ds(2 * this, 2)] = (gq * scale).astype(gq_ref.dtype).reshape(2, rows, hd)
        if half == 0:
            lane = lax.broadcasted_iota(jnp.int32, (tile, hd), 1)
            both = jnp.where(lane == 0, top * slope + jnp.log2(total), delta)
            refs[3][this] = both.T[:8]
        return carry

    lax.fori_loop(0, tiles, step, 0)


def attend(scale, depth, half, seq_lengths, mem_counts, after, events, near, far):
    _, _, rows, hd = events.shape
    keys = WINDOW + (near.shape[2] - 2 * rows) * (near.shape[0] + len(far))
    smem = pl.BlockSpec(memory_space=pltpu.SMEM)
    vmem = pl.BlockSpec(memory_space=pltpu.VMEM)
    outs = [((WINDOW // rows, rows, hd), jnp.bfloat16)]
    outs += [(((1 + half) * WINDOW, hd), jnp.float32)] * 2
    if half == 0:
        outs.append(((WINDOW // (2 * rows), 8, 2 * rows), jnp.float32))
    return call(
        functools.partial(attend_body, scale, depth, half, len(far)),
        in_specs=[smem] * 2 + [pl.BlockSpec(memory_space=pl.ANY)] + [vmem] * (2 + len(far)),
        out_specs=[vmem] * len(outs),
        out_shape=[jax.ShapeDtypeStruct(shape, dtype) for shape, dtype in outs],
        scratch_shapes=[pltpu.VMEM((2 * WINDOW, hd), events.dtype)] * 2,
        cost_estimate=pl.CostEstimate(
            flops=10 * WINDOW * keys * hd,
            bytes_accessed=4 * keys * hd,
            transcendentals=WINDOW * keys,
        ),
    )(seq_lengths, mem_counts, after, events, near, *far)


def finish_body(scale, length_ref, ev_ref, near_ref, stats_ref, *refs):
    (gq0, gk0, gv0, gq1, gk1, gv1), out_ref = refs[:-1], refs[-1]
    group, _, rows, hd = ev_ref.shape
    reach = WINDOW // rows
    early = group - reach
    near = near_ref.shape[2] - 2 * rows
    number = lax.axis_index("seq") // H
    length = length_ref[lax.axis_index("dp")]
    follows = number + 1 < lax.axis_size("seq") // H
    base = number * (H * rows)
    slope = scale * LOG2E
    span = group * rows

    def put(where, part, value):
        out_ref[where, part] = value.astype(out_ref.dtype).reshape(reach, rows, hd)

    first, last = slice(0, early), slice(early, group)
    out_ref[first, 0] = gq0[...]
    out_ref[last, 0] = gq1[...]
    put(first, 1, gk0[...] + gk1[:WINDOW])
    put(first, 2, gv0[...] + gv1[:WINDOW])
    k = ev_ref[early:, 1].reshape(WINDOW, hd)
    v = ev_ref[early:, 2].reshape(WINDOW, hd)
    gk = jnp.zeros((WINDOW, hd), jnp.float32)
    gv = jnp.zeros((WINDOW, hd), jnp.float32)
    kpos = base + span - WINDOW + lax.broadcasted_iota(jnp.int32, (WINDOW, TILE), 0)
    for tile in range(WINDOW // TILE):
        pairs = early // 2 + tile * TILE // (2 * rows)
        pairs = slice(pairs, pairs + TILE // (2 * rows))
        q = near_ref[pairs, 0, near:].reshape(TILE, hd)
        g = near_ref[pairs, 1, near:].reshape(TILE, hd)
        qpos = base + span + tile * TILE + lax.broadcasted_iota(jnp.int32, (WINDOW, TILE), 1)
        allowed = (qpos - kpos < WINDOW) & (kpos < length) & follows
        s = jnp.where(allowed, dot_nt(k, q) * slope - stats_ref[tile, 0:1], NEG)
        p = jnp.exp2(s)
        d = dot_nt(v, g)
        ds = p * (d - stats_ref[tile, 1:2])
        gk += dot_nn(ds.astype(jnp.bfloat16), q)
        gv += dot_nn(p.astype(jnp.bfloat16), g)
    put(last, 1, gk1[WINDOW:] + gk * scale)
    put(last, 2, gv1[WINDOW:] + gv)


def finish(scale, seq_lengths, events, near, stats, halves):
    group, _, rows, hd = events.shape
    vmem = pl.BlockSpec(memory_space=pltpu.VMEM)
    return call(
        functools.partial(finish_body, scale),
        in_specs=[pl.BlockSpec(memory_space=pltpu.SMEM)] + [vmem] * 9,
        out_specs=vmem,
        out_shape=jax.ShapeDtypeStruct((group, 3, rows, hd), jnp.bfloat16),
    )(seq_lengths, events, near, stats, *halves)


def join_body(in_ref, *refs):
    parts = in_ref.shape[1]
    outs, (whole, sems) = refs[:parts], refs[parts:]
    hd = in_ref.shape[-1]
    writes = [
        pltpu.make_async_copy(whole.at[part], out_ref.at[0], sems.at[part])
        for part, out_ref in enumerate(outs)
    ]
    for part, write in enumerate(writes):
        for head in range(H):
            whole[part, :, head * hd : (head + 1) * hd] = in_ref[head, part]
        write.start()
    for write in writes:
        write.wait()


def join_heads(pieces):
    heads, parts, rows, hd = pieces.shape
    return call(
        join_body,
        in_specs=[pl.BlockSpec(memory_space=pltpu.VMEM)],
        out_specs=[pl.BlockSpec(memory_space=pltpu.HBM)] * parts,
        out_shape=[jax.ShapeDtypeStruct((1, rows, heads * hd), pieces.dtype)] * parts,
        scratch_shapes=[
            pltpu.VMEM((parts, rows, heads * hd), pieces.dtype),
            pltpu.SemaphoreType.DMA((parts,)),
        ],
    )(pieces)


def on_device(
    queries,
    keys,
    values,
    grad_out,
    mem_keys,
    mem_values,
    seq_lengths,
    mem_counts,
    block_lists,
    block_slots,
):
    rows, width = queries.shape[1:]
    scale = 1.0 / math.sqrt(width // H)
    reach = WINDOW // rows
    seq, users = lax.axis_size("seq"), lax.axis_size("dp")
    groups = [[first + i for i in range(H)] for first in range(0, seq, H)]
    swap = functools.partial(
        lax.all_to_all, axis_name="seq", split_axis=0, concat_axis=0, tiled=True
    )

    arrays = (queries, keys, values, grad_out)
    packed = pack(users, seq_lengths, block_slots, block_lists, arrays, mem_keys, mem_values)
    packed = packed[: users + 1], packed[users + 1 :]
    sources = [packed[0][0]]
    sources.append(lax.ppermute(packed[1][0], "seq", [(i, i ^ 1) for i in range(seq)]))
    places = [(u, i) for u in range(users) for i in range(seq)]
    for step in range(1, users):
        for side in range(2):
            pairs = [
                (u * seq + i, (u + step) % users * seq + (i ^ side)) for u, i in places
            ]
            sources.append(lax.ppermute(packed[side][step], ("dp", "seq"), pairs))
    pairs = [(i, i - reach if i % H < reach else i + reach) for i in range(seq)]
    pairs = [(i, j) for i, j in pairs if 0 <= j < seq]
    edges = [
        lax.ppermute(packed[side][users], "seq", [(i, j ^ side) for i, j in pairs])
        for side in range(2)
    ]

    events = swap(split_heads(seq_lengths, arrays), axis_index_groups=groups)

    held, depth = mem_keys.shape[:2]
    pieces = far_pieces(held, depth, block_slots, block_lists, sources, *edges)
    far = []
    for around in range(1, seq // H):
        for step, piece in enumerate(pieces):
            pairs = [
                (i, ((i // H + around) * H) % seq + ((i % H) ^ (2 * step))) for i in range(seq)
            ]
            far.append(lax.ppermute(piece, "seq", pairs))
    after = arrived(far)
    near = near_pieces(held, depth, block_slots, block_lists, edges, sources, pieces[0])
    parities = [group[parity::2] for group in groups for parity in range(2)]
    near = swap(near, axis_index_groups=parities)

    part = functools.partial(attend, scale, depth)
    *first, stats = part(0, seq_lengths, mem_counts, after, events, near, far)
    stats = lax.ppermute(stats, "seq", [(i + H, i) for i in range(seq - H)])
    second = part(1, seq_lengths, mem_counts, after, events, near, far)
    out = finish(scale, seq_lengths, events, near, stats, [*first, *second])
    return tuple(join_heads(swap(out, axis_index_groups=groups)))


def solution(mesh):
    spread = P("dp", "seq", None)
    return jax.shard_map(
        on_device,
        mesh=mesh,
        in_specs=(spread,) * 6 + (P(),) * 4,
        out_specs=(spread,) * 3,
        check_vma=False,
    )
```

```python
import functools
import math

import jax
import jax.numpy as jnp
from jax import lax
from jax.experimental import pallas as pl
from jax.experimental.pallas import tpu as pltpu
from jax.sharding import PartitionSpec as P

H = 8
WINDOW = 512
TILE = 256
NEG = -1e30
LOG2E = 1.4426950408889634
FAR_COST = 0
ARRIVED_COST = 10**11
NEAR_COST = 0
VMEM_LIMIT = 32 * 1024 * 1024
VMEM_WHOLE = 64 * 1024 * 1024 - 256 * 1024

NT = (((1,), (1,)), ((), ()))
TN = (((0,), (0,)), ((), ()))


def dot_nt(a, b):
    return lax.dot_general(a, b, NT, preferred_element_type=jnp.float32)


def dot_tn(a, b):
    return lax.dot_general(a, b, TN, preferred_element_type=jnp.float32)


def dot_nn(a, b):
    return jnp.dot(a, b, preferred_element_type=jnp.float32)


def call(body, limit=VMEM_LIMIT, cost=None, **kw):
    if cost:
        kw["cost_estimate"] = pl.CostEstimate(flops=cost, bytes_accessed=0, transcendentals=0)
    return pl.pallas_call(
        body, compiler_params=pltpu.CompilerParams(vmem_limit_bytes=limit), **kw
    )


def load_listed(user, slots_ref, lists_ref, mk_ref, mv_ref, buffer, sems):
    copies = []
    for block in range(buffer.shape[0]):
        index = lax.rem(slots_ref[lists_ref[user, block]], mk_ref.shape[0])
        for part, pool in enumerate((mk_ref, mv_ref)):
            copies.append(
                pltpu.make_async_copy(
                    pool.at[index], buffer.at[block, part], sems.at[block, part]
                )
            )
    for copy in copies:
        copy.start()
    return copies


def split_parity(value, where, same_ref, other_ref):
    hd = value.shape[1] // H
    odd = lax.rem(lax.axis_index("seq"), 2) == 1
    for pair in range(H // 2):
        first = value[:, 2 * pair * hd : (2 * pair + 1) * hd]
        second = value[:, (2 * pair + 1) * hd : (2 * pair + 2) * hd]
        same_ref[(pair,) + where] = jnp.where(odd, second, first)
        other_ref[(pair,) + where] = jnp.where(odd, first, second)


def pack_body(users, length_ref, slots_ref, lists_ref, *refs):
    (q_ref, k_ref, v_ref, g_ref, mk_ref, mv_ref), refs = refs[:6], refs[6:]
    outs, refs = refs[: 2 * users + 2], refs[2 * users + 2 :]
    buffer, sems, edge, edge_sems, out_sems = refs[:5]
    cuts = refs[5:]
    same, other = cuts[: users + 1], cuts[users + 1 :]
    writes = [
        pltpu.make_async_copy(cut, out, out_sems.at[i])
        for i, (cut, out) in enumerate(zip(cuts, outs))
    ]
    user, shard = lax.axis_index("dp"), lax.axis_index("seq")
    _, blocks, parts, depth, _ = buffer.shape
    rows, width = edge.shape[1:]
    early = lax.rem(shard, H) < WINDOW // rows
    order = [step % users for step in range(1, users + 1)]
    loads = {
        step: load_listed(
            lax.rem(user + step, users),
            slots_ref,
            lists_ref,
            mk_ref,
            mv_ref,
            buffer.at[step],
            sems.at[step],
        )
        for step in order
    }

    @pl.when(early)
    def _():
        for part, ref in enumerate((q_ref, g_ref)):
            pltpu.make_async_copy(ref.at[0], edge.at[part], edge_sems.at[part]).start()

    @pl.when(jnp.logical_not(early))
    def _():
        for part, ref in enumerate((k_ref, v_ref)):
            pltpu.make_async_copy(ref.at[0], edge.at[part], edge_sems.at[part]).start()

    for step in order:
        for copy in loads[step]:
            copy.wait()
        for block in range(blocks):
            for part in range(parts):
                where = (part, slice(block * depth, (block + 1) * depth))
                split_parity(buffer[step, block, part], where, same[step], other[step])
        writes[step].start()
        writes[users + 1 + step].start()
    live = jnp.where(early, length_ref[user] - shard * rows, rows)
    for part in range(2):
        pltpu.make_async_copy(q_ref.at[0], edge.at[part], edge_sems.at[part]).wait()
        value = edge[part]
        if part == 1:
            position = lax.broadcasted_iota(jnp.int32, (rows, width), 0)
            value = jnp.where(position < live, value.astype(jnp.float32), 0.0)
            value = value.astype(edge.dtype)
        split_parity(value, (part,), same[users], other[users])
    writes[users].start()
    writes[2 * users + 1].start()
    for write in writes:
        write.wait()


def pack(users, seq_lengths, block_slots, block_lists, events, mem_keys, mem_values):
    _, depth, width = mem_keys.shape
    blocks = block_lists.shape[1]
    rows = events[0].shape[1]
    dtype = mem_keys.dtype
    smem = pl.BlockSpec(memory_space=pltpu.SMEM)
    hbm = pl.BlockSpec(memory_space=pltpu.HBM)
    pieces = jax.ShapeDtypeStruct((H // 2, 2, blocks * depth, width // H), dtype)
    edges = jax.ShapeDtypeStruct((H // 2, 2, rows, width // H), dtype)
    outs = ([pieces] * users + [edges]) * 2
    return call(
        functools.partial(pack_body, users),
        limit=VMEM_WHOLE,
        in_specs=[smem] * 3 + [hbm] * 6,
        out_specs=[hbm] * len(outs),
        out_shape=outs,
        scratch_shapes=[
            pltpu.VMEM((users, blocks, 2, depth, width), dtype),
            pltpu.SemaphoreType.DMA((users, blocks, 2)),
            pltpu.VMEM((2, rows, width), dtype),
            pltpu.SemaphoreType.DMA((2,)),
            pltpu.SemaphoreType.DMA((len(outs),)),
        ]
        + [pltpu.VMEM(out.shape, out.dtype) for out in outs],
    )(seq_lengths, block_slots, block_lists, *events, mem_keys, mem_values)


def split_body(hd, length_ref, *refs):
    sources, (out_ref, buffer, sems, cut, out_sems) = refs[:4], refs[4:]
    rows = buffer.shape[1]
    copies = [
        pltpu.make_async_copy(source.at[0], buffer.at[part], sems.at[part])
        for part, source in enumerate(sources)
    ]
    for copy in copies:
        copy.start()
    live = length_ref[lax.axis_index("dp")] - lax.axis_index("seq") * rows
    position = lax.broadcasted_iota(jnp.int32, (rows, hd), 0)
    for part, copy in enumerate(copies):
        copy.wait()
        for head in range(H):
            block = buffer[part, :, head * hd : (head + 1) * hd]
            if part == 3:
                block = jnp.where(position < live, block.astype(jnp.float32), 0.0)
            cut[part, head] = block.astype(cut.dtype)
        pltpu.make_async_copy(cut.at[part], out_ref.at[:, part], out_sems.at[part]).start()
    for part in range(len(copies)):
        pltpu.make_async_copy(cut.at[part], out_ref.at[:, part], out_sems.at[part]).wait()


def split_heads(seq_lengths, arrays):
    _, rows, width = arrays[0].shape
    parts = len(arrays)
    hbm = pl.BlockSpec(memory_space=pltpu.HBM)
    return call(
        functools.partial(split_body, width // H),
        limit=VMEM_WHOLE,
        in_specs=[pl.BlockSpec(memory_space=pltpu.SMEM)] + [hbm] * parts,
        out_specs=hbm,
        out_shape=jax.ShapeDtypeStruct((H, parts, rows, width // H), arrays[0].dtype),
        scratch_shapes=[
            pltpu.VMEM((parts, rows, width), arrays[0].dtype),
            pltpu.SemaphoreType.DMA((parts,)),
            pltpu.VMEM((parts, H, rows, width // H), arrays[0].dtype),
            pltpu.SemaphoreType.DMA((parts,)),
        ],
    )(seq_lengths, *arrays)


def memory_rows(held, slots_ref, lists_ref, block, depth, sources, side, pair, part):
    users = len(sources) // 2
    user = lax.axis_index("dp")
    slot = slots_ref[lists_ref[user, block]]
    source = lax.rem(user - slot // held + users, users)
    rows = slice(block * depth, (block + 1) * depth)
    value = sources[side][pair, part, rows]
    for other in range(1, users):
        value = jnp.where(source == other, sources[2 * other + side][pair, part, rows], value)
    return rows, value


def far_body(held, depth, number, slots_ref, lists_ref, *refs):
    outs = refs[-(H // 2) :]
    sources = refs[number - 2 : number] + refs[: number - 2]
    pair = lax.rem(lax.axis_index("seq") // 2, H // 2)
    for block in range(lists_ref.shape[1]):
        for step, out_ref in enumerate(outs):
            for side in range(2):
                for part in range(2):
                    rows, value = memory_rows(
                        held, slots_ref, lists_ref, block, depth, sources, side, pair ^ step, part
                    )
                    out_ref[part, side, rows] = value


def far_pieces(held, depth, block_slots, block_lists, sources, *later_than):
    _, parts, rows, hd = sources[0].shape
    smem = pl.BlockSpec(memory_space=pltpu.SMEM)
    vmem = pl.BlockSpec(memory_space=pltpu.VMEM)
    return call(
        functools.partial(far_body, held, depth, len(sources)),
        cost=FAR_COST,
        in_specs=[smem] * 2
        + [vmem] * len(sources)
        + [pl.BlockSpec(memory_space=pl.ANY)] * len(later_than),
        out_specs=[vmem] * (H // 2),
        out_shape=[jax.ShapeDtypeStruct((parts, 2, rows, hd), sources[0].dtype)] * (H // 2),
    )(block_slots, block_lists, *sources[2:], *sources[:2], *later_than)


def near_body(held, depth, slots_ref, lists_ref, _, *refs):
    (edge_same, edge_other), sources, out_ref = refs[:2], refs[2:-1], refs[-1]
    odd = lax.rem(lax.axis_index("seq"), 2) == 1
    memory, edges = sources[0].shape[2], edge_same.shape[2]
    for pair in range(H // 2):
        for part in range(2):
            for side in range(2):
                for block in range(lists_ref.shape[1]):
                    rows, value = memory_rows(
                        held, slots_ref, lists_ref, block, depth, sources, side, pair, part
                    )
                    first = side * memory + rows.start
                    out_ref[pair, part, first : first + depth] = value
            same, other = edge_same[pair, part], edge_other[pair, part]
            first = 2 * memory
            out_ref[pair, part, first : first + edges] = jnp.where(odd, other, same)
            out_ref[pair, part, first + edges :] = jnp.where(odd, same, other)


def near_pieces(held, depth, block_slots, block_lists, edges, sources, *later_than):
    pairs, parts, rows, hd = sources[0].shape
    smem = pl.BlockSpec(memory_space=pltpu.SMEM)
    vmem = pl.BlockSpec(memory_space=pltpu.VMEM)
    size = 2 * (rows + edges[0].shape[2])
    return call(
        functools.partial(near_body, held, depth),
        cost=NEAR_COST,
        in_specs=[smem] * 2
        + [pl.BlockSpec(memory_space=pl.ANY)] * len(later_than)
        + [vmem] * (2 + len(sources)),
        out_specs=vmem,
        out_shape=jax.ShapeDtypeStruct((pairs, parts, size, hd), sources[0].dtype),
    )(block_slots, block_lists, *later_than, *edges, *sources)


def arrived_body(*refs):
    refs[-1][...] = jnp.zeros_like(refs[-1])


def arrived(far):
    return call(
        arrived_body,
        cost=ARRIVED_COST,
        in_specs=[pl.BlockSpec(memory_space=pl.ANY)] * len(far),
        out_specs=pl.BlockSpec(memory_space=pltpu.VMEM),
        out_shape=jax.ShapeDtypeStruct((8, 128), jnp.float32),
    )(*far)


def attend_body(scale, depth, half, memories, length_ref, count_ref, _, ev_ref, near_ref, *refs):
    far_refs, refs = refs[:memories], refs[memories:]
    gq_ref, gk_ref, gv_ref = refs[:3]
    rows, hd = ev_ref.shape[2:]
    tile = 2 * rows
    tiles = WINDOW // tile
    near = near_ref.shape[2] - 2 * rows
    user = lax.axis_index("dp")
    length, count = length_ref[user], count_ref[user]
    base = (lax.axis_index("seq") // H) * (H * rows) + half * WINDOW
    slope = scale * LOG2E

    def events(part, chunk):
        return ev_ref[2 * chunk : 2 * chunk + 2, part].reshape(tile, hd)

    def window(part, chunk):
        chunk += half * tiles
        if chunk < 0:
            return near_ref[tiles + chunk, part - 1, near:].reshape(tile, hd)
        return events(part, chunk)

    per = max(1, tile // near)
    memory = [
        [
            near_ref[first : first + per, part, :near].reshape(-1, hd)
            for first in range(0, near_ref.shape[0], per)
        ]
        + [
            jnp.concatenate(
                [ref[part].reshape(near, hd) for ref in far_refs[first : first + per]], axis=0
            )
            for first in range(0, memories, per)
        ]
        for part in range(2)
    ]
    line = lax.broadcasted_iota(jnp.int32, (tile, tile), 0)
    column = lax.broadcasted_iota(jnp.int32, (tile, tile), 1)
    which = lax.broadcasted_iota(jnp.int32, (1, per * near), 1)
    live = lax.rem(which, near // 2) // depth < count

    sums = {}
    for this in range(tiles):
        q, g = events(0, half * tiles + this), events(3, half * tiles + this)
        chunks = list(range(this - tiles, this + 1))
        keys = [window(1, chunk) for chunk in chunks] + memory[0]
        values = [window(2, chunk) for chunk in chunks] + memory[1]
        score = []
        for i, key in enumerate(keys):
            s = dot_nt(q, key)
            if i <= tiles:
                position = base + chunks[i] * tile + column[:1]
                allowed = (position >= 0) & (position < length)
                if i == 0:
                    allowed = allowed & (column > line)
                elif i == tiles:
                    allowed = (allowed & (column < line)) | (column == line)
                s = jnp.where(allowed, s, NEG)
            else:
                s = jnp.where(live, s, NEG)
            score.append(s)
        top = functools.reduce(
            jnp.maximum, [s for s in score if s.shape == score[0].shape]
        )
        top = jnp.max(top, axis=1, keepdims=True)
        for s in score:
            if s.shape != score[0].shape:
                top = jnp.maximum(top, jnp.max(s, axis=1, keepdims=True))
        expo = [jnp.exp2((s - top) * slope) for s in score]
        dprob = [dot_nt(g, value) for value in values]

        def row_sum(blocks):
            first = [block for block in blocks if block.shape == score[0].shape]
            total = jnp.sum(functools.reduce(jnp.add, first), axis=1, keepdims=True)
            for block in blocks:
                if block.shape != score[0].shape:
                    total += jnp.sum(block, axis=1, keepdims=True)
            return total

        total = row_sum(expo)
        inv = 1.0 / total
        delta = row_sum([e * d for e, d in zip(expo, dprob)]) * inv
        gq = jnp.zeros((tile, hd), jnp.float32)
        for e, d, key in zip(expo[tiles + 1 :], dprob[tiles + 1 :], memory[0]):
            gq += dot_nn((e * (d - delta)).astype(jnp.bfloat16), key)
        gq = gq * inv
        for i, chunk in enumerate(chunks):
            prob = expo[i] * inv
            dscore = (prob * (dprob[i] - delta)).astype(jnp.bfloat16)
            gq += dot_nn(dscore, keys[i])
            if chunk + half * tiles >= 0:
                owed = dot_tn(dscore, q), dot_tn(prob.astype(jnp.bfloat16), g)
                old = sums.get(chunk)
                sums[chunk] = owed if old is None else (old[0] + owed[0], old[1] + owed[1])
        gq_ref[2 * this : 2 * this + 2] = (gq * scale).astype(gq_ref.dtype).reshape(2, rows, hd)
        if half == 0:
            lane = lax.broadcasted_iota(jnp.int32, (tile, hd), 1)
            both = jnp.where(lane == 0, top * slope + jnp.log2(total), delta)
            refs[3][this] = both.T[:8]
    for i, chunk in enumerate(sorted(sums)):
        gk_ref[i * tile : (i + 1) * tile] = sums[chunk][0] * scale
        gv_ref[i * tile : (i + 1) * tile] = sums[chunk][1]


def attend(scale, depth, half, seq_lengths, mem_counts, after, events, near, far):
    _, _, rows, hd = events.shape
    keys = WINDOW + (near.shape[2] - 2 * rows) * (near.shape[0] + len(far))
    smem = pl.BlockSpec(memory_space=pltpu.SMEM)
    vmem = pl.BlockSpec(memory_space=pltpu.VMEM)
    outs = [((WINDOW // rows, rows, hd), jnp.bfloat16)]
    outs += [(((1 + half) * WINDOW, hd), jnp.float32)] * 2
    if half == 0:
        outs.append(((WINDOW // (2 * rows), 8, 2 * rows), jnp.float32))
    return call(
        functools.partial(attend_body, scale, depth, half, len(far)),
        in_specs=[smem] * 2 + [pl.BlockSpec(memory_space=pl.ANY)] + [vmem] * (2 + len(far)),
        out_specs=[vmem] * len(outs),
        out_shape=[jax.ShapeDtypeStruct(shape, dtype) for shape, dtype in outs],
        cost_estimate=pl.CostEstimate(
            flops=10 * WINDOW * keys * hd,
            bytes_accessed=4 * keys * hd,
            transcendentals=WINDOW * keys,
        ),
    )(seq_lengths, mem_counts, after, events, near, *far)


def finish_body(scale, length_ref, ev_ref, near_ref, stats_ref, *refs):
    (gq0, gk0, gv0, gq1, gk1, gv1), out_ref = refs[:-1], refs[-1]
    group, _, rows, hd = ev_ref.shape
    reach = WINDOW // rows
    early = group - reach
    near = near_ref.shape[2] - 2 * rows
    number = lax.axis_index("seq") // H
    length = length_ref[lax.axis_index("dp")]
    follows = number + 1 < lax.axis_size("seq") // H
    base = number * (H * rows)
    slope = scale * LOG2E
    span = group * rows

    def put(where, part, value):
        out_ref[where, part] = value.astype(out_ref.dtype).reshape(reach, rows, hd)

    first, last = slice(0, early), slice(early, group)
    out_ref[first, 0] = gq0[...]
    out_ref[last, 0] = gq1[...]
    put(first, 1, gk0[...] + gk1[:WINDOW])
    put(first, 2, gv0[...] + gv1[:WINDOW])
    k = ev_ref[early:, 1].reshape(WINDOW, hd)
    v = ev_ref[early:, 2].reshape(WINDOW, hd)
    gk = jnp.zeros((WINDOW, hd), jnp.float32)
    gv = jnp.zeros((WINDOW, hd), jnp.float32)
    kpos = base + span - WINDOW + lax.broadcasted_iota(jnp.int32, (WINDOW, TILE), 0)
    for tile in range(WINDOW // TILE):
        pairs = early // 2 + tile * TILE // (2 * rows)
        pairs = slice(pairs, pairs + TILE // (2 * rows))
        q = near_ref[pairs, 0, near:].reshape(TILE, hd)
        g = near_ref[pairs, 1, near:].reshape(TILE, hd)
        qpos = base + span + tile * TILE + lax.broadcasted_iota(jnp.int32, (WINDOW, TILE), 1)
        allowed = (qpos - kpos < WINDOW) & (kpos < length) & follows
        s = jnp.where(allowed, dot_nt(k, q) * slope - stats_ref[tile, 0:1], NEG)
        p = jnp.exp2(s)
        d = dot_nt(v, g)
        ds = p * (d - stats_ref[tile, 1:2])
        gk += dot_nn(ds.astype(jnp.bfloat16), q)
        gv += dot_nn(p.astype(jnp.bfloat16), g)
    put(last, 1, gk1[WINDOW:] + gk * scale)
    put(last, 2, gv1[WINDOW:] + gv)


def finish(scale, seq_lengths, events, near, stats, halves):
    group, _, rows, hd = events.shape
    vmem = pl.BlockSpec(memory_space=pltpu.VMEM)
    return call(
        functools.partial(finish_body, scale),
        in_specs=[pl.BlockSpec(memory_space=pltpu.SMEM)] + [vmem] * 9,
        out_specs=vmem,
        out_shape=jax.ShapeDtypeStruct((group, 3, rows, hd), jnp.bfloat16),
    )(seq_lengths, events, near, stats, *halves)


def join_body(in_ref, *refs):
    parts = in_ref.shape[1]
    outs, (whole, sems) = refs[:parts], refs[parts:]
    hd = in_ref.shape[-1]
    writes = [
        pltpu.make_async_copy(whole.at[part], out_ref.at[0], sems.at[part])
        for part, out_ref in enumerate(outs)
    ]
    for part, write in enumerate(writes):
        for head in range(H):
            whole[part, :, head * hd : (head + 1) * hd] = in_ref[head, part]
        write.start()
    for write in writes:
        write.wait()


def join_heads(pieces):
    heads, parts, rows, hd = pieces.shape
    return call(
        join_body,
        in_specs=[pl.BlockSpec(memory_space=pltpu.VMEM)],
        out_specs=[pl.BlockSpec(memory_space=pltpu.HBM)] * parts,
        out_shape=[jax.ShapeDtypeStruct((1, rows, heads * hd), pieces.dtype)] * parts,
        scratch_shapes=[
            pltpu.VMEM((parts, rows, heads * hd), pieces.dtype),
            pltpu.SemaphoreType.DMA((parts,)),
        ],
    )(pieces)


def on_device(
    queries,
    keys,
    values,
    grad_out,
    mem_keys,
    mem_values,
    seq_lengths,
    mem_counts,
    block_lists,
    block_slots,
):
    rows, width = queries.shape[1:]
    scale = 1.0 / math.sqrt(width // H)
    reach = WINDOW // rows
    seq, users = lax.axis_size("seq"), lax.axis_size("dp")
    groups = [[first + i for i in range(H)] for first in range(0, seq, H)]
    swap = functools.partial(
        lax.all_to_all, axis_name="seq", split_axis=0, concat_axis=0, tiled=True
    )

    arrays = (queries, keys, values, grad_out)
    packed = pack(users, seq_lengths, block_slots, block_lists, arrays, mem_keys, mem_values)
    packed = packed[: users + 1], packed[users + 1 :]
    sources = [packed[0][0]]
    sources.append(lax.ppermute(packed[1][0], "seq", [(i, i ^ 1) for i in range(seq)]))
    places = [(u, i) for u in range(users) for i in range(seq)]
    for step in range(1, users):
        for side in range(2):
            pairs = [
                (u * seq + i, (u + step) % users * seq + (i ^ side)) for u, i in places
            ]
            sources.append(lax.ppermute(packed[side][step], ("dp", "seq"), pairs))
    pairs = [(i, i - reach if i % H < reach else i + reach) for i in range(seq)]
    pairs = [(i, j) for i, j in pairs if 0 <= j < seq]
    edges = [
        lax.ppermute(packed[side][users], "seq", [(i, j ^ side) for i, j in pairs])
        for side in range(2)
    ]

    events = swap(split_heads(seq_lengths, arrays), axis_index_groups=groups)

    held, depth = mem_keys.shape[:2]
    pieces = far_pieces(held, depth, block_slots, block_lists, sources, *edges)
    far = []
    for around in range(1, seq // H):
        for step, piece in enumerate(pieces):
            pairs = [
                (i, ((i // H + around) * H) % seq + ((i % H) ^ (2 * step))) for i in range(seq)
            ]
            far.append(lax.ppermute(piece, "seq", pairs))
    after = arrived(far)
    near = near_pieces(held, depth, block_slots, block_lists, edges, sources, pieces[0])
    parities = [group[parity::2] for group in groups for parity in range(2)]
    near = swap(near, axis_index_groups=parities)

    part = functools.partial(attend, scale, depth)
    *first, stats = part(0, seq_lengths, mem_counts, after, events, near, far)
    stats = lax.ppermute(stats, "seq", [(i + H, i) for i in range(seq - H)])
    second = part(1, seq_lengths, mem_counts, after, events, near, far)
    out = finish(scale, seq_lengths, events, near, stats, [*first, *second])
    return tuple(join_heads(swap(out, axis_index_groups=groups)))


def solution(mesh):
    spread = P("dp", "seq", None)
    return jax.shard_map(
        on_device,
        mesh=mesh,
        in_specs=(spread,) * 6 + (P(),) * 4,
        out_specs=(spread,) * 3,
        check_vma=False,
    )
```

```python
import functools
import math

import jax
import jax.numpy as jnp
from jax import lax
from jax.experimental import pallas as pl
from jax.experimental.pallas import tpu as pltpu
from jax.sharding import PartitionSpec as P

H = 8
WINDOW = 512
TILE = 256
NEG = -1e30
LOG2E = 1.4426950408889634
FAR_COST = 10**11
ARRIVED_COST = 10**11
NEAR_COST = 0
VMEM_LIMIT = 32 * 1024 * 1024
VMEM_WHOLE = 64 * 1024 * 1024 - 256 * 1024

NT = (((1,), (1,)), ((), ()))
TN = (((0,), (0,)), ((), ()))


def dot_nt(a, b):
    return lax.dot_general(a, b, NT, preferred_element_type=jnp.float32)


def dot_tn(a, b):
    return lax.dot_general(a, b, TN, preferred_element_type=jnp.float32)


def dot_nn(a, b):
    return jnp.dot(a, b, preferred_element_type=jnp.float32)


def call(body, limit=VMEM_LIMIT, cost=None, **kw):
    if cost:
        kw["cost_estimate"] = pl.CostEstimate(flops=cost, bytes_accessed=0, transcendentals=0)
    return pl.pallas_call(
        body, compiler_params=pltpu.CompilerParams(vmem_limit_bytes=limit), **kw
    )


def load_listed(user, slots_ref, lists_ref, mk_ref, mv_ref, buffer, sems):
    copies = []
    for block in range(buffer.shape[0]):
        index = lax.rem(slots_ref[lists_ref[user, block]], mk_ref.shape[0])
        for part, pool in enumerate((mk_ref, mv_ref)):
            copies.append(
                pltpu.make_async_copy(
                    pool.at[index], buffer.at[block, part], sems.at[block, part]
                )
            )
    for copy in copies:
        copy.start()
    return copies


def split_parity(value, where, same_ref, other_ref):
    hd = value.shape[1] // H
    odd = lax.rem(lax.axis_index("seq"), 2) == 1
    for pair in range(H // 2):
        first = value[:, 2 * pair * hd : (2 * pair + 1) * hd]
        second = value[:, (2 * pair + 1) * hd : (2 * pair + 2) * hd]
        same_ref[(pair,) + where] = jnp.where(odd, second, first)
        other_ref[(pair,) + where] = jnp.where(odd, first, second)


def pack_body(users, length_ref, slots_ref, lists_ref, *refs):
    (q_ref, k_ref, v_ref, g_ref, mk_ref, mv_ref), refs = refs[:6], refs[6:]
    outs, refs = refs[: 2 * users + 2], refs[2 * users + 2 :]
    buffer, sems, edge, edge_sems, out_sems = refs[:5]
    cuts = refs[5:]
    same, other = cuts[: users + 1], cuts[users + 1 :]
    writes = [
        pltpu.make_async_copy(cut, out, out_sems.at[i])
        for i, (cut, out) in enumerate(zip(cuts, outs))
    ]
    user, shard = lax.axis_index("dp"), lax.axis_index("seq")
    _, blocks, parts, depth, _ = buffer.shape
    rows, width = edge.shape[1:]
    early = lax.rem(shard, H) < WINDOW // rows
    order = [step % users for step in range(1, users + 1)]
    loads = {
        step: load_listed(
            lax.rem(user + step, users),
            slots_ref,
            lists_ref,
            mk_ref,
            mv_ref,
            buffer.at[step],
            sems.at[step],
        )
        for step in order
    }

    @pl.when(early)
    def _():
        for part, ref in enumerate((q_ref, g_ref)):
            pltpu.make_async_copy(ref.at[0], edge.at[part], edge_sems.at[part]).start()

    @pl.when(jnp.logical_not(early))
    def _():
        for part, ref in enumerate((k_ref, v_ref)):
            pltpu.make_async_copy(ref.at[0], edge.at[part], edge_sems.at[part]).start()

    for step in order:
        for copy in loads[step]:
            copy.wait()
        for block in range(blocks):
            for part in range(parts):
                where = (part, slice(block * depth, (block + 1) * depth))
                split_parity(buffer[step, block, part], where, same[step], other[step])
        writes[step].start()
        writes[users + 1 + step].start()
    live = jnp.where(early, length_ref[user] - shard * rows, rows)
    for part in range(2):
        pltpu.make_async_copy(q_ref.at[0], edge.at[part], edge_sems.at[part]).wait()
        value = edge[part]
        if part == 1:
            position = lax.broadcasted_iota(jnp.int32, (rows, width), 0)
            value = jnp.where(position < live, value.astype(jnp.float32), 0.0)
            value = value.astype(edge.dtype)
        split_parity(value, (part,), same[users], other[users])
    writes[users].start()
    writes[2 * users + 1].start()
    for write in writes:
        write.wait()


def pack(users, seq_lengths, block_slots, block_lists, events, mem_keys, mem_values):
    _, depth, width = mem_keys.shape
    blocks = block_lists.shape[1]
    rows = events[0].shape[1]
    dtype = mem_keys.dtype
    smem = pl.BlockSpec(memory_space=pltpu.SMEM)
    hbm = pl.BlockSpec(memory_space=pltpu.HBM)
    pieces = jax.ShapeDtypeStruct((H // 2, 2, blocks * depth, width // H), dtype)
    edges = jax.ShapeDtypeStruct((H // 2, 2, rows, width // H), dtype)
    outs = ([pieces] * users + [edges]) * 2
    return call(
        functools.partial(pack_body, users),
        limit=VMEM_WHOLE,
        in_specs=[smem] * 3 + [hbm] * 6,
        out_specs=[hbm] * len(outs),
        out_shape=outs,
        scratch_shapes=[
            pltpu.VMEM((users, blocks, 2, depth, width), dtype),
            pltpu.SemaphoreType.DMA((users, blocks, 2)),
            pltpu.VMEM((2, rows, width), dtype),
            pltpu.SemaphoreType.DMA((2,)),
            pltpu.SemaphoreType.DMA((len(outs),)),
        ]
        + [pltpu.VMEM(out.shape, out.dtype) for out in outs],
    )(seq_lengths, block_slots, block_lists, *events, mem_keys, mem_values)


def split_body(hd, length_ref, *refs):
    sources, (out_ref, buffer, sems, cut, out_sems) = refs[:4], refs[4:]
    rows = buffer.shape[1]
    copies = [
        pltpu.make_async_copy(source.at[0], buffer.at[part], sems.at[part])
        for part, source in enumerate(sources)
    ]
    for copy in copies:
        copy.start()
    live = length_ref[lax.axis_index("dp")] - lax.axis_index("seq") * rows
    position = lax.broadcasted_iota(jnp.int32, (rows, hd), 0)
    for part, copy in enumerate(copies):
        copy.wait()
        for head in range(H):
            block = buffer[part, :, head * hd : (head + 1) * hd]
            if part == 3:
                block = jnp.where(position < live, block.astype(jnp.float32), 0.0)
            cut[part, head] = block.astype(cut.dtype)
        pltpu.make_async_copy(cut.at[part], out_ref.at[:, part], out_sems.at[part]).start()
    for part in range(len(copies)):
        pltpu.make_async_copy(cut.at[part], out_ref.at[:, part], out_sems.at[part]).wait()


def split_heads(seq_lengths, arrays):
    _, rows, width = arrays[0].shape
    parts = len(arrays)
    hbm = pl.BlockSpec(memory_space=pltpu.HBM)
    return call(
        functools.partial(split_body, width // H),
        limit=VMEM_WHOLE,
        in_specs=[pl.BlockSpec(memory_space=pltpu.SMEM)] + [hbm] * parts,
        out_specs=hbm,
        out_shape=jax.ShapeDtypeStruct((H, parts, rows, width // H), arrays[0].dtype),
        scratch_shapes=[
            pltpu.VMEM((parts, rows, width), arrays[0].dtype),
            pltpu.SemaphoreType.DMA((parts,)),
            pltpu.VMEM((parts, H, rows, width // H), arrays[0].dtype),
            pltpu.SemaphoreType.DMA((parts,)),
        ],
    )(seq_lengths, *arrays)


def memory_rows(held, slots_ref, lists_ref, block, depth, sources, side, pair, part):
    users = len(sources) // 2
    user = lax.axis_index("dp")
    slot = slots_ref[lists_ref[user, block]]
    source = lax.rem(user - slot // held + users, users)
    rows = slice(block * depth, (block + 1) * depth)
    value = sources[side][pair, part, rows]
    for other in range(1, users):
        value = jnp.where(source == other, sources[2 * other + side][pair, part, rows], value)
    return rows, value


def far_body(held, depth, number, slots_ref, lists_ref, *refs):
    outs = refs[-(H // 2) :]
    sources = refs[number - 2 : number] + refs[: number - 2]
    pair = lax.rem(lax.axis_index("seq") // 2, H // 2)
    for block in range(lists_ref.shape[1]):
        for step, out_ref in enumerate(outs):
            for side in range(2):
                for part in range(2):
                    rows, value = memory_rows(
                        held, slots_ref, lists_ref, block, depth, sources, side, pair ^ step, part
                    )
                    out_ref[part, side, rows] = value


def far_pieces(held, depth, block_slots, block_lists, sources, *later_than):
    _, parts, rows, hd = sources[0].shape
    smem = pl.BlockSpec(memory_space=pltpu.SMEM)
    vmem = pl.BlockSpec(memory_space=pltpu.VMEM)
    return call(
        functools.partial(far_body, held, depth, len(sources)),
        cost=FAR_COST,
        in_specs=[smem] * 2
        + [vmem] * len(sources)
        + [pl.BlockSpec(memory_space=pl.ANY)] * len(later_than),
        out_specs=[vmem] * (H // 2),
        out_shape=[jax.ShapeDtypeStruct((parts, 2, rows, hd), sources[0].dtype)] * (H // 2),
    )(block_slots, block_lists, *sources[2:], *sources[:2], *later_than)


def near_body(held, depth, slots_ref, lists_ref, _, *refs):
    (edge_same, edge_other), sources, out_ref = refs[:2], refs[2:-1], refs[-1]
    odd = lax.rem(lax.axis_index("seq"), 2) == 1
    memory, edges = sources[0].shape[2], edge_same.shape[2]
    for pair in range(H // 2):
        for part in range(2):
            for side in range(2):
                for block in range(lists_ref.shape[1]):
                    rows, value = memory_rows(
                        held, slots_ref, lists_ref, block, depth, sources, side, pair, part
                    )
                    first = side * memory + rows.start
                    out_ref[pair, part, first : first + depth] = value
            same, other = edge_same[pair, part], edge_other[pair, part]
            first = 2 * memory
            out_ref[pair, part, first : first + edges] = jnp.where(odd, other, same)
            out_ref[pair, part, first + edges :] = jnp.where(odd, same, other)


def near_pieces(held, depth, block_slots, block_lists, edges, sources, *later_than):
    pairs, parts, rows, hd = sources[0].shape
    smem = pl.BlockSpec(memory_space=pltpu.SMEM)
    vmem = pl.BlockSpec(memory_space=pltpu.VMEM)
    size = 2 * (rows + edges[0].shape[2])
    return call(
        functools.partial(near_body, held, depth),
        cost=NEAR_COST,
        in_specs=[smem] * 2
        + [pl.BlockSpec(memory_space=pl.ANY)] * len(later_than)
        + [vmem] * (2 + len(sources)),
        out_specs=vmem,
        out_shape=jax.ShapeDtypeStruct((pairs, parts, size, hd), sources[0].dtype),
    )(block_slots, block_lists, *later_than, *edges, *sources)


def arrived_body(*refs):
    refs[-1][...] = jnp.zeros_like(refs[-1])


def arrived(far):
    return call(
        arrived_body,
        cost=ARRIVED_COST,
        in_specs=[pl.BlockSpec(memory_space=pl.ANY)] * len(far),
        out_specs=pl.BlockSpec(memory_space=pltpu.VMEM),
        out_shape=jax.ShapeDtypeStruct((8, 128), jnp.float32),
    )(*far)


def attend_body(scale, depth, half, memories, length_ref, count_ref, _, ev_ref, near_ref, *refs):
    far_refs, refs = refs[:memories], refs[memories:]
    gq_ref, gk_ref, gv_ref = refs[:3]
    rows, hd = ev_ref.shape[2:]
    tile = 2 * rows
    tiles = WINDOW // tile
    near = near_ref.shape[2] - 2 * rows
    user = lax.axis_index("dp")
    length, count = length_ref[user], count_ref[user]
    base = (lax.axis_index("seq") // H) * (H * rows) + half * WINDOW
    slope = scale * LOG2E

    def events(part, chunk):
        return ev_ref[2 * chunk : 2 * chunk + 2, part].reshape(tile, hd)

    def window(part, chunk):
        chunk += half * tiles
        if chunk < 0:
            return near_ref[tiles + chunk, part - 1, near:].reshape(tile, hd)
        return events(part, chunk)

    per = max(1, tile // near)
    memory = [
        [
            near_ref[first : first + per, part, :near].reshape(-1, hd)
            for first in range(0, near_ref.shape[0], per)
        ]
        + [
            jnp.concatenate(
                [ref[part].reshape(near, hd) for ref in far_refs[first : first + per]], axis=0
            )
            for first in range(0, memories, per)
        ]
        for part in range(2)
    ]
    line = lax.broadcasted_iota(jnp.int32, (tile, tile), 0)
    column = lax.broadcasted_iota(jnp.int32, (tile, tile), 1)
    which = lax.broadcasted_iota(jnp.int32, (1, per * near), 1)
    live = lax.rem(which, near // 2) // depth < count

    sums = {}
    for this in range(tiles):
        q, g = events(0, half * tiles + this), events(3, half * tiles + this)
        chunks = list(range(this - tiles, this + 1))
        keys = [window(1, chunk) for chunk in chunks] + memory[0]
        values = [window(2, chunk) for chunk in chunks] + memory[1]
        score = []
        for i, key in enumerate(keys):
            s = dot_nt(q, key)
            if i <= tiles:
                position = base + chunks[i] * tile + column[:1]
                allowed = (position >= 0) & (position < length)
                if i == 0:
                    allowed = allowed & (column > line)
                elif i == tiles:
                    allowed = (allowed & (column < line)) | (column == line)
                s = jnp.where(allowed, s, NEG)
            else:
                s = jnp.where(live, s, NEG)
            score.append(s)
        top = functools.reduce(
            jnp.maximum, [s for s in score if s.shape == score[0].shape]
        )
        top = jnp.max(top, axis=1, keepdims=True)
        for s in score:
            if s.shape != score[0].shape:
                top = jnp.maximum(top, jnp.max(s, axis=1, keepdims=True))
        expo = [jnp.exp2((s - top) * slope) for s in score]
        dprob = [dot_nt(g, value) for value in values]

        def row_sum(blocks):
            first = [block for block in blocks if block.shape == score[0].shape]
            total = jnp.sum(functools.reduce(jnp.add, first), axis=1, keepdims=True)
            for block in blocks:
                if block.shape != score[0].shape:
                    total += jnp.sum(block, axis=1, keepdims=True)
            return total

        total = row_sum(expo)
        inv = 1.0 / total
        delta = row_sum([e * d for e, d in zip(expo, dprob)]) * inv
        gq = jnp.zeros((tile, hd), jnp.float32)
        for e, d, key in zip(expo[tiles + 1 :], dprob[tiles + 1 :], memory[0]):
            gq += dot_nn((e * (d - delta)).astype(jnp.bfloat16), key)
        gq = gq * inv
        for i, chunk in enumerate(chunks):
            prob = expo[i] * inv
            dscore = (prob * (dprob[i] - delta)).astype(jnp.bfloat16)
            gq += dot_nn(dscore, keys[i])
            if chunk + half * tiles >= 0:
                owed = dot_tn(dscore, q), dot_tn(prob.astype(jnp.bfloat16), g)
                old = sums.get(chunk)
                sums[chunk] = owed if old is None else (old[0] + owed[0], old[1] + owed[1])
        gq_ref[2 * this : 2 * this + 2] = (gq * scale).astype(gq_ref.dtype).reshape(2, rows, hd)
        if half == 0:
            lane = lax.broadcasted_iota(jnp.int32, (tile, hd), 1)
            both = jnp.where(lane == 0, top * slope + jnp.log2(total), delta)
            refs[3][this] = both.T[:8]
    for i, chunk in enumerate(sorted(sums)):
        gk_ref[i * tile : (i + 1) * tile] = sums[chunk][0] * scale
        gv_ref[i * tile : (i + 1) * tile] = sums[chunk][1]


def attend(scale, depth, half, seq_lengths, mem_counts, after, events, near, far):
    _, _, rows, hd = events.shape
    keys = WINDOW + (near.shape[2] - 2 * rows) * (near.shape[0] + len(far))
    smem = pl.BlockSpec(memory_space=pltpu.SMEM)
    vmem = pl.BlockSpec(memory_space=pltpu.VMEM)
    outs = [((WINDOW // rows, rows, hd), jnp.bfloat16)]
    outs += [(((1 + half) * WINDOW, hd), jnp.float32)] * 2
    if half == 0:
        outs.append(((WINDOW // (2 * rows), 8, 2 * rows), jnp.float32))
    return call(
        functools.partial(attend_body, scale, depth, half, len(far)),
        in_specs=[smem] * 2 + [pl.BlockSpec(memory_space=pl.ANY)] + [vmem] * (2 + len(far)),
        out_specs=[vmem] * len(outs),
        out_shape=[jax.ShapeDtypeStruct(shape, dtype) for shape, dtype in outs],
        cost_estimate=pl.CostEstimate(
            flops=10 * WINDOW * keys * hd,
            bytes_accessed=4 * keys * hd,
            transcendentals=WINDOW * keys,
        ),
    )(seq_lengths, mem_counts, after, events, near, *far)


def finish_body(scale, length_ref, ev_ref, near_ref, stats_ref, *refs):
    (gq0, gk0, gv0, gq1, gk1, gv1), out_ref = refs[:-1], refs[-1]
    group, _, rows, hd = ev_ref.shape
    reach = WINDOW // rows
    early = group - reach
    near = near_ref.shape[2] - 2 * rows
    number = lax.axis_index("seq") // H
    length = length_ref[lax.axis_index("dp")]
    follows = number + 1 < lax.axis_size("seq") // H
    base = number * (H * rows)
    slope = scale * LOG2E
    span = group * rows

    def put(where, part, value):
        out_ref[where, part] = value.astype(out_ref.dtype).reshape(reach, rows, hd)

    first, last = slice(0, early), slice(early, group)
    out_ref[first, 0] = gq0[...]
    out_ref[last, 0] = gq1[...]
    put(first, 1, gk0[...] + gk1[:WINDOW])
    put(first, 2, gv0[...] + gv1[:WINDOW])
    line = lax.broadcasted_iota(jnp.int32, (TILE, TILE), 0)
    column = lax.broadcasted_iota(jnp.int32, (TILE, TILE), 1)
    blocks = TILE // rows
    for chunk in range(WINDOW // TILE):
        mine = slice(early + chunk * blocks, early + (chunk + 1) * blocks)
        k = ev_ref[mine, 1].reshape(TILE, hd)
        v = ev_ref[mine, 2].reshape(TILE, hd)
        gk = jnp.zeros((TILE, hd), jnp.float32)
        gv = jnp.zeros((TILE, hd), jnp.float32)
        kpos = base + span - WINDOW + chunk * TILE + line
        for tile in range(chunk + 1):
            pairs = early // 2 + tile * TILE // (2 * rows)
            pairs = slice(pairs, pairs + TILE // (2 * rows))
            q = near_ref[pairs, 0, near:].reshape(TILE, hd)
            g = near_ref[pairs, 1, near:].reshape(TILE, hd)
            allowed = (kpos < length) & follows
            if tile == chunk:
                allowed = allowed & (column < line)
            s = jnp.where(allowed, dot_nt(k, q) * slope - stats_ref[tile, 0:1], NEG)
            p = jnp.exp2(s)
            d = dot_nt(v, g)
            ds = p * (d - stats_ref[tile, 1:2])
            gk += dot_nn(ds.astype(jnp.bfloat16), q)
            gv += dot_nn(p.astype(jnp.bfloat16), g)
        here = slice(WINDOW + chunk * TILE, WINDOW + (chunk + 1) * TILE)
        for part, value in ((1, gk1[here] + gk * scale), (2, gv1[here] + gv)):
            out_ref[mine, part] = value.astype(out_ref.dtype).reshape(blocks, rows, hd)


def finish(scale, seq_lengths, events, near, stats, halves):
    group, _, rows, hd = events.shape
    vmem = pl.BlockSpec(memory_space=pltpu.VMEM)
    return call(
        functools.partial(finish_body, scale),
        in_specs=[pl.BlockSpec(memory_space=pltpu.SMEM)] + [vmem] * 9,
        out_specs=vmem,
        out_shape=jax.ShapeDtypeStruct((group, 3, rows, hd), jnp.bfloat16),
    )(seq_lengths, events, near, stats, *halves)


def join_body(in_ref, *refs):
    parts = in_ref.shape[1]
    outs, (whole, sems) = refs[:parts], refs[parts:]
    hd = in_ref.shape[-1]
    writes = [
        pltpu.make_async_copy(whole.at[part], out_ref.at[0], sems.at[part])
        for part, out_ref in enumerate(outs)
    ]
    for part, write in enumerate(writes):
        for head in range(H):
            whole[part, :, head * hd : (head + 1) * hd] = in_ref[head, part]
        write.start()
    for write in writes:
        write.wait()


def join_heads(pieces):
    heads, parts, rows, hd = pieces.shape
    return call(
        join_body,
        in_specs=[pl.BlockSpec(memory_space=pltpu.VMEM)],
        out_specs=[pl.BlockSpec(memory_space=pltpu.HBM)] * parts,
        out_shape=[jax.ShapeDtypeStruct((1, rows, heads * hd), pieces.dtype)] * parts,
        scratch_shapes=[
            pltpu.VMEM((parts, rows, heads * hd), pieces.dtype),
            pltpu.SemaphoreType.DMA((parts,)),
        ],
    )(pieces)


def on_device(
    queries,
    keys,
    values,
    grad_out,
    mem_keys,
    mem_values,
    seq_lengths,
    mem_counts,
    block_lists,
    block_slots,
):
    rows, width = queries.shape[1:]
    scale = 1.0 / math.sqrt(width // H)
    reach = WINDOW // rows
    seq, users = lax.axis_size("seq"), lax.axis_size("dp")
    groups = [[first + i for i in range(H)] for first in range(0, seq, H)]
    swap = functools.partial(
        lax.all_to_all, axis_name="seq", split_axis=0, concat_axis=0, tiled=True
    )

    arrays = (queries, keys, values, grad_out)
    packed = pack(users, seq_lengths, block_slots, block_lists, arrays, mem_keys, mem_values)
    packed = packed[: users + 1], packed[users + 1 :]
    sources = [packed[0][0]]
    sources.append(lax.ppermute(packed[1][0], "seq", [(i, i ^ 1) for i in range(seq)]))
    places = [(u, i) for u in range(users) for i in range(seq)]
    for step in range(1, users):
        for side in range(2):
            pairs = [
                (u * seq + i, (u + step) % users * seq + (i ^ side)) for u, i in places
            ]
            sources.append(lax.ppermute(packed[side][step], ("dp", "seq"), pairs))
    pairs = [(i, i - reach if i % H < reach else i + reach) for i in range(seq)]
    pairs = [(i, j) for i, j in pairs if 0 <= j < seq]
    edges = [
        lax.ppermute(packed[side][users], "seq", [(i, j ^ side) for i, j in pairs])
        for side in range(2)
    ]

    events = swap(split_heads(seq_lengths, arrays), axis_index_groups=groups)

    held, depth = mem_keys.shape[:2]
    pieces = far_pieces(held, depth, block_slots, block_lists, sources, *edges)
    far = []
    for around in range(1, seq // H):
        for step, piece in enumerate(pieces):
            pairs = [
                (i, ((i // H + around) * H) % seq + ((i % H) ^ (2 * step))) for i in range(seq)
            ]
            far.append(lax.ppermute(piece, "seq", pairs))
    after = arrived(far)
    near = near_pieces(held, depth, block_slots, block_lists, edges, sources, pieces[0])
    parities = [group[parity::2] for group in groups for parity in range(2)]
    near = swap(near, axis_index_groups=parities)

    part = functools.partial(attend, scale, depth)
    *first, stats = part(0, seq_lengths, mem_counts, after, events, near, far)
    stats = lax.ppermute(stats, "seq", [(i + H, i) for i in range(seq - H)])
    second = part(1, seq_lengths, mem_counts, after, events, near, far)
    out = finish(scale, seq_lengths, events, near, stats, [*first, *second])
    return tuple(join_heads(swap(out, axis_index_groups=groups)))


def solution(mesh):
    spread = P("dp", "seq", None)
    return jax.shard_map(
        on_device,
        mesh=mesh,
        in_specs=(spread,) * 6 + (P(),) * 4,
        out_specs=(spread,) * 3,
        check_vma=False,
    )
```
